32 devices in a mesh: win: 8 (over z, x), frm: 4 (over y, core).
Axes of the slice: x: 2, y: 2, z: 4, core: 2. Of those that a mesh axis runs over, the one named last changes fastest.
Arguments:
- tokens: bfloat16 [64, 512, 1024], P('win', 'frm'), may hold values from -6 to 6
- condition: bfloat16 [64, 1024], P('win'), may hold values from -6 to 6
- doubled: int32 [64], P('win'), may hold values from 0 to 3
- window_count: int32 [8], P('win'), may hold values from 4 to 8, as said below
- w_ada: bfloat16 [1024, 6144], P('win'), may hold values from -0.1875 to 0.1875
- b_ada: bfloat16 [6144], P('win'), may hold values from -3 to 3
- w_qkv: bfloat16 [1024, 3072], P('win'), may hold values from -0.1875 to 0.1875
- w_out: bfloat16 [1024, 1024], P('win'), may hold values from -1.5 to 1.5
- w_up: bfloat16 [1024, 4096], P('win'), may hold values from -0.1875 to 0.1875
- b_up: bfloat16 [4096], P('win'), may hold values from -3 to 3
- w_down: bfloat16 [4096, 1024], P('win'), may hold values from -0.09375 to 0.09375
- b_down: bfloat16 [1024], P('win'), may hold values from -3 to 3
- table_space: float32 [16, 225], replicated, may hold values from -4 to 4
- table_time: float32 [16, 9], replicated, may hold values from -4 to 4
- cotangent: bfloat16 [64, 512, 1024], P('win', 'frm'), may hold values from -6 to 6
Outputs:
- output: bfloat16 [64, 512, 1024], P('win', 'frm')
- grad_tokens: float32 [64, 512, 1024], P('win', 'frm')
- grad_condition: float32 [64, 1024], P('win')
- grad_w_ada: float32 [1024, 6144], P(None, ('win', 'frm'))
- grad_b_ada: float32 [6144], P(('win', 'frm'))
- grad_w_qkv: float32 [1024, 3072], P(None, ('win', 'frm'))
- grad_w_out: float32 [1024, 1024], P(None, ('win', 'frm'))
- grad_w_up: float32 [1024, 4096], P(None, ('win', 'frm'))
- grad_b_up: float32 [4096], P(('win', 'frm'))
- grad_w_down: float32 [4096, 1024], P(('win', 'frm'))
- grad_b_down: float32 [1024], P(('win', 'frm'))
- grad_table_space: float32 [16, 225], replicated
- grad_table_time: float32 [16, 9], replicated
The draws below stay inside these ranges and needn't reach their ends.
Inputs may be any that keep to these rules, and one draw needn't show every extreme that they name: `window_count`: each index of win has at most 8 live windows, its first ones; some index has exactly 8.
All inputs are finite; a program needn't handle non-finite values.
Results may differ from the reference program's by a relative error of at most 0.018.
Values may be sent and summed in bfloat16 or wider, within the bound.
No kernel may reach another device: no remote copies, remote signals or barrier semaphores. Data moves between devices by JAX's collectives and lax.ppermute only.
A program may use at most 320 MiB of HBM per device.

```python
import math
from functools import partial
import jax
import jax.numpy as jnp
from jax import lax

D = 1024
HEADS = 16
HEAD_DIM = 64
FF = 4096
W_CAP = 8
SIDE = 8
FRAMES = 5
ROWS = 512
WINDOWS = 64
SPACE_REL = 225
TIME_REL = 9
N_WIN = 8
N_FRM = 4


def draw_window_count(key, part):
    key = jax.random.fold_in(key, 11)
    first_key, second_key = jax.random.split(key)
    counts = jax.random.randint(first_key, (N_WIN,), (W_CAP + 1) // 2, W_CAP + 1)
    fullest = jax.random.randint(second_key, (), 0, N_WIN)
    return jnp.where(jnp.arange(N_WIN) == fullest, W_CAP, counts).astype(jnp.int32)


def with_ends(values, stream_key, least, top_value):
    place = [jax.random.randint(jax.random.fold_in(stream_key, axis), (), 0, length) for axis, length in enumerate(values.shape)]
    main_axis = values.shape.index(max(values.shape))
    next_to = place[:main_axis] + [(place[main_axis] + 1) % values.shape[main_axis]] + place[main_axis + 1:]
    return values.at[tuple(place)].set(least).at[tuple(next_to)].set(top_value)


def block_scale(key, dims, cuts, low, largest):
    loudness, own = 1.0, jax.random.fold_in(key, 6)
    for dim, parts in cuts:
        steps = jnp.exp(jax.random.uniform(jax.random.fold_in(own, dim), (parts,), jnp.float32, low / len(cuts), largest / len(cuts)))
        loudness = loudness * jnp.repeat(steps, dims[dim] // parts).reshape([-1 if axis == dim else 1 for axis in range(len(dims))])
    return loudness


def bell_draw(key, shape, deviation, bound, cuts=(), kind=jnp.bfloat16):
    array = deviation * jax.random.normal(key, shape, jnp.float32)
    if cuts:
        array = array * block_scale(key, shape, cuts, -0.22, 0.18)
    return jnp.clip(array, -bound, bound).astype(kind)


def setup_inputs(seed: int = 0) -> dict:
    splits = jax.random.split(jax.random.key(seed), 16)
    return {
        "tokens": bell_draw(splits[0], (WINDOWS, ROWS, D), 1.0, 6.0, ((0, 8), (1, 4))),
        "condition": bell_draw(splits[1], (WINDOWS, D), 1.0, 6.0, ((0, 8),)),
        "doubled": with_ends(jax.random.randint(splits[2], (WINDOWS,), 0, N_FRM), jax.random.fold_in(splits[2], 1), 0, N_FRM - 1).astype(jnp.int32),
        "window_count": draw_window_count(jax.random.fold_in(splits[15], 71), 0),
        "w_ada": bell_draw(splits[4], (D, 6 * D), D ** -0.5, 0.1875, ((0, 8),)),
        "b_ada": bell_draw(splits[5], (6 * D,), 0.5, 3.0, ((0, 8),)),
        "w_qkv": bell_draw(splits[6], (D, 3 * D), D ** -0.5, 0.1875, ((0, 8),)),
        "w_out": bell_draw(splits[7], (D, D), (D // 64) ** -0.5, 1.5, ((0, 8),)),
        "w_up": bell_draw(splits[8], (D, FF), D ** -0.5, 0.1875, ((0, 8),)),
        "b_up": bell_draw(splits[9], (FF,), 0.5, 3.0, ((0, 8),)),
        "w_down": bell_draw(splits[10], (FF, D), FF ** -0.5, 0.09375, ((0, 8),)),
        "b_down": bell_draw(splits[11], (D,), 0.5, 3.0, ((0, 8),)),
        "table_space": bell_draw(splits[12], (HEADS, SPACE_REL), 1.0, 4.0, (), jnp.float32),
        "table_time": bell_draw(splits[13], (HEADS, TIME_REL), 1.0, 4.0, (), jnp.float32),
        "cotangent": bell_draw(splits[14], (WINDOWS, ROWS, D), 1.0, 6.0, ((0, 8), (1, 4))),
    }


@jax.custom_vjp
def low(v):
    return lax.optimization_barrier(v.astype(jnp.bfloat16)).astype(jnp.float32)

@jax.custom_vjp
def low_back(v):
    return v

def low_keep(v):
    return (low(v), None)

def low_pass(kept, grad):
    return (grad,)

def back_keep(v):
    return (v, None)

def back_low(kept, grad):
    return (low(grad),)
low.defvjp(low_keep, low_pass)
low_back.defvjp(back_keep, back_low)
norm_eps = 1e-06
masked_score = -1e+30

def layer_norm(values_in):
    centred = values_in - lax.optimization_barrier(jnp.mean(values_in, axis=-1, keepdims=True))
    return centred * lax.rsqrt(lax.optimization_barrier(jnp.mean(centred * centred, axis=-1, keepdims=True)) + norm_eps)

def exact_dot(left, right):
    return jnp.dot(left, right, precision=lax.Precision.HIGHEST)

def space_index(side):
    places = jnp.arange(side * side, dtype=jnp.int32)
    across = places // side
    along = places % side
    return (across[:, None] - across[None, :] + side - 1) * (2 * side - 1) + (along[:, None] - along[None, :] + side - 1)

def window_group(params, grouped):
    tokens_in, cond_in, doubled_in, live_in = grouped
    w_ada, b_ada, w_qkv, w_out, w_up, b_up, w_down, b_down, table_space, table_time = params
    group_size, row_count, width = tokens_in.shape
    spatial = SIDE * SIDE
    slots = row_count // spatial
    slot_ids = jnp.arange(slots, dtype=jnp.int32)
    holder_ids = slot_ids // 2
    second_slot = slot_ids % 2
    later = (holder_ids[None, :] > doubled_in[:, None]).astype(jnp.int32)
    frame_ids = jnp.minimum(holder_ids[None, :] + later + second_slot[None, :], FRAMES - 1)
    slot_live = (second_slot[None, :] == 0) | (holder_ids[None, :] == doubled_in[:, None])
    row_live = jnp.repeat((slot_live & live_in[:, None]).astype(jnp.float32), spatial, axis=1)[:, :, None]
    silu_cond = low(jax.nn.silu(cond_in))
    modulation = low_back(exact_dot(silu_cond, w_ada) + b_ada)
    blocks = jnp.split(modulation, 6, axis=-1)
    shift_one, scale_one, gate_one = (blocks[0][:, None, :], blocks[1][:, None, :], blocks[2][:, None, :])
    shift_two, scale_two, gate_two = (blocks[3][:, None, :], blocks[4][:, None, :], blocks[5][:, None, :])
    hidden_one = low(layer_norm(tokens_in) * (1.0 + scale_one) + shift_one)
    projected = low(low_back(exact_dot(hidden_one, w_qkv)))
    projected = projected.reshape(group_size, row_count, 3, HEADS, HEAD_DIM)
    queries = projected[:, :, 0]
    key_heads = projected[:, :, 1]
    value_heads = projected[:, :, 2]
    scores = jnp.einsum('gqhe,gkhe->ghqk', queries, key_heads, precision=lax.Precision.HIGHEST) * HEAD_DIM ** (-0.5)
    space_bias = jnp.take(table_space, space_index(SIDE), axis=1)
    time_offset = frame_ids[:, :, None] - frame_ids[:, None, :] + FRAMES - 1
    time_bias = jnp.transpose(jnp.take(table_time, time_offset, axis=1), (1, 0, 2, 3))
    shaped = scores.reshape(group_size, HEADS, slots, spatial, slots, spatial)
    shaped = shaped + space_bias[None, :, None, :, None, :] + time_bias[:, :, :, None, :, None]
    shaped = low_back(shaped)
    shaped = jnp.where(slot_live[:, None, None, None, :, None], shaped, masked_score)
    probs = low(jax.nn.softmax(shaped.reshape(group_size, HEADS, row_count, row_count), axis=-1))
    attended = jnp.einsum('ghqk,gkhe->gqhe', probs, value_heads, precision=lax.Precision.HIGHEST)
    attended = low(low_back(attended)).reshape(group_size, row_count, width)
    branch_attn = low_back(exact_dot(attended, w_out))
    mid = tokens_in + row_live * gate_one * branch_attn
    hidden_two = low(layer_norm(mid) * (1.0 + scale_two) + shift_two)
    pre_act = low_back(exact_dot(hidden_two, w_up) + b_up)
    activated = low(jax.nn.gelu(pre_act))
    branch_mlp = low_back(exact_dot(activated, w_down) + b_down)
    return mid + row_live * gate_two * branch_mlp

def reference(tokens, condition, doubled, window_count, w_ada, b_ada, w_qkv, w_out, w_up, b_up, w_down, b_down, table_space, table_time, cotangent):
    windows_all = tokens.shape[0]
    window_ids = jnp.arange(windows_all, dtype=jnp.int32)
    window_live = window_ids % W_CAP < window_count[window_ids // W_CAP]
    group_size = math.gcd(windows_all, 8)
    params = (w_ada.astype(jnp.float32), b_ada.astype(jnp.float32), w_qkv.astype(jnp.float32), w_out.astype(jnp.float32), w_up.astype(jnp.float32), b_up.astype(jnp.float32), w_down.astype(jnp.float32), b_down.astype(jnp.float32), table_space.astype(jnp.float32), table_time.astype(jnp.float32))

    def forward(tokens_in, cond_in, weights_in):
        grouped = (tokens_in.reshape((windows_all // group_size, group_size) + tokens_in.shape[1:]), cond_in.reshape((windows_all // group_size, group_size) + cond_in.shape[1:]), doubled.reshape(windows_all // group_size, group_size), window_live.reshape(windows_all // group_size, group_size))
        stepper = jax.checkpoint(partial(window_group, weights_in))
        return lax.map(stepper, grouped).reshape(tokens_in.shape)
    result, backward = jax.vjp(forward, tokens.astype(jnp.float32), condition.astype(jnp.float32), params)
    grad_tokens, grad_cond, grads = backward(cotangent.astype(jnp.float32))
    return (result.astype(jnp.bfloat16), grad_tokens, grad_cond, grads[0], grads[1], grads[2], grads[3], grads[4], grads[5], grads[6], grads[7], grads[8], grads[9])
```

```python
import functools

import jax
import jax.numpy as jnp
from jax import lax
from jax.experimental import pallas as pl
from jax.experimental.pallas import tpu as pltpu
from jax.sharding import PartitionSpec as P

SIDE = 8
FRAMES = 5
SPATIAL = SIDE * SIDE
BOTH = ("win", "frm")
EPS = 1e-06
VMEM_LIMIT = 50 * 1024 * 1024

f32 = jnp.float32
bf16 = jnp.bfloat16
exact_mode = lax.Precision.HIGHEST


def swap_frm(array, bit):
    return lax.ppermute(array, "frm", [(j, j ^ bit) for j in range(4)])


def swap_core(array):
    return swap_frm(array, 1)


def swap_y(array):
    return swap_frm(array, 2)


def swap_win(array, bits):
    count = lax.axis_size("win")
    return lax.ppermute(array, "win", [(j, j ^ bits) for j in range(count)])


def exchange_all(array):
    return lax.all_to_all(array, BOTH, split_axis=0, concat_axis=0, tiled=True)


def pick(array, index, axis):
    return lax.dynamic_index_in_dim(array, index, axis, keepdims=False)


def place_kernel(where, *refs):
    count = (len(refs) - 2) // 4
    sources, out, sems = refs[: 4 * count], refs[4 * count], refs[4 * count + 1]
    z, x, y = where[0], where[1], where[2]
    cut = sources[0].shape[-1]
    copies = []
    for core in range(count):
        near_a, far_a, near_b, far_b = sources[4 * core : 4 * core + 4]
        for l in range(2):
            for j in range(2):
                for k in range(4):
                    index = (z ^ k) * 2 + (x ^ j)
                    half = y ^ l
                    own = where[3] ^ core
                    pieces = (
                        ((far_a if l else near_a).at[j, k], pl.ds(0, cut)),
                        (
                            (far_b if j else near_b).at[l, k],
                            pl.ds(cut, out.shape[-1] - cut),
                        ),
                    )
                    for source, columns in pieces:
                        target = (
                            out.at[index, own, half, :, columns]
                            if count == 2
                            else out.at[index, half, :, columns]
                        )
                        copy = pltpu.make_async_copy(source, target, sems.at[len(copies)])
                        copy.start()
                        copies.append(copy)
    for copy in copies:
        copy.wait()


def place(where, pieces, both_cores):
    near_a, near_b = pieces[0], pieces[2]
    rows = near_a.shape[2]
    columns = near_a.shape[3] + near_b.shape[3]
    shape = (8, 2, 2, rows, columns) if both_cores else (8, 2, rows, columns)
    return pl.pallas_call(
        place_kernel,
        out_shape=jax.ShapeDtypeStruct(shape, near_a.dtype),
        in_specs=[pl.BlockSpec(memory_space=pltpu.SMEM)]
        + [pl.BlockSpec(memory_space=pl.ANY)] * len(pieces),
        out_specs=pl.BlockSpec(memory_space=pl.ANY),
        scratch_shapes=[pltpu.SemaphoreType.DMA((8 * len(pieces),))],
        cost_estimate=pl.CostEstimate(
            flops=0, bytes_accessed=4 * near_a.dtype.itemsize * near_a.size, transcendentals=0
        ),
        name="place",
    )(where, *pieces)


def gather_weight(shard, where, both_cores):
    n_win = lax.axis_size("win")
    rows, columns = shard.shape
    if n_win != 8:
        whole = lax.all_gather(shard, "win", axis=0)
        if both_cores:
            other = swap_core(whole)
            first = where[3] == 0
            whole = jnp.stack(
                [jnp.where(first, whole, other), jnp.where(first, other, whole)], axis=1
            )
        return whole
    y = where[2]
    half = pick(shard.reshape(2, rows // 2, columns), y, 0)
    cut = (columns * 3 // 8) // 128 * 128
    along_z = [half] + [swap_win(half, 2 * k) for k in (1, 2, 3)]
    stack_a = jnp.stack([piece[:, :cut] for piece in along_z])
    stack_b = jnp.stack([piece[:, cut:] for piece in along_z])
    arrived_a = swap_win(stack_a, 1)
    arrived_b = swap_y(stack_b)
    near_a = jnp.stack([stack_a, arrived_a])
    near_b = jnp.stack([stack_b, arrived_b])
    far_a = swap_y(near_a)
    far_b = swap_win(near_b, 1)
    pieces = [near_a, far_a, near_b, far_b]
    if both_cores:
        pieces = pieces + [swap_core(piece) for piece in pieces]
        return place(where, pieces, True).reshape(8, 2, rows, columns)
    return place(where, pieces, False).reshape(8, rows, columns)


def add_low(left, right):
    return (left.astype(f32) + right.astype(f32)).astype(bf16)


def scatter_sum(grad, where):
    n_win = lax.axis_size("win")
    z, x, y = where[0], where[1], where[2]
    if n_win != 8:
        mine = lax.psum_scatter(grad.astype(f32), "win", scatter_dimension=0, tiled=False)
        return pick(mine, y, 0) + swap_y(pick(mine, 1 - y, 0))
    rows, columns = grad.shape[2:]
    cube = grad.reshape(4, 2, 2, rows, columns)
    cut = columns // 2
    side_a, side_b = cube[..., :cut], cube[..., cut:]
    got_a = swap_win(pick(side_a, 1 - x, 1), 1)
    got_b = swap_y(pick(side_b, 1 - y, 2))
    own_a = pick(side_a, x, 1)
    own_b = pick(side_b, y, 2)
    more_a = swap_y(add_low(pick(own_a, 1 - y, 1), pick(got_a, 1 - y, 1)))
    more_b = swap_win(add_low(pick(own_b, 1 - x, 1), pick(got_b, 1 - x, 1)), 1)
    kept_a = pick(own_a, y, 1).astype(f32) + pick(got_a, y, 1).astype(f32) + more_a.astype(f32)
    kept_b = pick(own_b, x, 1).astype(f32) + pick(got_b, x, 1).astype(f32) + more_b.astype(f32)
    kept = jnp.concatenate([kept_a.astype(bf16), kept_b.astype(bf16)], axis=-1)
    total = pick(kept, z, 0).astype(f32)
    for k in (1, 2, 3):
        total = total + swap_win(pick(kept, z ^ k, 0), 2 * k).astype(f32)
    return total


def windows_in(array, doubled, y, c):
    width = array.shape[-1]
    split = array.reshape(2, 2, 2, 2, SPATIAL, width)
    other = swap_core(pick(split, 1 - c, 1))
    own = pick(split, c, 1)
    evens_own, evens_other = own[:, :, 0], other[:, :, 0]
    first = c == 0
    even_0 = jnp.where(first, evens_own, evens_other)
    even_1 = jnp.where(first, evens_other, evens_own)
    twice = pick(doubled.reshape(2, 2, 2), c, 1)
    odd = jnp.where((twice == 2 * y + c)[:, :, None, None], own[:, :, 1], other[:, :, 1])
    packed = jnp.stack([even_0, even_1, odd], axis=2)
    away = swap_y(pick(packed, 1 - y, 0))
    here = pick(packed, y, 0)
    low_y = y == 0
    pair_0 = jnp.where(low_y, here[:, :2], away[:, :2])
    pair_1 = jnp.where(low_y, away[:, :2], here[:, :2])
    mine = pick(twice, y, 0)
    last = jnp.where((mine // 2 == y)[:, None, None], here[:, 2], away[:, 2])
    return jnp.concatenate([pair_0, pair_1, last[:, None]], axis=1)


def windows_out(array, y, c):
    evens, last = array[:, :4], array[:, 4:]
    away = jnp.concatenate([jnp.where(y == 0, evens[:, 2:], evens[:, :2]), last], axis=1)
    here = jnp.concatenate([jnp.where(y == 0, evens[:, :2], evens[:, 2:]), last], axis=1)
    back = swap_y(away)
    first = y == 0
    both = jnp.stack([jnp.where(first, here, back), jnp.where(first, back, here)])
    odd = both[:, :, 2]
    mine = jnp.stack([pick(both[:, :, :2], c, 2), odd], axis=2)
    theirs = jnp.stack([pick(both[:, :, :2], 1 - c, 2), odd], axis=2)
    got = swap_core(theirs)
    low_c = c == 0
    whole = jnp.stack([jnp.where(low_c, mine, got), jnp.where(low_c, got, mine)], axis=1)
    return whole.reshape((8, 2) + array.shape[2:])


def head_lanes(head):
    lanes = lax.broadcasted_iota(jnp.int32, (1, 128), 1)
    return (lanes // 64) == head


def attend_kernel(q_ref, k_ref, v_ref, space_ref, time_ref, o_ref, p_ref):
    q, k, v = q_ref[...], k_ref[...], v_ref[...]
    rows = q.shape[0]
    total = jnp.zeros((rows, 128), f32)
    for head in range(2):
        lanes = head_lanes(head)
        scaled = jnp.where(lanes, q * jnp.asarray(0.125, bf16), jnp.zeros_like(q))
        scores = lax.dot_general(scaled, k, (((1,), (1,)), ((), ())), preferred_element_type=f32)
        shaped = scores.reshape(rows // SPATIAL, SPATIAL, rows)
        shaped = shaped + space_ref[head][None] + time_ref[0, head, : rows // SPATIAL][:, None, :]
        scores = shaped.reshape(rows, rows)
        grown = jnp.exp(scores - jnp.max(scores, axis=-1, keepdims=True))
        inverse = 1.0 / jnp.sum(grown, axis=-1, keepdims=True)
        probs = (grown * inverse).astype(bf16)
        p_ref[0, head] = probs
        masked = jnp.where(lanes, v, jnp.zeros_like(v))
        total = total + jnp.dot(probs, masked, preferred_element_type=f32)
    o_ref[...] = total.astype(bf16)


def attend_back_kernel(
    q_ref, k_ref, v_ref, do_ref, o_ref, p_ref, grad_ref, space_ref, time_ref
):
    q, k, v, do = q_ref[...], k_ref[...], v_ref[...], do_ref[...]
    rows = q.shape[0]
    slots = rows // SPATIAL
    product = do.astype(f32) * o_ref[...].astype(f32)
    grad_q = jnp.zeros((rows, 128), f32)
    grad_k = jnp.zeros((rows, 128), f32)
    grad_v = jnp.zeros((rows, 128), f32)

    @pl.when(pl.program_id(1) == 0)
    def _():
        space_ref[...] = jnp.zeros_like(space_ref)

    for head in range(2):
        lanes = head_lanes(head)
        none = jnp.zeros_like(q)
        scale = jnp.asarray(0.125, bf16)
        row_dot = jnp.sum(jnp.where(lanes, product, 0.0), axis=-1, keepdims=True)
        grads = jnp.where(lanes, do, none)
        probs = p_ref[0, head]
        grad_probs = lax.dot_general(
            grads, v, (((1,), (1,)), ((), ())), preferred_element_type=f32
        )
        grad_scores = probs.astype(f32) * (grad_probs - row_dot)
        low = grad_scores.astype(bf16)
        over_rows = (((0,), (0,)), ((), ()))
        grad_v = grad_v + lax.dot_general(probs, grads, over_rows, preferred_element_type=f32)
        grad_k = grad_k + lax.dot_general(
            low, jnp.where(lanes, q * scale, none), over_rows, preferred_element_type=f32
        )
        grad_q = grad_q + jnp.dot(
            low, jnp.where(lanes, k * scale, none), preferred_element_type=f32
        )
        shaped = grad_scores.reshape(slots, SPATIAL, rows)
        space_ref[head] += jnp.sum(shaped, axis=0)
        time_ref[0, head, :slots] = jnp.sum(shaped, axis=1)
    grad_ref[0] = grad_q.astype(bf16)
    grad_ref[1] = grad_k.astype(bf16)
    grad_ref[2] = grad_v.astype(bf16)


def attention_specs(rows, pairs):
    q_spec = pl.BlockSpec((rows, 128), lambda pair, window: (window, pair))
    k_spec = pl.BlockSpec((rows, 128), lambda pair, window: (window, pair + pairs))
    v_spec = pl.BlockSpec((rows, 128), lambda pair, window: (window, pair + 2 * pairs))
    p_spec = pl.BlockSpec((1, 2, rows, rows), lambda pair, window: (window, pair, 0, 0))
    space_spec = pl.BlockSpec((2, SPATIAL, rows), lambda pair, window: (pair, 0, 0))
    time_spec = pl.BlockSpec((1, 2, 8, rows), lambda pair, window: (window, pair, 0, 0))
    return q_spec, k_spec, v_spec, p_spec, space_spec, time_spec


def attend(projected, space_bias, time_bias, windows):
    rows = projected.shape[0] // windows
    heads = space_bias.shape[0]
    q_spec, k_spec, v_spec, p_spec, space_spec, time_spec = attention_specs(rows, heads // 2)
    width = heads * 64
    return pl.pallas_call(
        attend_kernel,
        grid=(heads // 2, windows),
        in_specs=[q_spec, k_spec, v_spec, space_spec, time_spec],
        out_specs=[q_spec, p_spec],
        out_shape=[
            jax.ShapeDtypeStruct((windows * rows, width), bf16),
            jax.ShapeDtypeStruct((windows, heads, rows, rows), bf16),
        ],
        compiler_params=pltpu.CompilerParams(vmem_limit_bytes=VMEM_LIMIT),
        cost_estimate=pl.CostEstimate(
            flops=16 * windows * heads * rows * rows * 64,
            bytes_accessed=windows * heads * rows * rows * 2,
            transcendentals=windows * heads * rows * rows,
        ),
        name="attend",
    )(projected, projected, projected, space_bias, time_bias)


def attend_back(projected, grad_attended, attended, probs, windows):
    heads, rows = probs.shape[1], probs.shape[2]
    q_spec, k_spec, v_spec, p_spec, space_spec, time_spec = attention_specs(rows, heads // 2)
    width = heads * 64
    return pl.pallas_call(
        attend_back_kernel,
        grid=(heads // 2, windows),
        in_specs=[q_spec, k_spec, v_spec, q_spec, q_spec, p_spec],
        out_specs=[
            pl.BlockSpec((3, rows, 128), lambda pair, window: (0, window, pair)),
            space_spec,
            time_spec,
        ],
        out_shape=[
            jax.ShapeDtypeStruct((3, windows * rows, width), bf16),
            jax.ShapeDtypeStruct((heads, SPATIAL, rows), f32),
            jax.ShapeDtypeStruct((windows, heads, 8, rows), f32),
        ],
        compiler_params=pltpu.CompilerParams(vmem_limit_bytes=VMEM_LIMIT),
        cost_estimate=pl.CostEstimate(
            flops=40 * windows * heads * rows * rows * 64,
            bytes_accessed=windows * heads * rows * rows * 2,
            transcendentals=0,
        ),
        name="attend_back",
    )(projected, projected, projected, grad_attended, attended, probs)


def normalize(values_in):
    centred = values_in - jnp.mean(values_in, axis=-1, keepdims=True)
    inverse = lax.rsqrt(jnp.mean(centred * centred, axis=-1, keepdims=True) + EPS)
    return centred * inverse, inverse


def normalize_back(grad_normed, normed, inverse):
    return inverse * (
        grad_normed
        - jnp.mean(grad_normed, axis=-1, keepdims=True)
        - normed * jnp.mean(grad_normed * normed, axis=-1, keepdims=True)
    )


def space_onehot():
    places = jnp.arange(SPATIAL, dtype=jnp.int32)
    across, along = places // SIDE, places % SIDE
    index = (across[:, None] - across[None, :] + SIDE - 1) * (2 * SIDE - 1) + (
        along[:, None] - along[None, :] + SIDE - 1
    )
    ids = jnp.arange((2 * SIDE - 1) ** 2, dtype=jnp.int32)
    return (index.reshape(-1)[:, None] == ids[None, :]).astype(f32)


def dot32(left, right, dims):
    return lax.dot_general(left, right, (dims, ((), ())), preferred_element_type=f32)


def on_device(
    tokens,
    condition,
    doubled,
    window_count,
    w_ada,
    b_ada,
    w_qkv,
    w_out,
    w_up,
    b_up,
    w_down,
    b_down,
    table_space,
    table_time,
    cotangent,
):
    windows, _, width = tokens.shape
    heads = table_space.shape[0]
    n_win = lax.axis_size("win")
    devices = n_win * 4
    win = lax.axis_index("win")
    frm = lax.axis_index("frm")
    z, x, y, c = win // 2, win % 2, frm // 2, frm % 2
    where = jnp.stack([z, x, y, c]).astype(jnp.int32)
    local = windows // 4
    ff = w_up.shape[1]
    ff_block = ff // devices
    shard_rows = w_qkv.shape[0]

    split_ff = pick(w_up.reshape(shard_rows, n_win * 2, 2, ff_block), c, 2)
    up_shard = split_ff.reshape(shard_rows, ff // 2)
    down_shard = pick(w_down.reshape(2, 2, ff_block, width), c, 1).reshape(2 * ff_block, width)
    attn_shard = pick(
        jnp.concatenate([w_qkv, w_out], axis=1).reshape(2, shard_rows // 2, 4 * width), c, 0
    )

    token_rows = windows_in(tokens, doubled, y, c)
    own_columns = b_ada.shape[0], b_up.shape[0], b_down.shape[0]
    small = jnp.concatenate([condition.reshape(-1), b_ada, b_up, b_down])
    small_all = lax.all_to_all(
        jnp.broadcast_to(small[None], (n_win, small.shape[0])),
        "win",
        split_axis=0,
        concat_axis=0,
        tiled=True,
    )
    attn_full = gather_weight(attn_shard, where, True).reshape(width, 4 * width)
    up_full = gather_weight(up_shard, where, False).reshape(width, ff // 2)
    down_full = gather_weight(down_shard, where, False).reshape(ff // 2, width)

    cond_size = windows * width
    cond_all = small_all[:, :cond_size].reshape(n_win * windows, width).astype(f32)
    cuts = [cond_size, cond_size + own_columns[0], cond_size + own_columns[0] + own_columns[1]]
    ada_bias = small_all[:, cuts[0] : cuts[1]].reshape(-1).astype(f32)
    up_bias = small_all[:, cuts[1] : cuts[2]].reshape(n_win * 2, 2, ff_block)
    up_bias = pick(up_bias, c, 1).reshape(-1).astype(f32)
    down_bias = small_all[:, cuts[2] :].reshape(-1).astype(f32)

    silu_all = jax.nn.silu(cond_all).astype(bf16)
    silu_part = lax.dynamic_slice_in_dim(silu_all, win * shard_rows, shard_rows, 1)
    ada_block = w_ada.shape[1] // devices
    ada_part = pick(w_ada.reshape(shard_rows, n_win, 4, ada_block), frm, 2)
    ada_part = ada_part.reshape(shard_rows, n_win * ada_block)
    mod_part = dot32(silu_part, ada_part, ((1,), (0,)))
    mod_parts = exchange_all(mod_part.reshape(devices, local, n_win * ada_block))
    modulation = jnp.sum(mod_parts.reshape(n_win, 4, local, n_win, ada_block), axis=0)
    modulation = jnp.transpose(modulation, (1, 2, 0, 3)).reshape(local, 6 * width) + ada_bias
    shift_one, scale_one, gate_one, shift_two, scale_two, gate_two = (
        block[:, None, :] for block in jnp.split(modulation, 6, axis=-1)
    )
    my_window = frm * local + jnp.arange(local, dtype=jnp.int32)
    live = (my_window < window_count[0]).astype(f32)[:, None, None]
    gate_one = gate_one * live
    gate_two = gate_two * live

    onehot_space = space_onehot()
    space_bias = jnp.dot(table_space, onehot_space.T, precision=exact_mode)
    space_bias = jnp.tile(space_bias.reshape(heads, SPATIAL, SPATIAL), (1, 1, FRAMES))
    mine_doubled = lax.dynamic_slice_in_dim(doubled, frm * local, local, 0)
    holders = jnp.arange(4, dtype=jnp.int32)
    frames = holders[None, :] + (holders[None, :] > mine_doubled[:, None]).astype(jnp.int32)
    frames = jnp.concatenate([frames, mine_doubled[:, None] + 1], axis=1)
    offset = frames[:, :, None] - frames[:, None, :] + FRAMES - 1
    onehot_time = (
        offset[..., None] == jnp.arange(table_time.shape[1], dtype=jnp.int32)
    ).astype(f32)
    time_bias = jnp.einsum("wabt,ht->whab", onehot_time, table_time, precision=exact_mode)
    time_bias = jnp.repeat(time_bias, SPATIAL, axis=-1)
    time_bias = jnp.pad(time_bias, ((0, 0), (0, 0), (0, 8 - FRAMES), (0, 0)))

    rows = FRAMES * SPATIAL
    token_full = token_rows.reshape(local, rows, width).astype(f32)
    normed_one, inverse_one = normalize(token_full)
    hidden_one = (normed_one * (1.0 + scale_one) + shift_one).astype(bf16)
    hidden_one = hidden_one.reshape(local * rows, width)
    qkv_full, out_full = attn_full[:, : 3 * width], attn_full[:, 3 * width :]
    projected = dot32(hidden_one, qkv_full, ((1,), (0,))).astype(bf16)
    attended, probs = attend(projected, space_bias, time_bias, local)
    branch_attn = dot32(attended, out_full, ((1,), (0,))).reshape(local, rows, width)
    mid = token_full + gate_one * branch_attn
    normed_two, inverse_two = normalize(mid)
    hidden_two = (normed_two * (1.0 + scale_two) + shift_two).astype(bf16)
    hidden_two = hidden_two.reshape(local * rows, width)

    grad_out = windows_in(cotangent, doubled, y, c).reshape(local, rows, width).astype(f32)
    grad_mlp = (gate_two * grad_out).astype(bf16).reshape(local * rows, width)
    hidden_both = jnp.concatenate([hidden_two, swap_core(hidden_two)])
    mlp_both = jnp.concatenate([grad_mlp, swap_core(grad_mlp)])
    pre_act = dot32(hidden_both, up_full, ((1,), (0,))) + up_bias
    activated = jax.nn.gelu(pre_act).astype(bf16)
    grad_down_w = dot32(activated, mlp_both, ((0,), (0,))).astype(bf16)
    down_grad = scatter_sum(grad_down_w.reshape(n_win, 2, ff_block, width), where)
    grad_activated = dot32(mlp_both, down_full, ((1,), (1,)))
    _, gelu_back = jax.vjp(jax.nn.gelu, pre_act)
    grad_pre = gelu_back(grad_activated)[0].astype(bf16)
    grad_up_w = dot32(grad_pre, hidden_both, ((0,), (0,))).astype(bf16)
    up_grad = scatter_sum(grad_up_w.reshape(n_win, 2, ff_block, width), where)
    grad_hidden_both = dot32(grad_pre, up_full, ((1,), (1,)))
    count = local * rows
    grad_hidden_two = (
        grad_hidden_both[:count]
        + swap_core(grad_hidden_both[count:].astype(bf16)).astype(f32)
    ).reshape(local, rows, width)
    mlp_part = dot32(activated, down_full, ((1,), (0,)))
    branch_mlp = mlp_part[:count] + swap_core(mlp_part[count:].astype(bf16)).astype(f32)
    branch_mlp = (branch_mlp + down_bias).reshape(local, rows, width)
    result = (mid + gate_two * branch_mlp).astype(bf16)
    result_back = windows_out(result.reshape(local, FRAMES, SPATIAL, width), y, c)

    grad_mid = grad_out + normalize_back(
        grad_hidden_two * (1.0 + scale_two), normed_two, inverse_two
    )
    grad_branch = (gate_one * grad_mid).astype(bf16).reshape(count, width)
    grad_attended = dot32(grad_branch, out_full, ((1,), (1,))).astype(bf16)
    grad_out_w = dot32(grad_branch, attended, ((0,), (0,))).astype(bf16)
    grad_projected, space_sums, time_sums = attend_back(
        projected, grad_attended, attended, probs, local
    )
    grad_qkv_w = lax.dot_general(
        grad_projected, hidden_one, (((1,), (0,)), ((), ())), preferred_element_type=f32
    ).astype(bf16)
    qkv_block, out_block = 3 * width // devices, width // devices
    grad_attn_w = jnp.concatenate(
        [
            grad_qkv_w.reshape(n_win, 2, 2, qkv_block, width),
            grad_out_w.reshape(n_win, 2, 2, out_block, width),
        ],
        axis=3,
    )
    attn_own = pick(grad_attn_w, c, 2)
    attn_other = swap_core(pick(grad_attn_w, 1 - c, 2))
    attn_grad = scatter_sum(add_low(attn_own, attn_other), where)
    grad_hidden_one = lax.dot_general(
        grad_projected[0], qkv_full[:, :width], (((1,), (1,)), ((), ())), preferred_element_type=f32
    )
    for part in (1, 2):
        grad_hidden_one = grad_hidden_one + dot32(
            grad_projected[part], qkv_full[:, part * width : (part + 1) * width], ((1,), (1,))
        )
    grad_hidden_one = grad_hidden_one.reshape(local, rows, width)
    grad_tokens = grad_mid + normalize_back(
        grad_hidden_one * (1.0 + scale_one), normed_one, inverse_one
    )
    tokens_back = windows_out(
        grad_tokens.astype(bf16).reshape(local, FRAMES, SPATIAL, width), y, c
    )

    row_live = jnp.stack([jnp.ones_like(doubled, dtype=bool), doubled == frm], axis=1)
    window_live = jnp.arange(windows, dtype=jnp.int32) < window_count[0]
    row_live = (row_live & window_live[:, None])[:, :, None, None]
    slots = (windows, 2, SPATIAL, width)
    result = jnp.where(row_live, result_back, tokens.reshape(slots)).reshape(tokens.shape)
    grad_tokens = jnp.where(
        row_live, tokens_back.astype(f32), cotangent.reshape(slots).astype(f32)
    ).reshape(tokens.shape)

    grad_mod = jnp.concatenate(
        [
            jnp.sum(grad_hidden_one, axis=1),
            jnp.sum(grad_hidden_one * normed_one, axis=1),
            jnp.sum(live * branch_attn * grad_mid, axis=1),
            jnp.sum(grad_hidden_two, axis=1),
            jnp.sum(grad_hidden_two * normed_two, axis=1),
            jnp.sum(live * branch_mlp * grad_out, axis=1),
        ],
        axis=-1,
    ).astype(bf16)
    mod_send = jnp.transpose(grad_mod.reshape(local, n_win, 4, ada_block), (2, 0, 1, 3))
    mod_send = jnp.broadcast_to(mod_send[None], (n_win, 4, local, n_win, ada_block))
    mod_got = exchange_all(mod_send.reshape(devices, local, n_win * ada_block))
    mod_got = mod_got.reshape(n_win * windows, n_win * ada_block)
    mod_own = lax.dynamic_slice_in_dim(mod_got, win * ada_block, ada_block, 1)
    grad_ada_w = dot32(silu_all, mod_own, ((0,), (0,)))
    grad_ada_b = jnp.sum(mod_own.astype(f32), axis=0)
    cond_part = dot32(mod_got, ada_part, ((1,), (1,)))

    grad_up_b = jnp.sum(grad_pre.astype(f32), axis=0).reshape(n_win * 2, 1, ff_block)
    core_mask = (jnp.arange(2, dtype=jnp.int32) == c).astype(f32)[None, :, None]
    grad_up_b = (grad_up_b * core_mask).reshape(devices, ff_block)
    grad_down_b = jnp.sum(grad_mlp.astype(f32), axis=0).reshape(devices, width // devices)
    space_sum = jnp.sum(space_sums.reshape(heads, SPATIAL, FRAMES, SPATIAL), axis=2)
    space_sum = jnp.dot(
        space_sum.reshape(heads, SPATIAL * SPATIAL), onehot_space, precision=exact_mode
    )
    time_sum = jnp.sum(
        time_sums[:, :, :FRAMES].reshape(local, heads, FRAMES, FRAMES, SPATIAL), axis=-1
    )
    time_sum = jnp.einsum("whab,wabt->ht", time_sum, onehot_time, precision=exact_mode)
    tables = jnp.concatenate([space_sum.reshape(-1), time_sum.reshape(-1)])
    share = -(-tables.shape[0] // devices)
    tables = jnp.pad(tables, (0, share * devices - tables.shape[0])).reshape(devices, share)
    sums = jnp.concatenate([grad_up_b, grad_down_b, tables], axis=1)
    sums = jnp.sum(exchange_all(sums), axis=0)
    out_up_b = sums[:ff_block]
    out_down_b = sums[ff_block : ff_block + width // devices]
    table_share = sums[ff_block + width // devices :]

    cond_send = cond_part.reshape(n_win, 1, windows * shard_rows)
    cond_send = jnp.broadcast_to(cond_send, (n_win, 4, windows * shard_rows))
    cond_send = cond_send.reshape(devices, windows * shard_rows)
    last_send = jnp.concatenate(
        [cond_send, jnp.broadcast_to(table_share[None], (devices, share))], axis=1
    )
    last_got = exchange_all(last_send)
    cond_grad = last_got[:, : windows * shard_rows].reshape(n_win, 4, windows, shard_rows)
    cond_grad = jnp.transpose(jnp.sum(cond_grad, axis=1), (1, 0, 2)).reshape(windows, width)
    _, silu_back = jax.vjp(jax.nn.silu, condition.astype(f32))
    grad_condition = silu_back(cond_grad)[0]
    table_all = last_got[:, windows * shard_rows :].reshape(-1)
    space_size = table_space.size
    grad_space = table_all[:space_size].reshape(table_space.shape)
    grad_time = table_all[space_size : space_size + table_time.size].reshape(table_time.shape)

    return (
        result,
        grad_tokens,
        grad_condition,
        grad_ada_w,
        grad_ada_b,
        attn_grad[:qkv_block].T,
        attn_grad[qkv_block:].T,
        up_grad.T,
        out_up_b,
        down_grad,
        out_down_b,
        grad_space,
        grad_time,
    )


def solution(mesh):
    return jax.shard_map(
        on_device,
        mesh=mesh,
        in_specs=(
            P("win", "frm", None),
            P("win", None),
            P("win"),
            P("win"),
            P("win", None),
            P("win"),
            P("win", None),
            P("win", None),
            P("win", None),
            P("win"),
            P("win", None),
            P("win"),
            P(),
            P(),
            P("win", "frm", None),
        ),
        out_specs=(
            P("win", "frm", None),
            P("win", "frm", None),
            P("win", None),
            P(None, BOTH),
            P(BOTH),
            P(None, BOTH),
            P(None, BOTH),
            P(None, BOTH),
            P(BOTH),
            P(BOTH, None),
            P(BOTH),
            P(),
            P(),
        ),
        check_vma=False,
    )
```

```python
import functools

import jax
import jax.numpy as jnp
from jax import lax
from jax.experimental import pallas as pl
from jax.experimental.pallas import tpu as pltpu
from jax.sharding import PartitionSpec as P

SIDE = 8
FRAMES = 5
SPATIAL = SIDE * SIDE
BOTH = ("win", "frm")
EPS = 1e-06
VMEM_LIMIT = 50 * 1024 * 1024

f32 = jnp.float32
bf16 = jnp.bfloat16
exact_mode = lax.Precision.HIGHEST
SMALL = pl.CostEstimate(flops=1024, bytes_accessed=1024, transcendentals=0)


def swap_frm(array, bit):
    return lax.ppermute(array, "frm", [(j, j ^ bit) for j in range(4)])


def swap_core(array):
    return swap_frm(array, 1)


def swap_y(array):
    return swap_frm(array, 2)


def swap_win(array, bits):
    count = lax.axis_size("win")
    return lax.ppermute(array, "win", [(j, j ^ bits) for j in range(count)])


def exchange_all(array):
    return lax.all_to_all(array, BOTH, split_axis=0, concat_axis=0, tiled=True)


def pick(array, index, axis):
    return lax.dynamic_index_in_dim(array, index, axis, keepdims=False)


def sync(*arrays):
    return lax.optimization_barrier(arrays)


def exchange_z(blocks):
    groups = [[2 * z + x for z in range(4)] for x in range(2)]
    return lax.all_to_all(
        blocks, "win", split_axis=0, concat_axis=0, axis_index_groups=groups, tiled=True
    )


def gather_z(half):
    return exchange_z(jnp.broadcast_to(half[None], (4,) + half.shape))


def gather_z_direct(half):
    return [half] + [swap_win(half, 2 * k) for k in (1, 2, 3)]


def move_kernel(body, count, where, *refs):
    sems = refs[count]
    refs = refs[:count] + refs[count + 1 :]
    waits = []

    def copy(sources, target):
        sem = sems.at[len(waits)]
        if len(sources) == 1:
            pltpu.make_async_copy(sources[0], target, sem).start()
        else:
            condition, first, second = sources

            @pl.when(condition)
            def _():
                pltpu.make_async_copy(first, target, sem).start()

            @pl.when(jnp.logical_not(condition))
            def _():
                pltpu.make_async_copy(second, target, sem).start()

        waits.append(pltpu.make_async_copy(sources[-1], target, sem))

    def finish():
        for wait in waits:
            wait.wait()

    body(where, refs, copy, finish)


def move_call(body, name, where, inputs, outputs, copies, scratch=()):
    return pl.pallas_call(
        functools.partial(move_kernel, body, len(inputs) + len(outputs)),
        out_shape=outputs,
        in_specs=[pl.BlockSpec(memory_space=pltpu.SMEM)]
        + [pl.BlockSpec(memory_space=pl.ANY)] * len(inputs),
        out_specs=[pl.BlockSpec(memory_space=pltpu.VMEM)] * len(outputs),
        scratch_shapes=[pltpu.SemaphoreType.DMA((copies,))] + list(scratch),
        compiler_params=pltpu.CompilerParams(vmem_limit_bytes=VMEM_LIMIT),
        cost_estimate=SMALL,
        name=name,
    )(where, *inputs)


def low_shape(*shape):
    return jax.ShapeDtypeStruct(shape, bf16)


def halves(where, w_qkv, w_out, w_up, w_down):
    rows, width = w_out.shape
    blocks = w_up.shape[1] // 256
    block = w_down.shape[0] // 4

    def body(where, refs, copy, finish):
        qkv, out, up, down, q_half, up_half, down_half = refs
        y, c = where[2], where[3]
        quarter = rows // 4
        q_rows = pl.ds(pl.multiple_of((c * 2 + y) * quarter, quarter), quarter)
        copy([qkv.at[q_rows]], q_half.at[:, pl.ds(0, 3 * width)])
        copy([out.at[q_rows]], q_half.at[:, pl.ds(3 * width, width)])
        up_rows = pl.ds(pl.multiple_of(y * (rows // 2), rows // 2), rows // 2)
        for n in range(blocks):
            column = pl.multiple_of((2 * n + c) * 128, 128)
            copy([up.at[up_rows, pl.ds(column, 128)]], up_half.at[:, pl.ds(n * 128, 128)])
        copy([down.at[pl.ds(pl.multiple_of((y * 2 + c) * block, block), block)]], down_half)
        finish()

    return move_call(
        body,
        "halves",
        where,
        [w_qkv, w_out, w_up, w_down],
        [
            low_shape(rows // 4, 4 * width),
            low_shape(rows // 2, blocks * 128),
            low_shape(block, width),
        ],
        blocks + 3,
    )


def gather_near(along_z):
    return [along_z, swap_win(along_z, 1), swap_y(along_z)]


def gather_far(near, cut=0):
    if not cut:
        return [swap_win(near[2], 1)]
    return [swap_y(near[1][:cut]), swap_win(near[2][cut:], 1)]


PLACES = ((0, 0), (1, 0), (0, 1), (1, 1))


def piece(refs, number, k):
    if number < 3 or len(refs) == 4:
        return refs[number].at[k]
    cut = refs[3].shape[0]
    return refs[3].at[k] if k < cut else refs[4].at[k - cut]


def place_qkv(where, pieces):
    _, rows, columns = pieces[0].shape
    width = columns // 4

    def body(where, refs, copy, finish):
        z, x, y, c = where[0], where[1], where[2], where[3]
        for core in range(2):
            for n, (j, l) in enumerate(PLACES):
                for k in range(4):
                    source = piece(refs[4 * core : 4 * core + 4], n, k)
                    at = ((z ^ k) * 2 + (x ^ j), c ^ core, y ^ l)
                    copy([source.at[:, pl.ds(0, 3 * width)]], refs[8].at[at])
                    copy([source.at[:, pl.ds(3 * width, width)]], refs[9].at[at])
        finish()

    qkv, out = move_call(
        body,
        "place_qkv",
        where,
        pieces,
        [low_shape(8, 2, 2, rows, 3 * width), low_shape(8, 2, 2, rows, width)],
        64,
    )
    return qkv.reshape(32 * rows, 3 * width), out.reshape(32 * rows, width)


def place_up(where, pieces):
    _, rows, columns = pieces[0].shape

    def body(where, refs, copy, finish):
        z, x, y = where[0], where[1], where[2]
        for n, (j, l) in enumerate(PLACES):
            for k in range(4):
                copy([piece(refs[:4], n, k)], refs[4].at[(z ^ k) * 2 + (x ^ j), y ^ l])
        finish()

    return move_call(
        body, "place_up", where, pieces, [low_shape(8, 2, rows, columns)], 16
    )[0].reshape(16 * rows, columns)


def place_down(where, pieces):
    _, rows, columns = pieces[0].shape

    def body(where, refs, copy, finish):
        for n in range(4):
            for k in range(4):
                quarter = QUARTERS.index(PLACES[n])
                copy([piece(refs[:5], n, k)], refs[5].at[quarter, where[0] ^ k])
        finish()

    return move_call(
        body, "place_down", where, pieces, [low_shape(4, 4, rows, columns)], 16
    )[0].reshape(16 * rows, columns)


QUARTERS = ((1, 1), (1, 0), (0, 1), (0, 0))


FAR_CUT = 2
LAST_CUT = 1


def add_low(*terms):
    return functools.reduce(jnp.add, [term.astype(f32) for term in terms]).astype(bf16)


def block_specs(array, first, cut=0):
    if array.ndim == 4:
        return pl.BlockSpec((1, 1) + array.shape[2:], lambda i: (first, i, 0, 0))
    rows = array.shape[0] // (4 if first is None else first)
    last = array.shape[0] // rows - 1
    return pl.BlockSpec((rows, array.shape[1]), lambda i: (jnp.clip(i - cut, 0, last), 0))


def read(ref):
    return ref[...].reshape(ref.shape[-2:]).astype(f32)


def merge_kernel(counts, cut, *refs):
    x_terms, y_terms = refs[: counts[0]], refs[counts[0] : counts[0] + counts[1]]
    far_y, far_x, send_x, send_y = refs[-4:]
    first = pl.program_id(0) < cut
    to_x = functools.reduce(jnp.add, [read(ref) for ref in x_terms])
    to_y = functools.reduce(jnp.add, [read(ref) for ref in y_terms])
    send_x[...] = jnp.where(first, to_x + read(far_y), to_x).astype(bf16)
    send_y[...] = jnp.where(first, to_y, to_y + read(far_x)).astype(bf16)


def merge(x_terms, y_terms, far_y, far_x, cut=FAR_CUT):
    rows, width = far_y.shape[0] // cut, far_y.shape[1]
    block = pl.BlockSpec((rows, width), lambda i: (i, 0))
    return dense_call(
        functools.partial(merge_kernel, (len(x_terms), len(y_terms)), cut),
        "merge",
        (4,),
        [block_specs(*term) for term in list(x_terms) + list(y_terms)]
        + [block_specs(far_y, cut), block_specs(far_x, 4 - cut, cut)],
        [block, block],
        [low_shape(4 * rows, width)] * 2,
    )(*[term[0] for term in list(x_terms) + list(y_terms)], far_y, far_x)


def total_kernel(*refs):
    refs[-1][...] = functools.reduce(jnp.add, [read(ref) for ref in refs[:-1]]).astype(bf16)


def total(terms, rows, width):
    return dense_call(
        total_kernel,
        "total",
        (4,),
        [block_specs(*term) for term in terms],
        pl.BlockSpec((rows, width), lambda i: (i, 0)),
        low_shape(4 * rows, width),
    )(*[term[0] for term in terms])


def first_kernel(own_ref, got_ref, far_y, far_x, x_ref):
    far = own_ref[0].astype(f32) + got_ref[0].astype(f32)
    far_y[...] = far[:LAST_CUT].astype(bf16).reshape(far_y.shape)
    far_x[...] = far[LAST_CUT:].astype(bf16).reshape(far_x.shape)
    x_ref[...] = (own_ref[1].astype(f32) + got_ref[1].astype(f32)).astype(bf16).reshape(x_ref.shape)


def first_quarters(own, got):
    _, _, rows, width = own.shape
    shapes = [(LAST_CUT * rows, width), ((4 - LAST_CUT) * rows, width), (4 * rows, width)]
    return dense_call(
        first_kernel,
        "first_quarters",
        (1,),
        [full_spec(own.shape)] * 2,
        [full_spec(shape) for shape in shapes],
        [low_shape(*shape) for shape in shapes],
    )(own, got)


def sum_z(kept):
    blocks = kept.reshape((4, kept.shape[0] // 4) + kept.shape[1:])
    return jnp.sum(exchange_z(blocks).astype(f32), axis=0)


def sum_z_direct(kept, z):
    blocks = kept.reshape((4, kept.shape[0] // 4) + kept.shape[1:])
    sent = [swap_win(pick(blocks, z ^ k, 0), 2 * k) for k in (1, 2, 3)]
    return functools.reduce(jnp.add, [part.astype(f32) for part in [pick(blocks, z, 0)] + sent])


def scatter_plain(grad, where):
    mine = lax.psum_scatter(grad.astype(f32), "win", scatter_dimension=0, tiled=False)
    return pick(mine, where[2], 0) + swap_y(pick(mine, 1 - where[2], 0))


def windows_send(where, slots):
    def body(where, refs, copy, finish):
        for half in range(2):
            first = half * 8 + (1 - where[3]) * 4
            copy([refs[0].at[pl.ds(first, 4)]], refs[1].at[pl.ds(half * 4, 4)])
        finish()

    return move_call(body, "rows_send", where, [slots], [low_shape(8, *slots.shape[1:])], 2)[0]


def windows_pack(where, slots, got):
    def body(where, refs, copy, finish):
        own, other, here, away = refs
        y, c = where[2], where[3]
        for target, half in ((here, y), (away, 1 - y)):
            for t in range(2):
                window = half * 4 + c * 2 + t
                mine, theirs = window * 2, half * 4 + t * 2
                copy([c == 0, own.at[mine], other.at[theirs]], target.at[t * 3])
                copy([c == 0, other.at[theirs], own.at[mine]], target.at[t * 3 + 1])
                copy(
                    [where[6 + window] == where[4], own.at[mine + 1], other.at[theirs + 1]],
                    target.at[t * 3 + 2],
                )
        finish()

    shape = low_shape(6, *slots.shape[1:])
    return move_call(body, "rows_pack", where, [slots, got], [shape, shape], 12)


def windows_join(where, here, away):
    def body(where, refs, copy, finish):
        here, away, out = refs
        y = where[2]
        for t in range(2):
            for slot in range(4):
                source = t * 3 + slot % 2
                copy([y == slot // 2, here.at[source], away.at[source]], out.at[t * 5 + slot])
            near = where[6 + where[4] * 2 + t] // 2 == y
            copy([near, here.at[t * 3 + 2], away.at[t * 3 + 2]], out.at[t * 5 + 4])
        finish()

    shape = low_shape(10, *here.shape[1:])
    out = move_call(body, "rows_join", where, [here, away], [shape], 10)[0]
    return out.reshape(10 * here.shape[1], here.shape[2])


def windows_back_pack(where, rows, back):
    def body(where, refs, copy, finish):
        rows, back, out = refs
        y, c = where[2], where[3]
        for t in range(2):
            here, there = y * 4 + t * 2, (1 - y) * 4 + t * 2
            copy([rows.at[t * 5 + 2 * y + 1 - c]], out.at[here])
            copy([rows.at[t * 5 + 4]], out.at[here + 1])
            copy([back.at[t * 3 + 1 - c]], out.at[there])
            copy([back.at[t * 3 + 2]], out.at[there + 1])
        finish()

    slots = rows.reshape(10, SPATIAL, rows.shape[1])
    shape = low_shape(8, SPATIAL, rows.shape[1])
    return move_call(body, "rows_back_pack", where, [slots, back], [shape], 8)[0]


def windows_back_join(where, rows, back, got, dead, dtype):
    width = rows.shape[1]

    def body(where, refs, copy, finish):
        rows, back, got, dead, out, arrived = refs
        y, c, frm, count = where[2], where[3], where[4], where[5]
        for half in range(2):
            side = y if half == 0 else 1 - y
            for core in range(2):
                for t in range(2):
                    window = side * 4 + (c if core == 0 else 1 - c) * 2 + t
                    if core == 1:
                        even, odd = got.at[side * 4 + t * 2], got.at[side * 4 + t * 2 + 1]
                    elif half == 0:
                        even, odd = rows.at[t * 5 + 2 * y + c], rows.at[t * 5 + 4]
                    else:
                        even, odd = back.at[t * 3 + c], back.at[t * 3 + 2]
                    live = window < count
                    place = window * 2
                    copy([live, even, dead.at[place]], arrived.at[place])
                    doubled = jnp.logical_and(live, where[6 + window] == frm)
                    copy([doubled, odd, dead.at[place + 1]], arrived.at[place + 1])
        finish()
        out[...] = arrived[...].astype(out.dtype)

    slots = rows.reshape(10, SPATIAL, width)
    out = move_call(
        body,
        "rows_back_join",
        where,
        [slots, back, got, dead.reshape(16, SPATIAL, width)],
        [jax.ShapeDtypeStruct((16, SPATIAL, width), dtype)],
        16,
        [pltpu.VMEM((16, SPATIAL, width), bf16)],
    )[0]
    return out.reshape(dead.shape)


def head_lanes(head):
    lanes = lax.broadcasted_iota(jnp.int32, (1, 128), 1)
    return (lanes // 64) == head


def attend_kernel(q_ref, k_ref, v_ref, space_ref, time_ref, o_ref, p_ref):
    q, k, v = q_ref[...], k_ref[...], v_ref[...]
    rows = q.shape[0]
    total = jnp.zeros((rows, 128), f32)
    for head in range(2):
        lanes = head_lanes(head)
        scaled = jnp.where(lanes, q * jnp.asarray(0.125, bf16), jnp.zeros_like(q))
        scores = lax.dot_general(scaled, k, (((1,), (1,)), ((), ())), preferred_element_type=f32)
        shaped = scores.reshape(rows // SPATIAL, SPATIAL, rows)
        shaped = shaped + space_ref[head][None] + time_ref[0, head, : rows // SPATIAL][:, None, :]
        scores = shaped.reshape(rows, rows)
        grown = jnp.exp(scores - jnp.max(scores, axis=-1, keepdims=True))
        inverse = 1.0 / jnp.sum(grown, axis=-1, keepdims=True)
        probs = (grown * inverse).astype(bf16)
        p_ref[0, head] = probs
        masked = jnp.where(lanes, v, jnp.zeros_like(v))
        total = total + jnp.dot(probs, masked, preferred_element_type=f32)
    o_ref[...] = total.astype(bf16)


def attend_back_kernel(
    q_ref, k_ref, v_ref, do_ref, o_ref, p_ref, grad_ref, space_ref, time_ref
):
    q, k, v, do = q_ref[...], k_ref[...], v_ref[...], do_ref[...]
    rows = q.shape[0]
    slots = rows // SPATIAL
    product = do.astype(f32) * o_ref[...].astype(f32)
    grad_q = jnp.zeros((rows, 128), f32)
    grad_k = jnp.zeros((rows, 128), f32)
    grad_v = jnp.zeros((rows, 128), f32)

    @pl.when(pl.program_id(1) == 0)
    def _():
        space_ref[...] = jnp.zeros_like(space_ref)

    for head in range(2):
        lanes = head_lanes(head)
        none = jnp.zeros_like(q)
        scale = jnp.asarray(0.125, bf16)
        row_dot = jnp.sum(jnp.where(lanes, product, 0.0), axis=-1, keepdims=True)
        grads = jnp.where(lanes, do, none)
        probs = p_ref[0, head]
        grad_probs = lax.dot_general(
            grads, v, (((1,), (1,)), ((), ())), preferred_element_type=f32
        )
        grad_scores = probs.astype(f32) * (grad_probs - row_dot)
        low = grad_scores.astype(bf16)
        over_rows = (((0,), (0,)), ((), ()))
        grad_v = grad_v + lax.dot_general(probs, grads, over_rows, preferred_element_type=f32)
        grad_k = grad_k + lax.dot_general(
            low, jnp.where(lanes, q * scale, none), over_rows, preferred_element_type=f32
        )
        grad_q = grad_q + jnp.dot(
            low, jnp.where(lanes, k * scale, none), preferred_element_type=f32
        )
        shaped = grad_scores.reshape(slots, SPATIAL, rows)
        space_ref[head] += jnp.sum(shaped, axis=0)
        time_ref[0, head, :slots] = jnp.sum(shaped, axis=1)
    grad_ref[0] = grad_q.astype(bf16)
    grad_ref[1] = grad_k.astype(bf16)
    grad_ref[2] = grad_v.astype(bf16)


def attention_specs(rows, pairs):
    q_spec = pl.BlockSpec((rows, 128), lambda pair, window: (window, pair))
    k_spec = pl.BlockSpec((rows, 128), lambda pair, window: (window, pair + pairs))
    v_spec = pl.BlockSpec((rows, 128), lambda pair, window: (window, pair + 2 * pairs))
    p_spec = pl.BlockSpec((1, 2, rows, rows), lambda pair, window: (window, pair, 0, 0))
    space_spec = pl.BlockSpec((2, SPATIAL, rows), lambda pair, window: (pair, 0, 0))
    time_spec = pl.BlockSpec((1, 2, 8, rows), lambda pair, window: (window, pair, 0, 0))
    return q_spec, k_spec, v_spec, p_spec, space_spec, time_spec


def attend(projected, space_bias, time_bias, windows):
    rows = projected.shape[0] // windows
    heads = space_bias.shape[0]
    q_spec, k_spec, v_spec, p_spec, space_spec, time_spec = attention_specs(rows, heads // 2)
    width = heads * 64
    return pl.pallas_call(
        attend_kernel,
        grid=(heads // 2, windows),
        in_specs=[q_spec, k_spec, v_spec, space_spec, time_spec],
        out_specs=[q_spec, p_spec],
        out_shape=[
            jax.ShapeDtypeStruct((windows * rows, width), bf16),
            jax.ShapeDtypeStruct((windows, heads, rows, rows), bf16),
        ],
        compiler_params=pltpu.CompilerParams(vmem_limit_bytes=VMEM_LIMIT),
        cost_estimate=SMALL,
        name="attend",
    )(projected, projected, projected, space_bias, time_bias)


def attend_back(projected, grad_attended, attended, probs, windows):
    heads, rows = probs.shape[1], probs.shape[2]
    q_spec, k_spec, v_spec, p_spec, space_spec, time_spec = attention_specs(rows, heads // 2)
    width = heads * 64
    return pl.pallas_call(
        attend_back_kernel,
        grid=(heads // 2, windows),
        in_specs=[q_spec, k_spec, v_spec, q_spec, q_spec, p_spec],
        out_specs=[
            pl.BlockSpec((3, rows, 128), lambda pair, window: (0, window, pair)),
            space_spec,
            time_spec,
        ],
        out_shape=[
            jax.ShapeDtypeStruct((3, windows * rows, width), bf16),
            jax.ShapeDtypeStruct((heads, SPATIAL, rows), f32),
            jax.ShapeDtypeStruct((windows, heads, 8, rows), f32),
        ],
        compiler_params=pltpu.CompilerParams(vmem_limit_bytes=VMEM_LIMIT),
        cost_estimate=SMALL,
        name="attend_back",
    )(projected, projected, projected, grad_attended, attended, probs)


def full_spec(shape):
    return pl.BlockSpec(shape, lambda *_: (0,) * len(shape))


def dense_call(kernel, name, grid, in_specs, out_specs, out_shape, scratch=()):
    return pl.pallas_call(
        kernel,
        grid=grid,
        in_specs=in_specs,
        out_specs=out_specs,
        out_shape=out_shape,
        scratch_shapes=list(scratch),
        compiler_params=pltpu.CompilerParams(vmem_limit_bytes=VMEM_LIMIT),
        cost_estimate=SMALL,
        name=name,
    )


def normalize(values_in):
    centred = values_in - jnp.mean(values_in, axis=-1, keepdims=True)
    inverse = lax.rsqrt(jnp.mean(centred * centred, axis=-1, keepdims=True) + EPS)
    return centred * inverse, inverse


def normalize_back(grad_normed, normed, inverse):
    return inverse * (
        grad_normed
        - jnp.mean(grad_normed, axis=-1, keepdims=True)
        - normed * jnp.mean(grad_normed * normed, axis=-1, keepdims=True)
    )


def dot32(left, right, dims):
    return lax.dot_general(left, right, (dims, ((), ())), preferred_element_type=f32)


def modulation(mod_ref, number, window=0):
    width = mod_ref.shape[2] // 6
    return mod_ref[window, :, number * width : (number + 1) * width]


PLAIN = ((1,), (0,))
RIGHT_T = ((1,), (1,))
LEFT_T = ((0,), (0,))


def qkv_kernel(tokens_ref, mod_ref, w_ref, projected_ref, hidden_ref):
    local = mod_ref.shape[0]
    rows = tokens_ref.shape[0] // local

    @pl.when(pl.program_id(0) == 0)
    def _():
        for window in range(local):
            part = pl.ds(window * rows, rows)
            normed, _ = normalize(tokens_ref[part, :].astype(f32))
            shift, scale = modulation(mod_ref, 0, window), modulation(mod_ref, 1, window)
            hidden_ref[part, :] = (normed * (1.0 + scale) + shift).astype(bf16)

    projected_ref[...] = dot32(hidden_ref[...], w_ref[...], PLAIN).astype(bf16)


def qkv_forward(tokens, mod, w_attn):
    count, width = tokens.shape
    tile = 512
    return dense_call(
        qkv_kernel,
        "qkv",
        (3 * width // tile,),
        [
            full_spec(tokens.shape),
            full_spec(mod.shape),
            pl.BlockSpec((width, tile), lambda i: (0, i)),
        ],
        [pl.BlockSpec((count, tile), lambda i: (0, i)), full_spec(tokens.shape)],
        [jax.ShapeDtypeStruct((count, 3 * width), bf16), jax.ShapeDtypeStruct((count, width), bf16)],
    )(tokens, mod, w_attn)


def out_kernel(attended_ref, w_ref, tokens_ref, mod_ref, branch_ref, mid_ref, hidden_ref):
    branch = dot32(attended_ref[...], w_ref[...], PLAIN)
    mid = tokens_ref[...].astype(f32) + modulation(mod_ref, 2) * branch
    normed, _ = normalize(mid)
    branch_ref[...] = branch.astype(bf16)
    mid_ref[...] = mid
    hidden_ref[...] = (normed * (1.0 + modulation(mod_ref, 4)) + modulation(mod_ref, 3)).astype(bf16)


def out_forward(attended, w_attn, tokens, mod):
    count, width = tokens.shape
    local = mod.shape[0]
    rows = count // local
    row_spec = pl.BlockSpec((rows, width), lambda i: (i, 0))
    return dense_call(
        out_kernel,
        "attn_out",
        (local,),
        [
            row_spec,
            full_spec((width, width)),
            row_spec,
            pl.BlockSpec((1,) + mod.shape[1:], lambda i: (i, 0, 0)),
        ],
        [row_spec] * 3,
        [
            jax.ShapeDtypeStruct((count, width), bf16),
            jax.ShapeDtypeStruct((count, width), f32),
            jax.ShapeDtypeStruct((count, width), bf16),
        ],
    )(attended, w_attn, tokens, mod)


def gelu_parts(value):
    factor = 0.7978845608028654
    square = value * value
    half = 0.5 + 0.5 * jnp.tanh(value * (factor + (factor * 0.044715) * square))
    gelu = value * half
    slope = half + gelu * (1.0 - half) * (2.0 * factor + (6.0 * factor * 0.044715) * square)
    return gelu, slope


def joined(refs, axis):
    parts = [ref[...] for ref in refs]
    return parts[0] if len(parts) == 1 else jnp.concatenate(parts, axis=axis)


def hidden_specs(width, tile, part, fast, rows):
    if not fast:
        return [pl.BlockSpec((rows, tile), lambda i, where: (0, 2 * part + i))]

    def block(z):
        def index(i, where):
            j, l = 1 - part, 1 - i
            return 0, z * 4 + (where[1] ^ j) * 2 + (where[2] ^ l)

        return pl.BlockSpec((rows, tile // 4), index)

    return [block(z) for z in range(4)]


def held_spec(shape):
    return pl.BlockSpec(shape, lambda i, where: (0,) * len(shape))


def hidden_call(kernel, name, where, inputs, in_specs, out_specs, out_shape, scratch=()):
    return pl.pallas_call(
        kernel,
        grid_spec=pltpu.PrefetchScalarGridSpec(
            num_scalar_prefetch=1,
            grid=(2,),
            in_specs=in_specs,
            out_specs=out_specs,
            scratch_shapes=list(scratch),
        ),
        out_shape=out_shape,
        compiler_params=pltpu.CompilerParams(vmem_limit_bytes=VMEM_LIMIT),
        cost_estimate=SMALL,
        name=name,
    )(where, *inputs)


def write_quarters(refs, value):
    @pl.when(pl.program_id(0) == 0)
    def _():
        start = 0
        for ref in refs[:-1]:
            ref[...] = value[start : start + ref.shape[0]].astype(bf16)
            start += ref.shape[0]

    @pl.when(pl.program_id(0) == 1)
    def _():
        refs[-1][...] = value.astype(bf16)


def quarter_shapes(tile, width, part):
    cut = FAR_CUT * tile // 4
    return [(tile, width)] * 2 if part else [(cut, width), (tile - cut, width), (tile, width)]


def up_kernel(pieces, where_ref, own_ref, other_ref, mlp_ref, mlp_other_ref, *refs):
    w, bias = joined(refs[:pieces], 1), joined(refs[pieces : 2 * pieces], 1)
    act_ref, slope_ref = refs[2 * pieces : 2 * pieces + 2]
    grad_refs = refs[2 * pieces + 2 :]
    total = None
    for half, (hidden, mlp) in enumerate(((own_ref, mlp_ref), (other_ref, mlp_other_ref))):
        activated, slope = gelu_parts(dot32(hidden[...], w, PLAIN) + bias)
        activated = activated.astype(bf16)
        act_ref[half] = activated
        slope_ref[half] = slope.astype(bf16)
        part = dot32(activated, mlp[...], LEFT_T)
        total = part if total is None else total + part
    write_quarters(grad_refs, total)


def up_forward(where, rows_both, w_up, bias, part, fast):
    count, width = rows_both[0].shape
    inner = w_up.shape[1]
    tile = inner // 4
    both = pl.BlockSpec((2, count, tile), lambda i, where: (0, 0, i))
    w_specs = hidden_specs(width, tile, part, fast, width)
    bias_specs = hidden_specs(width, tile, part, fast, 1)
    pieces = len(w_specs)
    return hidden_call(
        functools.partial(up_kernel, pieces),
        "mlp_up",
        where,
        list(rows_both) + [w_up] * pieces + [bias] * pieces,
        [held_spec((count, width))] * 4 + w_specs + bias_specs,
        [both, both] + [held_spec(shape) for shape in quarter_shapes(tile, width, part)],
        [low_shape(2, count, 2 * tile)] * 2
        + [low_shape(*shape) for shape in quarter_shapes(tile, width, part)],
    )


def down_back_kernel(pieces, part, where_ref, own_ref, other_ref, mlp_ref, mlp_other_ref, down_ref, *refs):
    up = joined(refs[:pieces], 1)
    slope_ref = refs[pieces]
    refs = refs[pieces + 1 :]
    earlier_ref = refs[0] if part else None
    outs = refs[1:] if part else refs
    quarters = 2 if part else 3
    grad_refs, bias_ref = outs[:quarters], outs[quarters]
    back_refs, total_ref = outs[quarters + 1 : -1], outs[-1]
    step = pl.program_id(0)
    down = down_ref[...]
    total, sums = None, None
    for half, (hidden, mlp) in enumerate(((own_ref, mlp_ref), (other_ref, mlp_other_ref))):
        grad_pre = dot32(mlp[...], down, RIGHT_T) * slope_ref[half].astype(f32)
        column = jnp.sum(grad_pre, axis=0, keepdims=True)
        grad_pre = grad_pre.astype(bf16)
        add = dot32(grad_pre, hidden[...], LEFT_T)
        total = add if total is None else total + add
        sums = column if sums is None else sums + column
        back = dot32(grad_pre, up, RIGHT_T)

        @pl.when(step == 0)
        def _(half=half, back=back):
            total_ref[half] = back + earlier_ref[half] if part else back

        @pl.when(step > 0)
        def _(half=half, back=back):
            total_ref[half] += back

    bias_ref[...] = sums
    write_quarters(grad_refs, total)

    @pl.when(step == 1)
    def _():
        if part:
            back_refs[0][...] = total_ref[0]
            back_refs[1][...] = total_ref[1].astype(bf16)
        else:
            back_refs[0][...] = total_ref[...]


def down_backward(where, rows_both, w_down, w_up, slope, part, earlier, fast):
    count, width = rows_both[0].shape
    inner = w_up.shape[1]
    tile = inner // 4
    back_shape = (2, count, width)
    if part:
        back_specs = [held_spec((count, width))] * 2
        back_shapes = [jax.ShapeDtypeStruct((count, width), f32), low_shape(count, width)]
    else:
        back_specs = [held_spec(back_shape)]
        back_shapes = [jax.ShapeDtypeStruct(back_shape, f32)]
    w_specs = hidden_specs(width, tile, part, fast, width)
    pieces = len(w_specs)
    return hidden_call(
        functools.partial(down_back_kernel, pieces, part),
        "mlp_back",
        where,
        list(rows_both) + [w_down] + [w_up] * pieces + [slope] + ([earlier] if part else []),
        [held_spec((count, width))] * 4
        + [pl.BlockSpec((tile, width), lambda i, where: (2 * part + i, 0))]
        + w_specs
        + [pl.BlockSpec((2, count, tile), lambda i, where: (0, 0, i))]
        + ([held_spec(back_shape)] if part else []),
        [held_spec(shape) for shape in quarter_shapes(tile, width, part)]
        + [pl.BlockSpec((1, tile), lambda i, where: (0, i))]
        + back_specs,
        [low_shape(*shape) for shape in quarter_shapes(tile, width, part)]
        + [jax.ShapeDtypeStruct((1, 2 * tile), f32)]
        + back_shapes,
        [pltpu.VMEM(back_shape, f32)],
    )


def down_kernel(first_ref, second_ref, w_ref, own_ref, other_ref):
    half = first_ref.shape[2]
    for number, out_ref in enumerate((own_ref, other_ref)):
        total = dot32(first_ref[number], w_ref[:half], PLAIN)
        total = total + dot32(second_ref[number], w_ref[half:], PLAIN)
        out_ref[...] = total.astype(out_ref.dtype)


def down_forward(first, second, w_down):
    _, count, half = first.shape
    width = w_down.shape[1]
    tile = 256
    row_spec = pl.BlockSpec((count, tile), lambda i: (0, i))
    return dense_call(
        down_kernel,
        "mlp_down",
        (width // tile,),
        [full_spec(first.shape)] * 2 + [pl.BlockSpec((2 * half, tile), lambda i: (0, i))],
        [row_spec, row_spec],
        [jax.ShapeDtypeStruct((count, width), f32), low_shape(count, width)],
    )(first, second, w_down)


def split_away(where_ref, rows_ref, away_ref):
    first = pl.multiple_of((1 - where_ref[2]) * 2 * SPATIAL, 2 * SPATIAL)
    away_ref[: 2 * SPATIAL] = rows_ref[pl.ds(first, 2 * SPATIAL), :]
    away_ref[2 * SPATIAL :] = rows_ref[4 * SPATIAL :, :]


def result_kernel(
    where_ref, own_ref, other_ref, bias_ref, mid_ref, cot_ref, mod_ref, live_ref,
    result_ref, away_ref, gate_ref,
):
    branch = own_ref[...] + other_ref[...].astype(f32) + bias_ref[...]
    result_ref[...] = (mid_ref[...] + modulation(mod_ref, 5) * branch).astype(bf16)
    split_away(where_ref, result_ref, away_ref)
    gate_ref[0] = live_ref[0] * jnp.sum(branch * cot_ref[...].astype(f32), axis=0, keepdims=True)


def result_forward(where, own, other, bias, mid, cotangent, mod, live):
    count, width = own.shape
    local = mod.shape[0]
    row_spec = pl.BlockSpec((count // local, width), lambda i: (i, 0))
    one = pl.BlockSpec((1, 1, width), lambda i: (i, 0, 0))
    return dense_call(
        result_kernel,
        "result",
        (local,),
        [pl.BlockSpec(memory_space=pltpu.SMEM)]
        + [row_spec, row_spec, full_spec(bias.shape), row_spec, row_spec]
        + [pl.BlockSpec((1,) + mod.shape[1:], lambda i: (i, 0, 0)), one],
        [row_spec, pl.BlockSpec((3 * SPATIAL, width), lambda i: (i, 0)), one],
        [
            low_shape(count, width),
            low_shape(local * 3 * SPATIAL, width),
            jax.ShapeDtypeStruct((local, 1, width), f32),
        ],
    )(where, own, other, bias, mid, cotangent, mod, live)


def mid_back_kernel(
    own_ref, other_ref, mid_ref, cot_ref, branch_ref, attended_ref, w_ref, mod_ref, live_ref,
    grad_mid_ref, grad_attended_ref, sums_ref, grad_ref, total_ref,
):
    step, last = pl.program_id(0), pl.num_programs(0) - 1
    grad_hidden = own_ref[...] + other_ref[...].astype(f32)
    normed, inverse = normalize(mid_ref[...])
    back = normalize_back(grad_hidden * (1.0 + modulation(mod_ref, 4)), normed, inverse)
    grad_mid = cot_ref[...].astype(f32) + back
    grad_mid_ref[...] = grad_mid
    gate = jnp.sum(branch_ref[...].astype(f32) * grad_mid, axis=0, keepdims=True)
    sums_ref[0, 0:1] = live_ref[0] * gate
    sums_ref[0, 1:2] = jnp.sum(grad_hidden, axis=0, keepdims=True)
    sums_ref[0, 2:3] = jnp.sum(grad_hidden * normed, axis=0, keepdims=True)
    grad_branch = (modulation(mod_ref, 2) * grad_mid).astype(bf16)
    grad_attended_ref[...] = dot32(grad_branch, w_ref[...], RIGHT_T).astype(bf16)
    part = dot32(grad_branch, attended_ref[...], LEFT_T)

    @pl.when(step == 0)
    def _():
        total_ref[...] = part

    @pl.when(step > 0)
    def _():
        total_ref[...] += part

    @pl.when(step == last)
    def _():
        grad_ref[...] = total_ref[...].astype(bf16)


def mid_backward(own, other, mid, cotangent, branch, attended, w_attn, mod, live):
    count, width = own.shape
    local = mod.shape[0]
    row_spec = pl.BlockSpec((count // local, width), lambda i: (i, 0))
    return dense_call(
        mid_back_kernel,
        "mid_back",
        (local,),
        [row_spec] * 6
        + [
            full_spec((width, width)),
            pl.BlockSpec((1,) + mod.shape[1:], lambda i: (i, 0, 0)),
            pl.BlockSpec((1, 1, width), lambda i: (i, 0, 0)),
        ],
        [
            row_spec,
            row_spec,
            pl.BlockSpec((1, 8, width), lambda i: (i, 0, 0)),
            full_spec((width, width)),
        ],
        [
            jax.ShapeDtypeStruct((count, width), f32),
            jax.ShapeDtypeStruct((count, width), bf16),
            jax.ShapeDtypeStruct((local, 8, width), f32),
            jax.ShapeDtypeStruct((width, width), bf16),
        ],
        [pltpu.VMEM((width, width), f32)],
    )(own, other, mid, cotangent, branch, attended, w_attn, mod, live)


def qkv_grad_kernel(where_ref, grad_ref, hidden_ref, out_grad_ref, *refs):
    outs, whole_ref, sems = refs[:4], refs[4], refs[5]
    x, y, c = where_ref[1], where_ref[2], where_ref[3]
    step, steps = pl.program_id(0), pl.num_programs(0)
    tile, width = whole_ref.shape[1:]
    block = whole_ref.shape[0] * tile // 32
    out_block = width // 32
    whole_ref[step] = dot32(grad_ref[0], hidden_ref[...], LEFT_T).astype(bf16)

    @pl.when(step == steps - 1)
    def _():
        def target(number, rows):
            z, j, l, core = number // 8, number // 4 % 2 ^ x, number // 2 % 2 ^ y, number % 2 ^ c
            quarter = (1 - j) * 2 + 1 - l
            for output in range(4):
                condition = jnp.logical_and(core == output // 2, quarter // 2 == output % 2)
                yield condition, outs[output].at[quarter % 2, z, rows]

        count = 0
        for number in range(32):
            first, rest, to = number * block, block, 0
            pieces = [(out_grad_ref.at[pl.ds(number * out_block, out_block)], block, out_block)]
            while rest:
                size = min(rest, tile - first % tile)
                pieces.append((whole_ref.at[first // tile, pl.ds(first % tile, size)], to, size))
                first, rest, to = first + size, rest - size, to + size
            for source, start, size in pieces:
                for condition, place in target(number, pl.ds(start, size)):

                    @pl.when(condition)
                    def _(source=source, place=place, count=count):
                        pltpu.make_async_copy(source, place, sems.at[count]).start()

                count += 1
        count = 0
        for number in range(32):
            first, rest = number * block, block
            sizes = [out_block]
            while rest:
                size = min(rest, tile - first % tile)
                sizes.append(size)
                first, rest = first + size, rest - size
            for size in sizes:
                place = outs[0].at[0, 0, pl.ds(0, size)]
                pltpu.make_async_copy(place, place, sems.at[count]).wait()
                count += 1


def qkv_grad(where, grad_projected, hidden, grad_out):
    count, width = hidden.shape
    tile = 512
    per = width // tile
    rows = 4 * width // 32
    shape = low_shape(2, 4, rows, width)
    return pl.pallas_call(
        qkv_grad_kernel,
        grid=(3 * per,),
        in_specs=[
            pl.BlockSpec(memory_space=pltpu.SMEM),
            pl.BlockSpec((1, count, tile), lambda i: (i // per, 0, i % per)),
            full_spec(hidden.shape),
            full_spec(grad_out.shape),
        ],
        out_specs=[pl.BlockSpec(memory_space=pl.ANY)] * 4,
        out_shape=[shape] * 4,
        scratch_shapes=[
            pltpu.VMEM((3 * per, tile, width), bf16),
            pltpu.SemaphoreType.DMA((32 * 3,)),
        ],
        compiler_params=pltpu.CompilerParams(vmem_limit_bytes=VMEM_LIMIT),
        cost_estimate=SMALL,
        name="qkv_grad",
    )(where, grad_projected, hidden, grad_out)


def qkv_grad_plain(grad_projected, hidden):
    return lax.dot_general(
        grad_projected, hidden, (((1,), (0,)), ((), ())), preferred_element_type=f32
    ).astype(bf16)


def tokens_back_kernel(
    where_ref, grad_ref, w_ref, tokens_ref, grad_mid_ref, mod_ref, out_ref, away_ref, sums_ref
):
    width = tokens_ref.shape[1]
    grad_hidden = None
    for part in range(3):
        add = dot32(grad_ref[part], w_ref[:, part * width : (part + 1) * width], RIGHT_T)
        grad_hidden = add if grad_hidden is None else grad_hidden + add
    normed, inverse = normalize(tokens_ref[...].astype(f32))
    back = normalize_back(grad_hidden * (1.0 + modulation(mod_ref, 1)), normed, inverse)
    out_ref[...] = (grad_mid_ref[...] + back).astype(bf16)
    split_away(where_ref, out_ref, away_ref)
    sums_ref[0, 0:1] = jnp.sum(grad_hidden, axis=0, keepdims=True)
    sums_ref[0, 1:2] = jnp.sum(grad_hidden * normed, axis=0, keepdims=True)


def tokens_backward(where, grad_projected, w_qkv, tokens, grad_mid, mod):
    count, width = tokens.shape
    local = mod.shape[0]
    rows = count // local
    row_spec = pl.BlockSpec((rows, width), lambda i: (i, 0))
    return dense_call(
        tokens_back_kernel,
        "tokens_back",
        (local,),
        [
            pl.BlockSpec(memory_space=pltpu.SMEM),
            pl.BlockSpec((3, rows, width), lambda i: (0, i, 0)),
            full_spec((width, 3 * width)),
            row_spec,
            row_spec,
            pl.BlockSpec((1,) + mod.shape[1:], lambda i: (i, 0, 0)),
        ],
        [
            row_spec,
            pl.BlockSpec((3 * SPATIAL, width), lambda i: (i, 0)),
            pl.BlockSpec((1, 8, width), lambda i: (i, 0, 0)),
        ],
        [
            low_shape(count, width),
            low_shape(local * 3 * SPATIAL, width),
            jax.ShapeDtypeStruct((local, 8, width), f32),
        ],
    )(where, grad_projected, w_qkv, tokens, grad_mid, mod)


def modulation_kernel(parts_ref, bias_ref, live_ref, out_ref):
    sources, holders, local, part = parts_ref.shape
    width = out_ref.shape[2] // 6
    for window in range(local):
        for holder in range(holders):
            total = parts_ref[0, holder, window : window + 1]
            for source in range(1, sources):
                total = total + parts_ref[source, holder, window : window + 1]
            columns = slice(holder * part, (holder + 1) * part)
            out_ref[window, :, columns] = total + bias_ref[:, columns]
        for gate in (2, 5):
            columns = slice(gate * width, (gate + 1) * width)
            out_ref[window, :, columns] = out_ref[window, :, columns] * live_ref[window]


def modulate(parts, bias, live):
    local, _, width = live.shape
    return dense_call(
        modulation_kernel,
        "modulation",
        (1,),
        [full_spec(parts.shape), full_spec(bias.shape), full_spec(live.shape)],
        full_spec((local, 1, 6 * width)),
        jax.ShapeDtypeStruct((local, 1, 6 * width), f32),
    )(parts, bias, live)


def gated_kernel(where_ref, rows_ref, mod_ref, out_ref):
    out_ref[...] = (modulation(mod_ref, 5) * rows_ref[...].astype(f32)).astype(bf16)


def gated(where, rows, mod):
    count, width = rows.shape
    local = mod.shape[0]
    row_spec = pl.BlockSpec((count // local, width), lambda i: (i, 0))
    return dense_call(
        gated_kernel,
        "gated",
        (local,),
        [
            pl.BlockSpec(memory_space=pltpu.SMEM),
            row_spec,
            pl.BlockSpec((1,) + mod.shape[1:], lambda i: (i, 0, 0)),
        ],
        row_spec,
        low_shape(count, width),
    )(where, rows, mod)


def space_onehot():
    places = jnp.arange(SPATIAL, dtype=jnp.int32)
    across, along = places // SIDE, places % SIDE
    index = (across[:, None] - across[None, :] + SIDE - 1) * (2 * SIDE - 1) + (
        along[:, None] - along[None, :] + SIDE - 1
    )
    ids = jnp.arange((2 * SIDE - 1) ** 2, dtype=jnp.int32)
    return (index.reshape(-1)[:, None] == ids[None, :]).astype(f32)


def on_device(
    tokens,
    condition,
    doubled,
    window_count,
    w_ada,
    b_ada,
    w_qkv,
    w_out,
    w_up,
    b_up,
    w_down,
    b_down,
    table_space,
    table_time,
    cotangent,
):
    windows, _, width = tokens.shape
    heads = table_space.shape[0]
    n_win = lax.axis_size("win")
    devices = n_win * 4
    win = lax.axis_index("win")
    frm = lax.axis_index("frm")
    z, x, y, c = win // 2, win % 2, frm // 2, frm % 2
    where = jnp.concatenate([jnp.stack([z, x, y, c, frm, window_count[0]]), doubled])
    where = where.astype(jnp.int32)
    local = windows // 4
    count = local * FRAMES * SPATIAL
    ff = w_up.shape[1]
    ff_block = ff // devices
    shard_rows = w_qkv.shape[0]
    half_width = width // 2
    fast = n_win == 8
    slot_shape = (2 * windows, SPATIAL, width)

    tok_slots, cot_slots = tokens.reshape(slot_shape), cotangent.reshape(slot_shape)
    tok_send = windows_send(where, tok_slots)
    biases = jnp.concatenate([b_ada, b_up, b_down])
    bias_rows = -(-biases.shape[0] // width)
    biases = jnp.pad(biases, (0, bias_rows * width - biases.shape[0])).reshape(bias_rows, width)
    small = jnp.concatenate([condition, biases])
    if fast:
        q_half, up_half, down_half = halves(where, w_qkv, w_out, w_up, w_down)
        q_direct = gather_z_direct(q_half)
        tok_send, _ = sync(tok_send, q_half)
        small, _ = sync(small, tok_send)
    small_all = lax.all_to_all(
        jnp.broadcast_to(small[None], (n_win,) + small.shape),
        "win",
        split_axis=0,
        concat_axis=0,
        tiled=True,
    )
    tok_got = swap_core(tok_send)
    tok_here, tok_away = windows_pack(where, tok_slots, tok_got)
    tok_back = swap_y(tok_away)

    onehot_space = space_onehot()
    space_bias = jnp.dot(table_space, onehot_space.T, precision=exact_mode)
    space_bias = jnp.tile(space_bias.reshape(heads, SPATIAL, SPATIAL), (1, 1, FRAMES))
    mine_doubled = lax.dynamic_slice_in_dim(doubled, frm * local, local, 0)
    holders = jnp.arange(4, dtype=jnp.int32)
    frames = holders[None, :] + (holders[None, :] > mine_doubled[:, None]).astype(jnp.int32)
    frames = jnp.concatenate([frames, mine_doubled[:, None] + 1], axis=1)
    offset = frames[:, :, None] - frames[:, None, :] + FRAMES - 1
    onehot_time = (
        offset[..., None] == jnp.arange(table_time.shape[1], dtype=jnp.int32)
    ).astype(f32)
    time_bias = jnp.einsum("wabt,ht->whab", onehot_time, table_time, precision=exact_mode)
    time_bias = jnp.repeat(time_bias, SPATIAL, axis=-1)
    time_bias = jnp.pad(time_bias, ((0, 0), (0, 0), (0, 8 - FRAMES), (0, 0)))

    if fast:
        *q_direct, _ = sync(*q_direct, tok_away)
        q_stack = jnp.stack(q_direct)
        q_near = gather_near(q_stack)
        small_all, up_half, _ = sync(small_all, up_half, q_stack)
        up_direct = gather_z_direct(up_half)

    cond_all = small_all[:, :windows].reshape(n_win * windows, width).astype(f32)
    bias_all = small_all[:, windows:].reshape(n_win, bias_rows * width).astype(f32)
    cuts = [b_ada.shape[0], b_ada.shape[0] + b_up.shape[0]]
    ada_bias = bias_all[:, : cuts[0]].reshape(1, 6 * width)
    up_bias = bias_all[:, cuts[0] : cuts[1]].reshape(n_win * 2, 2, ff_block)
    up_bias = pick(up_bias, c, 1).reshape(1, ff // 2)
    down_bias = bias_all[:, cuts[1] : cuts[1] + b_down.shape[0]].reshape(1, width)
    silu_all = jax.nn.silu(cond_all).astype(bf16)
    silu_part = lax.dynamic_slice_in_dim(silu_all, win * shard_rows, shard_rows, 1)
    ada_quarter = 6 * width // 4
    ada_part = lax.dynamic_slice_in_dim(w_ada, frm * ada_quarter, ada_quarter, 1)
    mod_part = dot32(silu_part, ada_part, PLAIN)
    if fast:
        *q_near, mod_part, up_bias, down_bias, space_bias, time_bias = sync(
            *q_near, mod_part, up_bias, down_bias, space_bias, time_bias
        )
        q_far = gather_far(q_near)
        *up_direct, q_near[0], q_near[1], q_near[2] = sync(*up_direct, *q_near)
        q_other = [swap_core(part) for part in q_near]
    else:
        qkv_full = lax.all_gather(w_qkv, "win", axis=0).reshape(width, 3 * width)
        out_full = lax.all_gather(w_out, "win", axis=0).reshape(width, width)
        up_shard = pick(w_up.reshape(shard_rows, n_win * 2, 2, ff_block), c, 2)
        up_full = lax.all_gather(up_shard, "win", axis=0).reshape(width, ff // 2)
        down_shard = pick(w_down.reshape(2, 2, ff_block, width), c, 1)
        down_full = lax.all_gather(down_shard, "win", axis=0).reshape(ff // 2, width)
    mod_parts = exchange_all(mod_part.reshape(devices, local, ada_quarter))
    my_window = frm * local + jnp.arange(local, dtype=jnp.int32)
    live = (my_window < window_count[0]).astype(f32)[:, None, None]
    live = jnp.broadcast_to(live, (local, 1, width))
    cot_send = windows_send(where, cot_slots)
    if fast:
        up_stack = jnp.stack(up_direct)
        q_far[0], tok_back, mod_parts, cot_send, up_stack, *q_other = sync(
            q_far[0], tok_back, mod_parts, cot_send, up_stack, *q_other
        )
        q_other = q_other + [swap_core(part) for part in q_far]
        up_near = gather_near(up_stack)
        qkv_full, out_full = place_qkv(where, list(q_near) + list(q_far) + q_other)
    cot_got = swap_core(cot_send)
    token_rows = windows_join(where, tok_here, tok_back)
    mod = modulate(mod_parts.reshape(n_win, 4, local, ada_quarter), ada_bias, live)

    projected, hidden_one = qkv_forward(token_rows, mod, qkv_full)
    cot_here, cot_away = windows_pack(where, cot_slots, cot_got)
    if fast:
        projected, cot_away, down_half, *up_near = sync(
            projected, cot_away, down_half, *up_near
        )
        up_far = gather_far(up_near)
        down_direct = gather_z_direct(down_half)
    cot_back = swap_y(cot_away)
    attended, probs = attend(projected, space_bias, time_bias, local)
    if fast:
        attended, cot_back, up_far[0], *down_direct = sync(
            attended, cot_back, up_far[0], *down_direct
        )
        down_near = gather_near(jnp.stack(down_direct))
    branch_attn, mid, hidden_two = out_forward(attended, out_full, token_rows, mod)
    grad_out = windows_join(where, cot_here, cot_back)
    grad_mlp = gated(where, grad_out, mod)
    mlp_other = swap_core(grad_mlp)

    hidden_other = swap_core(hidden_two)
    if fast:
        up_full = place_up(where, list(up_near) + list(up_far))
    rows_both = (hidden_two, hidden_other, grad_mlp, mlp_other)
    act_first, slope_first, *down_grads = up_forward(where, rows_both, up_full, up_bias, 0, fast)
    if fast:
        act_first, up_bias, *down_near = sync(act_first, up_bias, *down_near)
        down_far = gather_far(down_near, FAR_CUT)
    act_second, slope_second, *more = up_forward(where, rows_both, up_full, up_bias, 1, fast)
    if fast:
        act_second, *down_far = sync(act_second, *down_far)
        down_fy, down_fx = swap_y(down_grads[0]), swap_win(down_grads[1], 1)
        down_full = place_down(where, list(down_near) + list(down_far))
    down_grads = list(down_grads) + more
    block_rows = ff_block
    *up_grads, up_b_first, back_first = down_backward(
        where, rows_both, down_full, up_full, slope_first, 0, None, fast
    )
    if fast:
        back_first, *up_grads, down_fy, down_fx = sync(back_first, *up_grads, down_fy, down_fx)
        send_x, send_y = merge(
            [(down_grads[2], None)], [(down_grads[3], None)], down_fy, down_fx
        )
        back_first, send_x, send_y = sync(back_first, send_x, send_y)
        down_x, down_y = swap_win(send_x, 1), swap_y(send_y)
    *more, up_b_second, back_own, back_other = down_backward(
        where, rows_both, down_full, up_full, slope_second, 1, back_first, fast
    )
    up_grads = list(up_grads) + more
    if fast:
        back_other, act_first, down_x, down_y = sync(back_other, act_first, down_x, down_y)
        up_fy, up_fx = swap_y(up_grads[0]), swap_win(up_grads[1], 1)
        down_kept = total(
            [(down_grads[4], None), (down_x, None), (down_y, None)], block_rows, width
        )
    back_got = swap_core(back_other)
    mlp_own, mlp_away = down_forward(act_first, act_second, down_full)

    if fast:
        back_got, mlp_away, down_kept, *up_grads, up_fy, up_fx = sync(
            back_got, mlp_away, down_kept, *up_grads, up_fy, up_fx
        )
        down_grad = sum_z(down_kept)
        send_x, send_y = merge([(up_grads[2], None)], [(up_grads[3], None)], up_fy, up_fx)
        back_got, send_x, send_y = sync(back_got, send_x, send_y)
        up_x, up_y = swap_win(send_x, 1), swap_y(send_y)
    mlp_got = swap_core(mlp_away)
    grad_mid, grad_attended, mid_sums, grad_out_w = mid_backward(
        back_own, back_got, mid, grad_out, branch_attn, attended, out_full, mod, live
    )
    grad_attended, mlp_got = sync(grad_attended, mlp_got)
    result, res_away, gate_two_sum = result_forward(
        where, mlp_own, mlp_got, down_bias, mid, grad_out, mod, live
    )
    grad_attended, res_away = sync(grad_attended, res_away)
    res_back = swap_y(res_away.reshape(6, SPATIAL, width))
    grad_projected, space_sums, time_sums = attend_back(
        projected, grad_attended, attended, probs, local
    )
    qkv_block, out_block = 3 * width // devices, width // devices
    if fast:
        grad_projected, up_x, up_y, res_back, down_grad = sync(
            grad_projected, up_x, up_y, res_back, down_grad
        )
        own_first, own_second, other_first, other_second = qkv_grad(
            where, grad_projected, hidden_one, grad_out_w
        )
        up_x, other_first, other_second = sync(up_x, other_first, other_second)
        up_kept = total([(up_grads[4], None), (up_x, None), (up_y, None)], block_rows, width)
        up_grad = sum_z(up_kept)
        got_first, got_second = swap_core(other_first), swap_core(other_second)
    if fast:
        got_first, up_kept = sync(got_first, up_kept)
        send_fy, send_fx, attn_gx = first_quarters(own_first, got_first)
        send_fy, send_fx, grad_projected = sync(send_fy, send_fx, grad_projected)
        attn_fy, attn_fx = swap_y(send_fy), swap_win(send_fx, 1)
    else:
        grad_attn_w = jnp.concatenate(
            [
                qkv_grad_plain(grad_projected, hidden_one).reshape(n_win, 2, 2, qkv_block, width),
                grad_out_w.reshape(n_win, 2, 2, out_block, width),
            ],
            axis=3,
        )
        got = swap_core(pick(grad_attn_w, 1 - c, 2))
        attn_grad = scatter_plain(add_low(pick(grad_attn_w, c, 2), got), where)
        up_grad = scatter_plain(jnp.concatenate(up_grads).reshape(n_win, 2, ff_block, width), where)
        down_grad = scatter_plain(
            jnp.concatenate(down_grads).reshape(n_win, 2, ff_block, width), where
        )
    grad_tokens, gt_away, token_sums = tokens_backward(
        where, grad_projected, qkv_full, token_rows, grad_mid, mod
    )
    gt_away = gt_away.reshape(6, SPATIAL, width)
    if fast:
        token_sums, attn_fy, attn_fx, got_second = sync(
            token_sums, attn_fy, attn_fx, got_second
        )
        send_x, send_y = merge(
            [(attn_gx, None)], [(own_second, 0), (got_second, 0)], attn_fy, attn_fx, LAST_CUT
        )
        attn_x, attn_y = swap_win(send_x, 1), swap_y(send_y)
        token_sums, _, _ = sync(token_sums, send_x, send_y)

    grad_mod = jnp.concatenate(
        [
            token_sums[:, 0],
            token_sums[:, 1],
            mid_sums[:, 0],
            mid_sums[:, 1],
            mid_sums[:, 2],
            gate_two_sum[:, 0],
        ],
        axis=-1,
    ).astype(bf16)
    ada_block = 6 * width // devices
    to_quarter = jnp.transpose(grad_mod.reshape(local, 4, ada_quarter), (1, 0, 2))
    to_quarter = jnp.broadcast_to(to_quarter[None], (n_win, 4, local, ada_quarter))
    to_block = jnp.transpose(grad_mod.reshape(local, devices, ada_block), (1, 0, 2))
    grad_up_b = jnp.concatenate([up_b_first, up_b_second], axis=1)
    if fast:
        grad_up_b = grad_up_b.reshape(2, 2, 4, ff_block)
        grad_up_b = jnp.where(x == 0, grad_up_b[::-1], grad_up_b)
        grad_up_b = jnp.where(y == 0, grad_up_b[:, ::-1], grad_up_b)
        grad_up_b = jnp.transpose(grad_up_b, (2, 0, 1, 3))
    grad_up_b = grad_up_b.reshape(n_win * 2, 1, ff_block)
    core_mask = (jnp.arange(2, dtype=jnp.int32) == c).astype(f32)[None, :, None]
    grad_up_b = (grad_up_b * core_mask).reshape(devices, ff_block)
    grad_down_b = jnp.sum(grad_mlp.astype(f32), axis=0).reshape(devices, width // devices)
    first_send = jnp.concatenate(
        [
            to_quarter.reshape(devices, local * ada_quarter),
            to_block.reshape(devices, local * ada_block),
            grad_up_b.astype(bf16),
            grad_down_b.astype(bf16),
        ],
        axis=1,
    )
    first_got = exchange_all(first_send)
    if fast:
        attn_x, attn_y, gt_away, res_back, first_send = sync(
            attn_x, attn_y, gt_away, res_back, first_send
        )
        kept = total(
            [(own_second, 1), (got_second, 1), (attn_x, None), (attn_y, None)],
            qkv_block + out_block,
            width,
        )
        attn_grad = sum_z_direct(kept, z)
        first_got, res_back, space_sums, time_sums, _ = sync(
            first_got, res_back, space_sums, time_sums, kept
        )
    lanes = jnp.arange(FRAMES * SPATIAL, dtype=jnp.int32)
    to_place = (lanes[:, None] % SPATIAL == jnp.arange(SPATIAL)[None]).astype(f32)
    to_slot = (lanes[:, None] // SPATIAL == jnp.arange(FRAMES)[None]).astype(f32)
    space_sum = jnp.dot(
        space_sums.reshape(heads * SPATIAL, FRAMES * SPATIAL), to_place, precision=exact_mode
    )
    space_sum = jnp.dot(
        space_sum.reshape(heads, SPATIAL * SPATIAL), onehot_space, precision=exact_mode
    )
    time_sum = jnp.dot(
        time_sums.reshape(local * heads * 8, FRAMES * SPATIAL), to_slot, precision=exact_mode
    ).reshape(local, heads, 8, FRAMES)[:, :, :FRAMES]
    time_sum = jnp.einsum("whab,wabt->ht", time_sum, onehot_time, precision=exact_mode)
    tables = jnp.concatenate([space_sum.reshape(-1), time_sum.reshape(-1)])
    sizes = [local * ada_quarter, local * ada_block, ff_block, width // devices]
    ends = [sum(sizes[: n + 1]) for n in range(4)]
    mod_got = first_got[:, : ends[0]].reshape(n_win * windows, ada_quarter)
    mod_own = first_got[:, ends[0] : ends[1]].reshape(n_win * windows, ada_block)
    sums = jnp.sum(first_got[:, ends[1] :].astype(f32), axis=0)
    out_up_b = sums[:ff_block]
    out_down_b = sums[ff_block : ff_block + width // devices]
    grad_ada_w = dot32(silu_all, mod_own, LEFT_T)
    grad_ada_b = jnp.sum(mod_own.astype(f32), axis=0)
    cond_part = dot32(mod_got, ada_part, RIGHT_T)
    cond_send = cond_part.astype(bf16).reshape(n_win, 1, windows * shard_rows)
    cond_send = jnp.broadcast_to(cond_send, (n_win, 4, windows * shard_rows))
    cond_send = cond_send.reshape(devices, windows * shard_rows)
    table_send = jnp.broadcast_to(tables.astype(bf16)[None], (devices, tables.shape[0]))
    last_got = exchange_all(jnp.concatenate([cond_send, table_send], axis=1)).astype(f32)
    cond_grad = last_got[:, : windows * shard_rows].reshape(n_win, 4, windows, shard_rows)
    cond_grad = jnp.transpose(jnp.sum(cond_grad, axis=1), (1, 0, 2)).reshape(windows, width)
    _, silu_back = jax.vjp(jax.nn.silu, condition.astype(f32))
    grad_condition = silu_back(cond_grad)[0]
    table_all = jnp.sum(last_got[:, windows * shard_rows :], axis=0)
    space_size = table_space.size
    grad_space = table_all[:space_size].reshape(table_space.shape)
    grad_time = table_all[space_size : space_size + table_time.size].reshape(table_time.shape)

    res_other = swap_core(windows_back_pack(where, result, res_back))
    gt_back = swap_y(gt_away)
    gt_other = swap_core(windows_back_pack(where, grad_tokens, gt_back))
    result = windows_back_join(where, result, res_back, res_other, tokens, bf16)
    grad_tokens = windows_back_join(where, grad_tokens, gt_back, gt_other, cotangent, f32)

    return (
        result,
        grad_tokens,
        grad_condition,
        grad_ada_w,
        grad_ada_b,
        attn_grad[:qkv_block].T,
        attn_grad[qkv_block:].T,
        up_grad.T,
        out_up_b,
        down_grad,
        out_down_b,
        grad_space,
        grad_time,
    )


def solution(mesh):
    return jax.shard_map(
        on_device,
        mesh=mesh,
        in_specs=(
            P("win", "frm", None),
            P("win", None),
            P("win"),
            P("win"),
            P("win", None),
            P("win"),
            P("win", None),
            P("win", None),
            P("win", None),
            P("win"),
            P("win", None),
            P("win"),
            P(),
            P(),
            P("win", "frm", None),
        ),
        out_specs=(
            P("win", "frm", None),
            P("win", "frm", None),
            P("win", None),
            P(None, BOTH),
            P(BOTH),
            P(None, BOTH),
            P(None, BOTH),
            P(None, BOTH),
            P(BOTH),
            P(BOTH, None),
            P(BOTH),
            P(),
            P(),
        ),
        check_vma=False,
    )
```

```python
import functools

import jax
import jax.numpy as jnp
from jax import lax
from jax.experimental import pallas as pl
from jax.experimental.pallas import tpu as pltpu
from jax.sharding import PartitionSpec as P

SIDE = 8
FRAMES = 5
SPATIAL = SIDE * SIDE
BOTH = ("win", "frm")
EPS = 1e-06
VMEM_LIMIT = 50 * 1024 * 1024

f32 = jnp.float32
bf16 = jnp.bfloat16
exact_mode = lax.Precision.HIGHEST
SMALL = pl.CostEstimate(flops=1024, bytes_accessed=1024, transcendentals=0)


def swap_frm(array, bit):
    return lax.ppermute(array, "frm", [(j, j ^ bit) for j in range(4)])


def swap_core(array):
    return swap_frm(array, 1)


def swap_y(array):
    return swap_frm(array, 2)


def swap_win(array, bits):
    count = lax.axis_size("win")
    return lax.ppermute(array, "win", [(j, j ^ bits) for j in range(count)])


def exchange_all(array):
    return lax.all_to_all(array, BOTH, split_axis=0, concat_axis=0, tiled=True)


def pick(array, index, axis):
    return lax.dynamic_index_in_dim(array, index, axis, keepdims=False)


def sync(*arrays):
    return lax.optimization_barrier(arrays)


def exchange_z(blocks):
    groups = [[2 * z + x for z in range(4)] for x in range(2)]
    return lax.all_to_all(
        blocks, "win", split_axis=0, concat_axis=0, axis_index_groups=groups, tiled=True
    )


def gather_z(half):
    return exchange_z(jnp.broadcast_to(half[None], (4,) + half.shape))


def gather_z_direct(half):
    return [half] + [swap_win(half, 2 * k) for k in (1, 2, 3)]


def move_kernel(body, count, where, *refs):
    sems = refs[count]
    refs = refs[:count] + refs[count + 1 :]
    waits = []

    def copy(sources, target):
        sem = sems.at[len(waits)]
        if len(sources) == 1:
            pltpu.make_async_copy(sources[0], target, sem).start()
        else:
            condition, first, second = sources

            @pl.when(condition)
            def _():
                pltpu.make_async_copy(first, target, sem).start()

            @pl.when(jnp.logical_not(condition))
            def _():
                pltpu.make_async_copy(second, target, sem).start()

        waits.append(pltpu.make_async_copy(sources[-1], target, sem))

    def finish():
        for wait in waits:
            wait.wait()

    body(where, refs, copy, finish)


def move_call(body, name, where, inputs, outputs, copies, scratch=()):
    return pl.pallas_call(
        functools.partial(move_kernel, body, len(inputs) + len(outputs)),
        out_shape=outputs,
        in_specs=[pl.BlockSpec(memory_space=pltpu.SMEM)]
        + [pl.BlockSpec(memory_space=pltpu.HBM)] * len(inputs),
        out_specs=[pl.BlockSpec(memory_space=pltpu.VMEM)] * len(outputs),
        scratch_shapes=[pltpu.SemaphoreType.DMA((copies,))] + list(scratch),
        compiler_params=pltpu.CompilerParams(vmem_limit_bytes=VMEM_LIMIT),
        cost_estimate=SMALL,
        name=name,
    )(where, *inputs)


def low_shape(*shape):
    return jax.ShapeDtypeStruct(shape, bf16)


def halves(where, w_qkv, w_out, w_up, w_down):
    rows, width = w_out.shape
    blocks = w_up.shape[1] // 256
    block = w_down.shape[0] // 4

    def body(where, refs, copy, finish):
        qkv, out, up, down, q_half, up_half, down_half = refs
        y, c = where[2], where[3]
        quarter = rows // 4
        q_rows = pl.ds(pl.multiple_of((c * 2 + y) * quarter, quarter), quarter)
        copy([qkv.at[q_rows]], q_half.at[:, pl.ds(0, 3 * width)])
        copy([out.at[q_rows]], q_half.at[:, pl.ds(3 * width, width)])
        up_rows = pl.ds(pl.multiple_of(y * (rows // 2), rows // 2), rows // 2)
        for n in range(blocks):
            column = pl.multiple_of((2 * n + c) * 128, 128)
            copy([up.at[up_rows, pl.ds(column, 128)]], up_half.at[:, pl.ds(n * 128, 128)])
        copy([down.at[pl.ds(pl.multiple_of((y * 2 + c) * block, block), block)]], down_half)
        finish()

    return move_call(
        body,
        "halves",
        where,
        [w_qkv, w_out, w_up, w_down],
        [
            low_shape(rows // 4, 4 * width),
            low_shape(rows // 2, blocks * 128),
            low_shape(block, width),
        ],
        blocks + 3,
    )


def gather_near(along_z):
    return [along_z, swap_win(along_z, 1), swap_y(along_z)]


def gather_far(near, cut=0):
    if not cut:
        return [swap_win(near[2], 1)]
    return [swap_y(near[1][:cut]), swap_win(near[2][cut:], 1)]


PLACES = ((0, 0), (1, 0), (0, 1), (1, 1))


def piece(refs, number, k):
    if number < 3 or len(refs) == 4:
        return refs[number].at[k]
    cut = refs[3].shape[0]
    return refs[3].at[k] if k < cut else refs[4].at[k - cut]


def place_qkv(where, pieces):
    _, rows, columns = pieces[0].shape
    width = columns // 4

    def body(where, refs, copy, finish):
        z, x, y, c = where[0], where[1], where[2], where[3]
        for core in range(2):
            for n, (j, l) in enumerate(PLACES):
                for k in range(4):
                    source = piece(refs[4 * core : 4 * core + 4], n, k)
                    at = ((z ^ k) * 2 + (x ^ j), c ^ core, y ^ l)
                    copy([source.at[:, pl.ds(0, 3 * width)]], refs[8].at[at])
                    copy([source.at[:, pl.ds(3 * width, width)]], refs[9].at[at])
        finish()

    qkv, out = move_call(
        body,
        "place_qkv",
        where,
        pieces,
        [low_shape(8, 2, 2, rows, 3 * width), low_shape(8, 2, 2, rows, width)],
        64,
    )
    return qkv.reshape(32 * rows, 3 * width), out.reshape(32 * rows, width)


def place_up(where, pieces):
    _, rows, columns = pieces[0].shape

    def body(where, refs, copy, finish):
        z, x, y = where[0], where[1], where[2]
        for n, (j, l) in enumerate(PLACES):
            for k in range(4):
                copy([piece(refs[:4], n, k)], refs[4].at[(z ^ k) * 2 + (x ^ j), y ^ l])
        finish()

    return move_call(
        body, "place_up", where, pieces, [low_shape(8, 2, rows, columns)], 16
    )[0].reshape(16 * rows, columns)


def place_down(where, pieces):
    _, rows, columns = pieces[0].shape

    def body(where, refs, copy, finish):
        for n in range(4):
            for k in range(4):
                quarter = QUARTERS.index(PLACES[n])
                copy([piece(refs[:5], n, k)], refs[5].at[quarter, where[0] ^ k])
        finish()

    return move_call(
        body, "place_down", where, pieces, [low_shape(4, 4, rows, columns)], 16
    )[0].reshape(16 * rows, columns)


QUARTERS = ((1, 1), (1, 0), (0, 1), (0, 0))


FAR_CUT = 2
LAST_CUT = 1


def add_low(*terms):
    return functools.reduce(jnp.add, [term.astype(f32) for term in terms]).astype(bf16)


def block_specs(array, first, cut=0):
    if array.ndim == 4:
        return pl.BlockSpec((1, 1) + array.shape[2:], lambda i: (first, i, 0, 0))
    rows = array.shape[0] // (4 if first is None else first)
    last = array.shape[0] // rows - 1
    return pl.BlockSpec((rows, array.shape[1]), lambda i: (jnp.clip(i - cut, 0, last), 0))


def read(ref):
    return ref[...].reshape(ref.shape[-2:]).astype(f32)


def merge_kernel(counts, cut, *refs):
    x_terms, y_terms = refs[: counts[0]], refs[counts[0] : counts[0] + counts[1]]
    far_y, far_x, send_x, send_y = refs[-4:]
    first = pl.program_id(0) < cut
    to_x = functools.reduce(jnp.add, [read(ref) for ref in x_terms])
    to_y = functools.reduce(jnp.add, [read(ref) for ref in y_terms])
    send_x[...] = jnp.where(first, to_x + read(far_y), to_x).astype(bf16)
    send_y[...] = jnp.where(first, to_y, to_y + read(far_x)).astype(bf16)


def merge(x_terms, y_terms, far_y, far_x, cut=FAR_CUT):
    rows, width = far_y.shape[0] // cut, far_y.shape[1]
    block = pl.BlockSpec((rows, width), lambda i: (i, 0))
    return dense_call(
        functools.partial(merge_kernel, (len(x_terms), len(y_terms)), cut),
        "merge",
        (4,),
        [block_specs(*term) for term in list(x_terms) + list(y_terms)]
        + [block_specs(far_y, cut), block_specs(far_x, 4 - cut, cut)],
        [block, block],
        [low_shape(4 * rows, width)] * 2,
    )(*[term[0] for term in list(x_terms) + list(y_terms)], far_y, far_x)


def total_kernel(*refs):
    refs[-1][...] = functools.reduce(jnp.add, [read(ref) for ref in refs[:-1]]).astype(bf16)


def total(terms, rows, width):
    return dense_call(
        total_kernel,
        "total",
        (4,),
        [block_specs(*term) for term in terms],
        pl.BlockSpec((rows, width), lambda i: (i, 0)),
        low_shape(4 * rows, width),
    )(*[term[0] for term in terms])


def first_kernel(own_ref, got_ref, far_y, far_x, x_ref):
    far = own_ref[0].astype(f32) + got_ref[0].astype(f32)
    far_y[...] = far[:LAST_CUT].astype(bf16).reshape(far_y.shape)
    far_x[...] = far[LAST_CUT:].astype(bf16).reshape(far_x.shape)
    x_ref[...] = (own_ref[1].astype(f32) + got_ref[1].astype(f32)).astype(bf16).reshape(x_ref.shape)


def first_quarters(own, got):
    _, _, rows, width = own.shape
    shapes = [(LAST_CUT * rows, width), ((4 - LAST_CUT) * rows, width), (4 * rows, width)]
    return dense_call(
        first_kernel,
        "first_quarters",
        (1,),
        [full_spec(own.shape)] * 2,
        [full_spec(shape) for shape in shapes],
        [low_shape(*shape) for shape in shapes],
    )(own, got)


def sum_z(kept):
    blocks = kept.reshape((4, kept.shape[0] // 4) + kept.shape[1:])
    return jnp.sum(exchange_z(blocks).astype(f32), axis=0)


def sum_z_direct(kept, z):
    blocks = kept.reshape((4, kept.shape[0] // 4) + kept.shape[1:])
    sent = [swap_win(pick(blocks, z ^ k, 0), 2 * k) for k in (1, 2, 3)]
    return functools.reduce(jnp.add, [part.astype(f32) for part in [pick(blocks, z, 0)] + sent])


def scatter_plain(grad, where):
    mine = lax.psum_scatter(grad.astype(f32), "win", scatter_dimension=0, tiled=False)
    return pick(mine, where[2], 0) + swap_y(pick(mine, 1 - where[2], 0))


def windows_send(where, slots):
    def body(where, refs, copy, finish):
        for half in range(2):
            first = half * 8 + (1 - where[3]) * 4
            copy([refs[0].at[pl.ds(first, 4)]], refs[1].at[pl.ds(half * 4, 4)])
        finish()

    return move_call(body, "rows_send", where, [slots], [low_shape(8, *slots.shape[1:])], 2)[0]


def windows_pack(where, slots, got):
    def body(where, refs, copy, finish):
        own, other, here, away = refs
        y, c = where[2], where[3]
        for target, half in ((here, y), (away, 1 - y)):
            for t in range(2):
                window = half * 4 + c * 2 + t
                mine, theirs = window * 2, half * 4 + t * 2
                copy([c == 0, own.at[mine], other.at[theirs]], target.at[t * 3])
                copy([c == 0, other.at[theirs], own.at[mine]], target.at[t * 3 + 1])
                copy(
                    [where[6 + window] == where[4], own.at[mine + 1], other.at[theirs + 1]],
                    target.at[t * 3 + 2],
                )
        finish()

    shape = low_shape(6, *slots.shape[1:])
    return move_call(body, "rows_pack", where, [slots, got], [shape, shape], 12)


def windows_join(where, here, away):
    def body(where, refs, copy, finish):
        here, away, out = refs
        y = where[2]
        for t in range(2):
            for slot in range(4):
                source = t * 3 + slot % 2
                copy([y == slot // 2, here.at[source], away.at[source]], out.at[t * 5 + slot])
            near = where[6 + where[4] * 2 + t] // 2 == y
            copy([near, here.at[t * 3 + 2], away.at[t * 3 + 2]], out.at[t * 5 + 4])
        finish()

    shape = low_shape(10, *here.shape[1:])
    out = move_call(body, "rows_join", where, [here, away], [shape], 10)[0]
    return out.reshape(10 * here.shape[1], here.shape[2])


def windows_back_pack(where, rows, back):
    def body(where, refs, copy, finish):
        rows, back, out = refs
        y, c = where[2], where[3]
        for t in range(2):
            here, there = y * 4 + t * 2, (1 - y) * 4 + t * 2
            copy([rows.at[t * 5 + 2 * y + 1 - c]], out.at[here])
            copy([rows.at[t * 5 + 4]], out.at[here + 1])
            copy([back.at[t * 3 + 1 - c]], out.at[there])
            copy([back.at[t * 3 + 2]], out.at[there + 1])
        finish()

    slots = rows.reshape(10, SPATIAL, rows.shape[1])
    shape = low_shape(8, SPATIAL, rows.shape[1])
    return move_call(body, "rows_back_pack", where, [slots, back], [shape], 8)[0]


def windows_back_join(where, rows, back, got, dead, dtype):
    width = rows.shape[1]

    def body(where, refs, copy, finish):
        rows, back, got, dead, out, arrived = refs
        y, c, frm, count = where[2], where[3], where[4], where[5]
        for half in range(2):
            side = y if half == 0 else 1 - y
            for core in range(2):
                for t in range(2):
                    window = side * 4 + (c if core == 0 else 1 - c) * 2 + t
                    if core == 1:
                        even, odd = got.at[side * 4 + t * 2], got.at[side * 4 + t * 2 + 1]
                    elif half == 0:
                        even, odd = rows.at[t * 5 + 2 * y + c], rows.at[t * 5 + 4]
                    else:
                        even, odd = back.at[t * 3 + c], back.at[t * 3 + 2]
                    live = window < count
                    place = window * 2
                    copy([live, even, dead.at[place]], arrived.at[place])
                    doubled = jnp.logical_and(live, where[6 + window] == frm)
                    copy([doubled, odd, dead.at[place + 1]], arrived.at[place + 1])
        finish()
        out[...] = arrived[...].astype(out.dtype)

    slots = rows.reshape(10, SPATIAL, width)
    out = move_call(
        body,
        "rows_back_join",
        where,
        [slots, back, got, dead.reshape(16, SPATIAL, width)],
        [jax.ShapeDtypeStruct((16, SPATIAL, width), dtype)],
        16,
        [pltpu.VMEM((16, SPATIAL, width), bf16)],
    )[0]
    return out.reshape(dead.shape)


def head_lanes(head):
    lanes = lax.broadcasted_iota(jnp.int32, (1, 128), 1)
    return (lanes // 64) == head


def attend_kernel(q_ref, k_ref, v_ref, space_ref, time_ref, o_ref, p_ref):
    q, k, v = q_ref[...], k_ref[...], v_ref[...]
    rows = q.shape[0]
    total = jnp.zeros((rows, 128), f32)
    for head in range(2):
        lanes = head_lanes(head)
        scaled = jnp.where(lanes, q * jnp.asarray(0.125, bf16), jnp.zeros_like(q))
        scores = lax.dot_general(scaled, k, (((1,), (1,)), ((), ())), preferred_element_type=f32)
        shaped = scores.reshape(rows // SPATIAL, SPATIAL, rows)
        shaped = shaped + space_ref[head][None] + time_ref[0, head, : rows // SPATIAL][:, None, :]
        scores = shaped.reshape(rows, rows)
        grown = jnp.exp(scores - jnp.max(scores, axis=-1, keepdims=True))
        inverse = 1.0 / jnp.sum(grown, axis=-1, keepdims=True)
        probs = (grown * inverse).astype(bf16)
        p_ref[0, head] = probs
        masked = jnp.where(lanes, v, jnp.zeros_like(v))
        total = total + jnp.dot(probs, masked, preferred_element_type=f32)
    o_ref[...] = total.astype(bf16)


def attend_back_kernel(
    q_ref, k_ref, v_ref, do_ref, o_ref, p_ref, grad_ref, space_ref, time_ref
):
    q, k, v, do = q_ref[...], k_ref[...], v_ref[...], do_ref[...]
    rows = q.shape[0]
    slots = rows // SPATIAL
    product = do.astype(f32) * o_ref[...].astype(f32)
    grad_q = jnp.zeros((rows, 128), f32)
    grad_k = jnp.zeros((rows, 128), f32)
    grad_v = jnp.zeros((rows, 128), f32)

    @pl.when(pl.program_id(1) == 0)
    def _():
        space_ref[...] = jnp.zeros_like(space_ref)

    for head in range(2):
        lanes = head_lanes(head)
        none = jnp.zeros_like(q)
        scale = jnp.asarray(0.125, bf16)
        row_dot = jnp.sum(jnp.where(lanes, product, 0.0), axis=-1, keepdims=True)
        grads = jnp.where(lanes, do, none)
        probs = p_ref[0, head]
        grad_probs = lax.dot_general(
            grads, v, (((1,), (1,)), ((), ())), preferred_element_type=f32
        )
        grad_scores = probs.astype(f32) * (grad_probs - row_dot)
        low = grad_scores.astype(bf16)
        over_rows = (((0,), (0,)), ((), ()))
        grad_v = grad_v + lax.dot_general(probs, grads, over_rows, preferred_element_type=f32)
        grad_k = grad_k + lax.dot_general(
            low, jnp.where(lanes, q * scale, none), over_rows, preferred_element_type=f32
        )
        grad_q = grad_q + jnp.dot(
            low, jnp.where(lanes, k * scale, none), preferred_element_type=f32
        )
        shaped = grad_scores.reshape(slots, SPATIAL, rows)
        space_ref[head] += jnp.sum(shaped, axis=0)
        time_ref[0, head, :slots] = jnp.sum(shaped, axis=1)
    grad_ref[0] = grad_q.astype(bf16)
    grad_ref[1] = grad_k.astype(bf16)
    grad_ref[2] = grad_v.astype(bf16)


def attention_specs(rows, pairs):
    q_spec = pl.BlockSpec((rows, 128), lambda pair, window: (window, pair))
    k_spec = pl.BlockSpec((rows, 128), lambda pair, window: (window, pair + pairs))
    v_spec = pl.BlockSpec((rows, 128), lambda pair, window: (window, pair + 2 * pairs))
    p_spec = pl.BlockSpec((1, 2, rows, rows), lambda pair, window: (window, pair, 0, 0))
    space_spec = pl.BlockSpec((2, SPATIAL, rows), lambda pair, window: (pair, 0, 0))
    time_spec = pl.BlockSpec((1, 2, 8, rows), lambda pair, window: (window, pair, 0, 0))
    return q_spec, k_spec, v_spec, p_spec, space_spec, time_spec


def attend(projected, space_bias, time_bias, windows):
    rows = projected.shape[0] // windows
    heads = space_bias.shape[0]
    q_spec, k_spec, v_spec, p_spec, space_spec, time_spec = attention_specs(rows, heads // 2)
    width = heads * 64
    return pl.pallas_call(
        attend_kernel,
        grid=(heads // 2, windows),
        in_specs=[q_spec, k_spec, v_spec, space_spec, time_spec],
        out_specs=[q_spec, p_spec],
        out_shape=[
            pltpu.HBM((windows * rows, width), bf16),
            pltpu.HBM((windows, heads, rows, rows), bf16),
        ],
        compiler_params=pltpu.CompilerParams(vmem_limit_bytes=VMEM_LIMIT),
        cost_estimate=SMALL,
        name="attend",
    )(projected, projected, projected, space_bias, time_bias)


def attend_back(projected, grad_attended, attended, probs, windows):
    heads, rows = probs.shape[1], probs.shape[2]
    q_spec, k_spec, v_spec, p_spec, space_spec, time_spec = attention_specs(rows, heads // 2)
    width = heads * 64
    return pl.pallas_call(
        attend_back_kernel,
        grid=(heads // 2, windows),
        in_specs=[q_spec, k_spec, v_spec, q_spec, q_spec, p_spec],
        out_specs=[
            pl.BlockSpec((3, rows, 128), lambda pair, window: (0, window, pair)),
            space_spec,
            time_spec,
        ],
        out_shape=[
            pltpu.HBM((3, windows * rows, width), bf16),
            pltpu.HBM((heads, SPATIAL, rows), f32),
            pltpu.HBM((windows, heads, 8, rows), f32),
        ],
        compiler_params=pltpu.CompilerParams(vmem_limit_bytes=VMEM_LIMIT),
        cost_estimate=SMALL,
        name="attend_back",
    )(projected, projected, projected, grad_attended, attended, probs)


def full_spec(shape):
    return pl.BlockSpec(shape, lambda *_: (0,) * len(shape))


def in_hbm(shapes):
    if isinstance(shapes, list):
        return [in_hbm(shape) for shape in shapes]
    return pltpu.HBM(shapes.shape, shapes.dtype)


def dense_call(kernel, name, grid, in_specs, out_specs, out_shape, scratch=()):
    return pl.pallas_call(
        kernel,
        grid=grid,
        in_specs=in_specs,
        out_specs=out_specs,
        out_shape=in_hbm(out_shape),
        scratch_shapes=list(scratch),
        compiler_params=pltpu.CompilerParams(vmem_limit_bytes=VMEM_LIMIT),
        cost_estimate=SMALL,
        name=name,
    )


def normalize(values_in):
    centred = values_in - jnp.mean(values_in, axis=-1, keepdims=True)
    inverse = lax.rsqrt(jnp.mean(centred * centred, axis=-1, keepdims=True) + EPS)
    return centred * inverse, inverse


def normalize_back(grad_normed, normed, inverse):
    return inverse * (
        grad_normed
        - jnp.mean(grad_normed, axis=-1, keepdims=True)
        - normed * jnp.mean(grad_normed * normed, axis=-1, keepdims=True)
    )


def dot32(left, right, dims):
    return lax.dot_general(left, right, (dims, ((), ())), preferred_element_type=f32)


def modulation(mod_ref, number, window=0):
    width = mod_ref.shape[2] // 6
    return mod_ref[window, :, number * width : (number + 1) * width]


PLAIN = ((1,), (0,))
RIGHT_T = ((1,), (1,))
LEFT_T = ((0,), (0,))


def qkv_kernel(tokens_ref, mod_ref, w_ref, projected_ref, hidden_ref):
    local = mod_ref.shape[0]
    rows = tokens_ref.shape[0] // local

    @pl.when(pl.program_id(0) == 0)
    def _():
        for window in range(local):
            part = pl.ds(window * rows, rows)
            normed, _ = normalize(tokens_ref[part, :].astype(f32))
            shift, scale = modulation(mod_ref, 0, window), modulation(mod_ref, 1, window)
            hidden_ref[part, :] = (normed * (1.0 + scale) + shift).astype(bf16)

    projected_ref[...] = dot32(hidden_ref[...], w_ref[...], PLAIN).astype(bf16)


def qkv_forward(tokens, mod, w_attn):
    count, width = tokens.shape
    tile = 512
    return dense_call(
        qkv_kernel,
        "qkv",
        (3 * width // tile,),
        [
            full_spec(tokens.shape),
            full_spec(mod.shape),
            pl.BlockSpec((width, tile), lambda i: (0, i)),
        ],
        [pl.BlockSpec((count, tile), lambda i: (0, i)), full_spec(tokens.shape)],
        [jax.ShapeDtypeStruct((count, 3 * width), bf16), jax.ShapeDtypeStruct((count, width), bf16)],
    )(tokens, mod, w_attn)


def out_kernel(attended_ref, w_ref, tokens_ref, mod_ref, branch_ref, mid_ref, hidden_ref):
    branch = dot32(attended_ref[...], w_ref[...], PLAIN)
    mid = tokens_ref[...].astype(f32) + modulation(mod_ref, 2) * branch
    normed, _ = normalize(mid)
    branch_ref[...] = branch.astype(bf16)
    mid_ref[...] = mid
    hidden_ref[...] = (normed * (1.0 + modulation(mod_ref, 4)) + modulation(mod_ref, 3)).astype(bf16)


def out_forward(attended, w_attn, tokens, mod):
    count, width = tokens.shape
    local = mod.shape[0]
    rows = count // local
    row_spec = pl.BlockSpec((rows, width), lambda i: (i, 0))
    return dense_call(
        out_kernel,
        "attn_out",
        (local,),
        [
            row_spec,
            full_spec((width, width)),
            row_spec,
            pl.BlockSpec((1,) + mod.shape[1:], lambda i: (i, 0, 0)),
        ],
        [row_spec] * 3,
        [
            jax.ShapeDtypeStruct((count, width), bf16),
            jax.ShapeDtypeStruct((count, width), f32),
            jax.ShapeDtypeStruct((count, width), bf16),
        ],
    )(attended, w_attn, tokens, mod)


def gelu_parts(value):
    factor = 0.7978845608028654
    square = value * value
    half = 0.5 + 0.5 * jnp.tanh(value * (factor + (factor * 0.044715) * square))
    gelu = value * half
    slope = half + gelu * (1.0 - half) * (2.0 * factor + (6.0 * factor * 0.044715) * square)
    return gelu, slope


def joined(refs, axis):
    parts = [ref[...] for ref in refs]
    return parts[0] if len(parts) == 1 else jnp.concatenate(parts, axis=axis)


def hidden_specs(width, tile, part, fast, rows):
    if not fast:
        return [pl.BlockSpec((rows, tile), lambda i, where: (0, 2 * part + i))]

    def block(z):
        def index(i, where):
            j, l = 1 - part, 1 - i
            return 0, z * 4 + (where[1] ^ j) * 2 + (where[2] ^ l)

        return pl.BlockSpec((rows, tile // 4), index)

    return [block(z) for z in range(4)]


def held_spec(shape):
    return pl.BlockSpec(shape, lambda i, where: (0,) * len(shape))


def hidden_call(kernel, name, where, inputs, in_specs, out_specs, out_shape, scratch=()):
    return pl.pallas_call(
        kernel,
        grid_spec=pltpu.PrefetchScalarGridSpec(
            num_scalar_prefetch=1,
            grid=(2,),
            in_specs=in_specs,
            out_specs=out_specs,
            scratch_shapes=list(scratch),
        ),
        out_shape=in_hbm(out_shape),
        compiler_params=pltpu.CompilerParams(vmem_limit_bytes=VMEM_LIMIT),
        cost_estimate=SMALL,
        name=name,
    )(where, *inputs)


def write_quarters(refs, value):
    @pl.when(pl.program_id(0) == 0)
    def _():
        start = 0
        for ref in refs[:-1]:
            ref[...] = value[start : start + ref.shape[0]].astype(bf16)
            start += ref.shape[0]

    @pl.when(pl.program_id(0) == 1)
    def _():
        refs[-1][...] = value.astype(bf16)


def quarter_shapes(tile, width, part):
    cut = FAR_CUT * tile // 4
    return [(tile, width)] * 2 if part else [(cut, width), (tile - cut, width), (tile, width)]


def up_kernel(pieces, where_ref, own_ref, other_ref, mlp_ref, mlp_other_ref, *refs):
    w, bias = joined(refs[:pieces], 1), joined(refs[pieces : 2 * pieces], 1)
    act_ref, slope_ref = refs[2 * pieces : 2 * pieces + 2]
    grad_refs = refs[2 * pieces + 2 :]
    total = None
    for half, (hidden, mlp) in enumerate(((own_ref, mlp_ref), (other_ref, mlp_other_ref))):
        activated, slope = gelu_parts(dot32(hidden[...], w, PLAIN) + bias)
        activated = activated.astype(bf16)
        act_ref[half] = activated
        slope_ref[half] = slope.astype(bf16)
        part = dot32(activated, mlp[...], LEFT_T)
        total = part if total is None else total + part
    write_quarters(grad_refs, total)


def up_forward(where, rows_both, w_up, bias, part, fast):
    count, width = rows_both[0].shape
    inner = w_up.shape[1]
    tile = inner // 4
    both = pl.BlockSpec((2, count, tile), lambda i, where: (0, 0, i))
    w_specs = hidden_specs(width, tile, part, fast, width)
    bias_specs = hidden_specs(width, tile, part, fast, 1)
    pieces = len(w_specs)
    return hidden_call(
        functools.partial(up_kernel, pieces),
        "mlp_up",
        where,
        list(rows_both) + [w_up] * pieces + [bias] * pieces,
        [held_spec((count, width))] * 4 + w_specs + bias_specs,
        [both, both] + [held_spec(shape) for shape in quarter_shapes(tile, width, part)],
        [low_shape(2, count, 2 * tile)] * 2
        + [low_shape(*shape) for shape in quarter_shapes(tile, width, part)],
    )


def down_back_kernel(pieces, part, where_ref, own_ref, other_ref, mlp_ref, mlp_other_ref, down_ref, *refs):
    up = joined(refs[:pieces], 1)
    slope_ref = refs[pieces]
    refs = refs[pieces + 1 :]
    earlier_ref = refs[0] if part else None
    outs = refs[1:] if part else refs
    quarters = 2 if part else 3
    grad_refs, bias_ref = outs[:quarters], outs[quarters]
    back_refs, total_ref = outs[quarters + 1 : -1], outs[-1]
    step = pl.program_id(0)
    down = down_ref[...]
    total, sums = None, None
    for half, (hidden, mlp) in enumerate(((own_ref, mlp_ref), (other_ref, mlp_other_ref))):
        grad_pre = dot32(mlp[...], down, RIGHT_T) * slope_ref[half].astype(f32)
        column = jnp.sum(grad_pre, axis=0, keepdims=True)
        grad_pre = grad_pre.astype(bf16)
        add = dot32(grad_pre, hidden[...], LEFT_T)
        total = add if total is None else total + add
        sums = column if sums is None else sums + column
        back = dot32(grad_pre, up, RIGHT_T)

        @pl.when(step == 0)
        def _(half=half, back=back):
            total_ref[half] = back + earlier_ref[half] if part else back

        @pl.when(step > 0)
        def _(half=half, back=back):
            total_ref[half] += back

    bias_ref[...] = sums
    write_quarters(grad_refs, total)

    @pl.when(step == 1)
    def _():
        if part:
            back_refs[0][...] = total_ref[0]
            back_refs[1][...] = total_ref[1].astype(bf16)
        else:
            back_refs[0][...] = total_ref[...]


def down_backward(where, rows_both, w_down, w_up, slope, part, earlier, fast):
    count, width = rows_both[0].shape
    inner = w_up.shape[1]
    tile = inner // 4
    back_shape = (2, count, width)
    if part:
        back_specs = [held_spec((count, width))] * 2
        back_shapes = [jax.ShapeDtypeStruct((count, width), f32), low_shape(count, width)]
    else:
        back_specs = [held_spec(back_shape)]
        back_shapes = [jax.ShapeDtypeStruct(back_shape, f32)]
    w_specs = hidden_specs(width, tile, part, fast, width)
    pieces = len(w_specs)
    return hidden_call(
        functools.partial(down_back_kernel, pieces, part),
        "mlp_back",
        where,
        list(rows_both) + [w_down] + [w_up] * pieces + [slope] + ([earlier] if part else []),
        [held_spec((count, width))] * 4
        + [pl.BlockSpec((tile, width), lambda i, where: (2 * part + i, 0))]
        + w_specs
        + [pl.BlockSpec((2, count, tile), lambda i, where: (0, 0, i))]
        + ([held_spec(back_shape)] if part else []),
        [held_spec(shape) for shape in quarter_shapes(tile, width, part)]
        + [pl.BlockSpec((1, tile), lambda i, where: (0, i))]
        + back_specs,
        [low_shape(*shape) for shape in quarter_shapes(tile, width, part)]
        + [jax.ShapeDtypeStruct((1, 2 * tile), f32)]
        + back_shapes,
        [pltpu.VMEM(back_shape, f32)],
    )


def down_kernel(first_ref, second_ref, w_ref, own_ref, other_ref):
    half = first_ref.shape[2]
    for number, out_ref in enumerate((own_ref, other_ref)):
        total = dot32(first_ref[number], w_ref[:half], PLAIN)
        total = total + dot32(second_ref[number], w_ref[half:], PLAIN)
        out_ref[...] = total.astype(out_ref.dtype)


def down_forward(first, second, w_down):
    _, count, half = first.shape
    width = w_down.shape[1]
    tile = 256
    row_spec = pl.BlockSpec((count, tile), lambda i: (0, i))
    return dense_call(
        down_kernel,
        "mlp_down",
        (width // tile,),
        [full_spec(first.shape)] * 2 + [pl.BlockSpec((2 * half, tile), lambda i: (0, i))],
        [row_spec, row_spec],
        [jax.ShapeDtypeStruct((count, width), f32), low_shape(count, width)],
    )(first, second, w_down)


def split_away(where_ref, rows_ref, away_ref):
    first = pl.multiple_of((1 - where_ref[2]) * 2 * SPATIAL, 2 * SPATIAL)
    away_ref[: 2 * SPATIAL] = rows_ref[pl.ds(first, 2 * SPATIAL), :]
    away_ref[2 * SPATIAL :] = rows_ref[4 * SPATIAL :, :]


def result_kernel(
    where_ref, own_ref, other_ref, bias_ref, mid_ref, cot_ref, mod_ref, live_ref,
    result_ref, away_ref, gate_ref,
):
    branch = own_ref[...] + other_ref[...].astype(f32) + bias_ref[...]
    result_ref[...] = (mid_ref[...] + modulation(mod_ref, 5) * branch).astype(bf16)
    split_away(where_ref, result_ref, away_ref)
    gate_ref[0] = live_ref[0] * jnp.sum(branch * cot_ref[...].astype(f32), axis=0, keepdims=True)


def result_forward(where, own, other, bias, mid, cotangent, mod, live):
    count, width = own.shape
    local = mod.shape[0]
    row_spec = pl.BlockSpec((count // local, width), lambda i: (i, 0))
    one = pl.BlockSpec((1, 1, width), lambda i: (i, 0, 0))
    return dense_call(
        result_kernel,
        "result",
        (local,),
        [pl.BlockSpec(memory_space=pltpu.SMEM)]
        + [row_spec, row_spec, full_spec(bias.shape), row_spec, row_spec]
        + [pl.BlockSpec((1,) + mod.shape[1:], lambda i: (i, 0, 0)), one],
        [row_spec, pl.BlockSpec((3 * SPATIAL, width), lambda i: (i, 0)), one],
        [
            low_shape(count, width),
            low_shape(local * 3 * SPATIAL, width),
            jax.ShapeDtypeStruct((local, 1, width), f32),
        ],
    )(where, own, other, bias, mid, cotangent, mod, live)


def mid_back_kernel(
    own_ref, other_ref, mid_ref, cot_ref, branch_ref, attended_ref, w_ref, mod_ref, live_ref,
    grad_mid_ref, grad_attended_ref, sums_ref, grad_ref, total_ref,
):
    step, last = pl.program_id(0), pl.num_programs(0) - 1
    grad_hidden = own_ref[...] + other_ref[...].astype(f32)
    normed, inverse = normalize(mid_ref[...])
    back = normalize_back(grad_hidden * (1.0 + modulation(mod_ref, 4)), normed, inverse)
    grad_mid = cot_ref[...].astype(f32) + back
    grad_mid_ref[...] = grad_mid
    gate = jnp.sum(branch_ref[...].astype(f32) * grad_mid, axis=0, keepdims=True)
    sums_ref[0, 0:1] = live_ref[0] * gate
    sums_ref[0, 1:2] = jnp.sum(grad_hidden, axis=0, keepdims=True)
    sums_ref[0, 2:3] = jnp.sum(grad_hidden * normed, axis=0, keepdims=True)
    grad_branch = (modulation(mod_ref, 2) * grad_mid).astype(bf16)
    grad_attended_ref[...] = dot32(grad_branch, w_ref[...], RIGHT_T).astype(bf16)
    part = dot32(grad_branch, attended_ref[...], LEFT_T)

    @pl.when(step == 0)
    def _():
        total_ref[...] = part

    @pl.when(step > 0)
    def _():
        total_ref[...] += part

    @pl.when(step == last)
    def _():
        grad_ref[...] = total_ref[...].astype(bf16)


def mid_backward(own, other, mid, cotangent, branch, attended, w_attn, mod, live):
    count, width = own.shape
    local = mod.shape[0]
    row_spec = pl.BlockSpec((count // local, width), lambda i: (i, 0))
    return dense_call(
        mid_back_kernel,
        "mid_back",
        (local,),
        [row_spec] * 6
        + [
            full_spec((width, width)),
            pl.BlockSpec((1,) + mod.shape[1:], lambda i: (i, 0, 0)),
            pl.BlockSpec((1, 1, width), lambda i: (i, 0, 0)),
        ],
        [
            row_spec,
            row_spec,
            pl.BlockSpec((1, 8, width), lambda i: (i, 0, 0)),
            full_spec((width, width)),
        ],
        [
            jax.ShapeDtypeStruct((count, width), f32),
            jax.ShapeDtypeStruct((count, width), bf16),
            jax.ShapeDtypeStruct((local, 8, width), f32),
            jax.ShapeDtypeStruct((width, width), bf16),
        ],
        [pltpu.VMEM((width, width), f32)],
    )(own, other, mid, cotangent, branch, attended, w_attn, mod, live)


def qkv_grad_kernel(where_ref, grad_ref, hidden_ref, out_grad_ref, *refs):
    outs, whole_ref, sems = refs[:4], refs[4], refs[5]
    x, y, c = where_ref[1], where_ref[2], where_ref[3]
    step, steps = pl.program_id(0), pl.num_programs(0)
    tile, width = whole_ref.shape[1:]
    block = whole_ref.shape[0] * tile // 32
    out_block = width // 32
    whole_ref[step] = dot32(grad_ref[0], hidden_ref[...], LEFT_T).astype(bf16)

    @pl.when(step == steps - 1)
    def _():
        def target(number, rows):
            z, j, l, core = number // 8, number // 4 % 2 ^ x, number // 2 % 2 ^ y, number % 2 ^ c
            quarter = (1 - j) * 2 + 1 - l
            for output in range(4):
                condition = jnp.logical_and(core == output // 2, quarter // 2 == output % 2)
                yield condition, outs[output].at[quarter % 2, z, rows]

        count = 0
        for number in range(32):
            first, rest, to = number * block, block, 0
            pieces = [(out_grad_ref.at[pl.ds(number * out_block, out_block)], block, out_block)]
            while rest:
                size = min(rest, tile - first % tile)
                pieces.append((whole_ref.at[first // tile, pl.ds(first % tile, size)], to, size))
                first, rest, to = first + size, rest - size, to + size
            for source, start, size in pieces:
                for condition, place in target(number, pl.ds(start, size)):

                    @pl.when(condition)
                    def _(source=source, place=place, count=count):
                        pltpu.make_async_copy(source, place, sems.at[count]).start()

                count += 1
        count = 0
        for number in range(32):
            first, rest = number * block, block
            sizes = [out_block]
            while rest:
                size = min(rest, tile - first % tile)
                sizes.append(size)
                first, rest = first + size, rest - size
            for size in sizes:
                place = outs[0].at[0, 0, pl.ds(0, size)]
                pltpu.make_async_copy(place, place, sems.at[count]).wait()
                count += 1


def qkv_grad(where, grad_projected, hidden, grad_out):
    count, width = hidden.shape
    tile = 512
    per = width // tile
    rows = 4 * width // 32
    shape = low_shape(2, 4, rows, width)
    return pl.pallas_call(
        qkv_grad_kernel,
        grid=(3 * per,),
        in_specs=[
            pl.BlockSpec(memory_space=pltpu.SMEM),
            pl.BlockSpec((1, count, tile), lambda i: (i // per, 0, i % per)),
            full_spec(hidden.shape),
            full_spec(grad_out.shape),
        ],
        out_specs=[pl.BlockSpec(memory_space=pl.ANY)] * 4,
        out_shape=[shape] * 4,
        scratch_shapes=[
            pltpu.VMEM((3 * per, tile, width), bf16),
            pltpu.SemaphoreType.DMA((32 * 3,)),
        ],
        compiler_params=pltpu.CompilerParams(vmem_limit_bytes=VMEM_LIMIT),
        cost_estimate=SMALL,
        name="qkv_grad",
    )(where, grad_projected, hidden, grad_out)


def qkv_grad_plain(grad_projected, hidden):
    return lax.dot_general(
        grad_projected, hidden, (((1,), (0,)), ((), ())), preferred_element_type=f32
    ).astype(bf16)


def tokens_back_kernel(
    where_ref, grad_ref, w_ref, tokens_ref, grad_mid_ref, mod_ref, out_ref, away_ref, sums_ref
):
    width = tokens_ref.shape[1]
    grad_hidden = None
    for part in range(3):
        add = dot32(grad_ref[part], w_ref[:, part * width : (part + 1) * width], RIGHT_T)
        grad_hidden = add if grad_hidden is None else grad_hidden + add
    normed, inverse = normalize(tokens_ref[...].astype(f32))
    back = normalize_back(grad_hidden * (1.0 + modulation(mod_ref, 1)), normed, inverse)
    out_ref[...] = (grad_mid_ref[...] + back).astype(bf16)
    split_away(where_ref, out_ref, away_ref)
    sums_ref[0, 0:1] = jnp.sum(grad_hidden, axis=0, keepdims=True)
    sums_ref[0, 1:2] = jnp.sum(grad_hidden * normed, axis=0, keepdims=True)


def tokens_backward(where, grad_projected, w_qkv, tokens, grad_mid, mod):
    count, width = tokens.shape
    local = mod.shape[0]
    rows = count // local
    row_spec = pl.BlockSpec((rows, width), lambda i: (i, 0))
    return dense_call(
        tokens_back_kernel,
        "tokens_back",
        (local,),
        [
            pl.BlockSpec(memory_space=pltpu.SMEM),
            pl.BlockSpec((3, rows, width), lambda i: (0, i, 0)),
            full_spec((width, 3 * width)),
            row_spec,
            row_spec,
            pl.BlockSpec((1,) + mod.shape[1:], lambda i: (i, 0, 0)),
        ],
        [
            row_spec,
            pl.BlockSpec((3 * SPATIAL, width), lambda i: (i, 0)),
            pl.BlockSpec((1, 8, width), lambda i: (i, 0, 0)),
        ],
        [
            low_shape(count, width),
            low_shape(local * 3 * SPATIAL, width),
            jax.ShapeDtypeStruct((local, 8, width), f32),
        ],
    )(where, grad_projected, w_qkv, tokens, grad_mid, mod)


def modulation_kernel(parts_ref, bias_ref, live_ref, out_ref):
    sources, holders, local, part = parts_ref.shape
    width = out_ref.shape[2] // 6
    for window in range(local):
        for holder in range(holders):
            total = parts_ref[0, holder, window : window + 1]
            for source in range(1, sources):
                total = total + parts_ref[source, holder, window : window + 1]
            columns = slice(holder * part, (holder + 1) * part)
            out_ref[window, :, columns] = total + bias_ref[:, columns]
        for gate in (2, 5):
            columns = slice(gate * width, (gate + 1) * width)
            out_ref[window, :, columns] = out_ref[window, :, columns] * live_ref[window]


def modulate(parts, bias, live):
    local, _, width = live.shape
    return dense_call(
        modulation_kernel,
        "modulation",
        (1,),
        [full_spec(parts.shape), full_spec(bias.shape), full_spec(live.shape)],
        full_spec((local, 1, 6 * width)),
        jax.ShapeDtypeStruct((local, 1, 6 * width), f32),
    )(parts, bias, live)


def gated_kernel(where_ref, rows_ref, mod_ref, out_ref):
    out_ref[...] = (modulation(mod_ref, 5) * rows_ref[...].astype(f32)).astype(bf16)


def gated(where, rows, mod):
    count, width = rows.shape
    local = mod.shape[0]
    row_spec = pl.BlockSpec((count // local, width), lambda i: (i, 0))
    return dense_call(
        gated_kernel,
        "gated",
        (local,),
        [
            pl.BlockSpec(memory_space=pltpu.SMEM),
            row_spec,
            pl.BlockSpec((1,) + mod.shape[1:], lambda i: (i, 0, 0)),
        ],
        row_spec,
        low_shape(count, width),
    )(where, rows, mod)


def space_onehot():
    places = jnp.arange(SPATIAL, dtype=jnp.int32)
    across, along = places // SIDE, places % SIDE
    index = (across[:, None] - across[None, :] + SIDE - 1) * (2 * SIDE - 1) + (
        along[:, None] - along[None, :] + SIDE - 1
    )
    ids = jnp.arange((2 * SIDE - 1) ** 2, dtype=jnp.int32)
    return (index.reshape(-1)[:, None] == ids[None, :]).astype(f32)


def on_device(
    tokens,
    condition,
    doubled,
    window_count,
    w_ada,
    b_ada,
    w_qkv,
    w_out,
    w_up,
    b_up,
    w_down,
    b_down,
    table_space,
    table_time,
    cotangent,
):
    windows, _, width = tokens.shape
    heads = table_space.shape[0]
    n_win = lax.axis_size("win")
    devices = n_win * 4
    win = lax.axis_index("win")
    frm = lax.axis_index("frm")
    z, x, y, c = win // 2, win % 2, frm // 2, frm % 2
    where = jnp.concatenate([jnp.stack([z, x, y, c, frm, window_count[0]]), doubled])
    where = where.astype(jnp.int32)
    local = windows // 4
    count = local * FRAMES * SPATIAL
    ff = w_up.shape[1]
    ff_block = ff // devices
    shard_rows = w_qkv.shape[0]
    half_width = width // 2
    fast = n_win == 8
    slot_shape = (2 * windows, SPATIAL, width)

    tok_slots, cot_slots = tokens.reshape(slot_shape), cotangent.reshape(slot_shape)
    tok_send = windows_send(where, tok_slots)
    biases = jnp.concatenate([b_ada, b_up, b_down])
    bias_rows = -(-biases.shape[0] // width)
    biases = jnp.pad(biases, (0, bias_rows * width - biases.shape[0])).reshape(bias_rows, width)
    small = jnp.concatenate([condition, biases])
    if fast:
        q_half, up_half, down_half = halves(where, w_qkv, w_out, w_up, w_down)
        q_direct = gather_z_direct(q_half)
        tok_send, _ = sync(tok_send, q_half)
        small, _ = sync(small, tok_send)
    small_all = lax.all_to_all(
        jnp.broadcast_to(small[None], (n_win,) + small.shape),
        "win",
        split_axis=0,
        concat_axis=0,
        tiled=True,
    )
    tok_got = swap_core(tok_send)
    tok_here, tok_away = windows_pack(where, tok_slots, tok_got)
    tok_back = swap_y(tok_away)

    onehot_space = space_onehot()
    space_bias = jnp.dot(table_space, onehot_space.T, precision=exact_mode)
    space_bias = jnp.tile(space_bias.reshape(heads, SPATIAL, SPATIAL), (1, 1, FRAMES))
    mine_doubled = lax.dynamic_slice_in_dim(doubled, frm * local, local, 0)
    holders = jnp.arange(4, dtype=jnp.int32)
    frames = holders[None, :] + (holders[None, :] > mine_doubled[:, None]).astype(jnp.int32)
    frames = jnp.concatenate([frames, mine_doubled[:, None] + 1], axis=1)
    offset = frames[:, :, None] - frames[:, None, :] + FRAMES - 1
    onehot_time = (
        offset[..., None] == jnp.arange(table_time.shape[1], dtype=jnp.int32)
    ).astype(f32)
    time_bias = jnp.einsum("wabt,ht->whab", onehot_time, table_time, precision=exact_mode)
    time_bias = jnp.repeat(time_bias, SPATIAL, axis=-1)
    time_bias = jnp.pad(time_bias, ((0, 0), (0, 0), (0, 8 - FRAMES), (0, 0)))

    if fast:
        *q_direct, _ = sync(*q_direct, tok_away)
        q_stack = jnp.stack(q_direct)
        q_near = gather_near(q_stack)
        small_all, up_half, _ = sync(small_all, up_half, q_stack)
        up_direct = gather_z_direct(up_half)

    cond_all = small_all[:, :windows].reshape(n_win * windows, width).astype(f32)
    bias_all = small_all[:, windows:].reshape(n_win, bias_rows * width).astype(f32)
    cuts = [b_ada.shape[0], b_ada.shape[0] + b_up.shape[0]]
    ada_bias = bias_all[:, : cuts[0]].reshape(1, 6 * width)
    up_bias = bias_all[:, cuts[0] : cuts[1]].reshape(n_win * 2, 2, ff_block)
    up_bias = pick(up_bias, c, 1).reshape(1, ff // 2)
    down_bias = bias_all[:, cuts[1] : cuts[1] + b_down.shape[0]].reshape(1, width)
    silu_all = jax.nn.silu(cond_all).astype(bf16)
    silu_part = lax.dynamic_slice_in_dim(silu_all, win * shard_rows, shard_rows, 1)
    ada_quarter = 6 * width // 4
    ada_part = lax.dynamic_slice_in_dim(w_ada, frm * ada_quarter, ada_quarter, 1)
    mod_part = dot32(silu_part, ada_part, PLAIN)
    if fast:
        *q_near, mod_part, up_bias, down_bias, space_bias, time_bias = sync(
            *q_near, mod_part, up_bias, down_bias, space_bias, time_bias
        )
        q_far = gather_far(q_near)
        *up_direct, q_near[0], q_near[1], q_near[2] = sync(*up_direct, *q_near)
        q_other = [swap_core(part) for part in q_near]
    else:
        qkv_full = lax.all_gather(w_qkv, "win", axis=0).reshape(width, 3 * width)
        out_full = lax.all_gather(w_out, "win", axis=0).reshape(width, width)
        up_shard = pick(w_up.reshape(shard_rows, n_win * 2, 2, ff_block), c, 2)
        up_full = lax.all_gather(up_shard, "win", axis=0).reshape(width, ff // 2)
        down_shard = pick(w_down.reshape(2, 2, ff_block, width), c, 1)
        down_full = lax.all_gather(down_shard, "win", axis=0).reshape(ff // 2, width)
    mod_parts = exchange_all(mod_part.reshape(devices, local, ada_quarter))
    my_window = frm * local + jnp.arange(local, dtype=jnp.int32)
    live = (my_window < window_count[0]).astype(f32)[:, None, None]
    live = jnp.broadcast_to(live, (local, 1, width))
    cot_send = windows_send(where, cot_slots)
    if fast:
        up_stack = jnp.stack(up_direct)
        q_far[0], tok_back, mod_parts, cot_send, up_stack, *q_other = sync(
            q_far[0], tok_back, mod_parts, cot_send, up_stack, *q_other
        )
        q_other = q_other + [swap_core(part) for part in q_far]
        up_near = gather_near(up_stack)
        qkv_full, out_full = place_qkv(where, list(q_near) + list(q_far) + q_other)
    cot_got = swap_core(cot_send)
    token_rows = windows_join(where, tok_here, tok_back)
    mod = modulate(mod_parts.reshape(n_win, 4, local, ada_quarter), ada_bias, live)

    projected, hidden_one = qkv_forward(token_rows, mod, qkv_full)
    cot_here, cot_away = windows_pack(where, cot_slots, cot_got)
    if fast:
        projected, cot_away, down_half, *up_near = sync(
            projected, cot_away, down_half, *up_near
        )
        up_far = gather_far(up_near)
        down_direct = gather_z_direct(down_half)
    cot_back = swap_y(cot_away)
    attended, probs = attend(projected, space_bias, time_bias, local)
    if fast:
        attended, cot_back, up_far[0], *down_direct = sync(
            attended, cot_back, up_far[0], *down_direct
        )
        down_near = gather_near(jnp.stack(down_direct))
    branch_attn, mid, hidden_two = out_forward(attended, out_full, token_rows, mod)
    grad_out = windows_join(where, cot_here, cot_back)
    grad_mlp = gated(where, grad_out, mod)
    mlp_other = swap_core(grad_mlp)

    hidden_other = swap_core(hidden_two)
    if fast:
        up_full = place_up(where, list(up_near) + list(up_far))
    rows_both = (hidden_two, hidden_other, grad_mlp, mlp_other)
    act_first, slope_first, *down_grads = up_forward(where, rows_both, up_full, up_bias, 0, fast)
    if fast:
        act_first, up_bias, *down_near = sync(act_first, up_bias, *down_near)
        down_far = gather_far(down_near, FAR_CUT)
    act_second, slope_second, *more = up_forward(where, rows_both, up_full, up_bias, 1, fast)
    if fast:
        act_second, *down_far = sync(act_second, *down_far)
        down_fy, down_fx = swap_y(down_grads[0]), swap_win(down_grads[1], 1)
        down_full = place_down(where, list(down_near) + list(down_far))
    down_grads = list(down_grads) + more
    block_rows = ff_block
    *up_grads, up_b_first, back_first = down_backward(
        where, rows_both, down_full, up_full, slope_first, 0, None, fast
    )
    if fast:
        back_first, *up_grads, down_fy, down_fx = sync(back_first, *up_grads, down_fy, down_fx)
        send_x, send_y = merge(
            [(down_grads[2], None)], [(down_grads[3], None)], down_fy, down_fx
        )
        back_first, send_x, send_y = sync(back_first, send_x, send_y)
        down_x, down_y = swap_win(send_x, 1), swap_y(send_y)
    *more, up_b_second, back_own, back_other = down_backward(
        where, rows_both, down_full, up_full, slope_second, 1, back_first, fast
    )
    up_grads = list(up_grads) + more
    if fast:
        back_other, act_first, down_x, down_y = sync(back_other, act_first, down_x, down_y)
        up_fy, up_fx = swap_y(up_grads[0]), swap_win(up_grads[1], 1)
        down_kept = total(
            [(down_grads[4], None), (down_x, None), (down_y, None)], block_rows, width
        )
    back_got = swap_core(back_other)
    mlp_own, mlp_away = down_forward(act_first, act_second, down_full)

    if fast:
        back_got, mlp_away, down_kept, *up_grads, up_fy, up_fx = sync(
            back_got, mlp_away, down_kept, *up_grads, up_fy, up_fx
        )
        down_grad = sum_z(down_kept)
        send_x, send_y = merge([(up_grads[2], None)], [(up_grads[3], None)], up_fy, up_fx)
        back_got, send_x, send_y = sync(back_got, send_x, send_y)
        up_x, up_y = swap_win(send_x, 1), swap_y(send_y)
    mlp_got = swap_core(mlp_away)
    grad_mid, grad_attended, mid_sums, grad_out_w = mid_backward(
        back_own, back_got, mid, grad_out, branch_attn, attended, out_full, mod, live
    )
    grad_attended, mlp_got = sync(grad_attended, mlp_got)
    result, res_away, gate_two_sum = result_forward(
        where, mlp_own, mlp_got, down_bias, mid, grad_out, mod, live
    )
    grad_attended, res_away = sync(grad_attended, res_away)
    res_back = swap_y(res_away.reshape(6, SPATIAL, width))
    grad_projected, space_sums, time_sums = attend_back(
        projected, grad_attended, attended, probs, local
    )
    qkv_block, out_block = 3 * width // devices, width // devices
    if fast:
        grad_projected, up_x, up_y, res_back, down_grad = sync(
            grad_projected, up_x, up_y, res_back, down_grad
        )
        own_first, own_second, other_first, other_second = qkv_grad(
            where, grad_projected, hidden_one, grad_out_w
        )
        up_x, other_first, other_second = sync(up_x, other_first, other_second)
        up_kept = total([(up_grads[4], None), (up_x, None), (up_y, None)], block_rows, width)
        up_grad = sum_z(up_kept)
        got_first, got_second = swap_core(other_first), swap_core(other_second)
    if fast:
        got_first, up_kept = sync(got_first, up_kept)
        send_fy, send_fx, attn_gx = first_quarters(own_first, got_first)
        send_fy, send_fx, grad_projected = sync(send_fy, send_fx, grad_projected)
        attn_fy, attn_fx = swap_y(send_fy), swap_win(send_fx, 1)
    else:
        grad_attn_w = jnp.concatenate(
            [
                qkv_grad_plain(grad_projected, hidden_one).reshape(n_win, 2, 2, qkv_block, width),
                grad_out_w.reshape(n_win, 2, 2, out_block, width),
            ],
            axis=3,
        )
        got = swap_core(pick(grad_attn_w, 1 - c, 2))
        attn_grad = scatter_plain(add_low(pick(grad_attn_w, c, 2), got), where)
        up_grad = scatter_plain(jnp.concatenate(up_grads).reshape(n_win, 2, ff_block, width), where)
        down_grad = scatter_plain(
            jnp.concatenate(down_grads).reshape(n_win, 2, ff_block, width), where
        )
    grad_tokens, gt_away, token_sums = tokens_backward(
        where, grad_projected, qkv_full, token_rows, grad_mid, mod
    )
    gt_away = gt_away.reshape(6, SPATIAL, width)
    if fast:
        token_sums, attn_fy, attn_fx, got_second = sync(
            token_sums, attn_fy, attn_fx, got_second
        )
        send_x, send_y = merge(
            [(attn_gx, None)], [(own_second, 0), (got_second, 0)], attn_fy, attn_fx, LAST_CUT
        )
        attn_x, attn_y = swap_win(send_x, 1), swap_y(send_y)
        token_sums, _, _ = sync(token_sums, send_x, send_y)

    grad_mod = jnp.concatenate(
        [
            token_sums[:, 0],
            token_sums[:, 1],
            mid_sums[:, 0],
            mid_sums[:, 1],
            mid_sums[:, 2],
            gate_two_sum[:, 0],
        ],
        axis=-1,
    ).astype(bf16)
    ada_block = 6 * width // devices
    to_quarter = jnp.transpose(grad_mod.reshape(local, 4, ada_quarter), (1, 0, 2))
    to_quarter = jnp.broadcast_to(to_quarter[None], (n_win, 4, local, ada_quarter))
    to_block = jnp.transpose(grad_mod.reshape(local, devices, ada_block), (1, 0, 2))
    grad_up_b = jnp.concatenate([up_b_first, up_b_second], axis=1)
    if fast:
        grad_up_b = grad_up_b.reshape(2, 2, 4, ff_block)
        grad_up_b = jnp.where(x == 0, grad_up_b[::-1], grad_up_b)
        grad_up_b = jnp.where(y == 0, grad_up_b[:, ::-1], grad_up_b)
        grad_up_b = jnp.transpose(grad_up_b, (2, 0, 1, 3))
    grad_up_b = grad_up_b.reshape(n_win * 2, 1, ff_block)
    core_mask = (jnp.arange(2, dtype=jnp.int32) == c).astype(f32)[None, :, None]
    grad_up_b = (grad_up_b * core_mask).reshape(devices, ff_block)
    grad_down_b = jnp.sum(grad_mlp.astype(f32), axis=0).reshape(devices, width // devices)
    first_send = jnp.concatenate(
        [
            to_quarter.reshape(devices, local * ada_quarter),
            to_block.reshape(devices, local * ada_block),
            grad_up_b.astype(bf16),
            grad_down_b.astype(bf16),
        ],
        axis=1,
    )
    first_got = exchange_all(first_send)
    if fast:
        attn_x, attn_y, gt_away, res_back, first_send = sync(
            attn_x, attn_y, gt_away, res_back, first_send
        )
        kept = total(
            [(own_second, 1), (got_second, 1), (attn_x, None), (attn_y, None)],
            qkv_block + out_block,
            width,
        )
        attn_grad = sum_z_direct(kept, z)
        first_got, res_back, space_sums, time_sums, _ = sync(
            first_got, res_back, space_sums, time_sums, kept
        )
    lanes = jnp.arange(FRAMES * SPATIAL, dtype=jnp.int32)
    to_place = (lanes[:, None] % SPATIAL == jnp.arange(SPATIAL)[None]).astype(f32)
    to_slot = (lanes[:, None] // SPATIAL == jnp.arange(FRAMES)[None]).astype(f32)
    space_sum = jnp.dot(
        space_sums.reshape(heads * SPATIAL, FRAMES * SPATIAL), to_place, precision=exact_mode
    )
    space_sum = jnp.dot(
        space_sum.reshape(heads, SPATIAL * SPATIAL), onehot_space, precision=exact_mode
    )
    time_sum = jnp.dot(
        time_sums.reshape(local * heads * 8, FRAMES * SPATIAL), to_slot, precision=exact_mode
    ).reshape(local, heads, 8, FRAMES)[:, :, :FRAMES]
    time_sum = jnp.einsum("whab,wabt->ht", time_sum, onehot_time, precision=exact_mode)
    tables = jnp.concatenate([space_sum.reshape(-1), time_sum.reshape(-1)])
    sizes = [local * ada_quarter, local * ada_block, ff_block, width // devices]
    ends = [sum(sizes[: n + 1]) for n in range(4)]
    mod_got = first_got[:, : ends[0]].reshape(n_win * windows, ada_quarter)
    mod_own = first_got[:, ends[0] : ends[1]].reshape(n_win * windows, ada_block)
    sums = jnp.sum(first_got[:, ends[1] :].astype(f32), axis=0)
    out_up_b = sums[:ff_block]
    out_down_b = sums[ff_block : ff_block + width // devices]
    grad_ada_w = dot32(silu_all, mod_own, LEFT_T)
    grad_ada_b = jnp.sum(mod_own.astype(f32), axis=0)
    cond_part = dot32(mod_got, ada_part, RIGHT_T)
    cond_send = cond_part.astype(bf16).reshape(n_win, 1, windows * shard_rows)
    cond_send = jnp.broadcast_to(cond_send, (n_win, 4, windows * shard_rows))
    cond_send = cond_send.reshape(devices, windows * shard_rows)
    table_send = jnp.broadcast_to(tables.astype(bf16)[None], (devices, tables.shape[0]))
    last_got = exchange_all(jnp.concatenate([cond_send, table_send], axis=1)).astype(f32)
    cond_grad = last_got[:, : windows * shard_rows].reshape(n_win, 4, windows, shard_rows)
    cond_grad = jnp.transpose(jnp.sum(cond_grad, axis=1), (1, 0, 2)).reshape(windows, width)
    _, silu_back = jax.vjp(jax.nn.silu, condition.astype(f32))
    grad_condition = silu_back(cond_grad)[0]
    table_all = jnp.sum(last_got[:, windows * shard_rows :], axis=0)
    space_size = table_space.size
    grad_space = table_all[:space_size].reshape(table_space.shape)
    grad_time = table_all[space_size : space_size + table_time.size].reshape(table_time.shape)

    res_other = swap_core(windows_back_pack(where, result, res_back))
    gt_back = swap_y(gt_away)
    gt_other = swap_core(windows_back_pack(where, grad_tokens, gt_back))
    result = windows_back_join(where, result, res_back, res_other, tokens, bf16)
    grad_tokens = windows_back_join(where, grad_tokens, gt_back, gt_other, cotangent, f32)

    return (
        result,
        grad_tokens,
        grad_condition,
        grad_ada_w,
        grad_ada_b,
        attn_grad[:qkv_block].T,
        attn_grad[qkv_block:].T,
        up_grad.T,
        out_up_b,
        down_grad,
        out_down_b,
        grad_space,
        grad_time,
    )


def solution(mesh):
    return jax.shard_map(
        on_device,
        mesh=mesh,
        in_specs=(
            P("win", "frm", None),
            P("win", None),
            P("win"),
            P("win"),
            P("win", None),
            P("win"),
            P("win", None),
            P("win", None),
            P("win", None),
            P("win"),
            P("win", None),
            P("win"),
            P(),
            P(),
            P("win", "frm", None),
        ),
        out_specs=(
            P("win", "frm", None),
            P("win", "frm", None),
            P("win", None),
            P(None, BOTH),
            P(BOTH),
            P(None, BOTH),
            P(None, BOTH),
            P(None, BOTH),
            P(BOTH),
            P(BOTH, None),
            P(BOTH),
            P(),
            P(),
        ),
        check_vma=False,
    )
```

```python
import functools

import jax
import jax.numpy as jnp
from jax import lax
from jax.experimental import pallas as pl
from jax.experimental.pallas import tpu as pltpu
from jax.sharding import PartitionSpec as P

SIDE = 8
FRAMES = 5
SPATIAL = SIDE * SIDE
BOTH = ("win", "frm")
EPS = 1e-06
VMEM_LIMIT = 50 * 1024 * 1024

f32 = jnp.float32
bf16 = jnp.bfloat16
exact_mode = lax.Precision.HIGHEST
SMALL = pl.CostEstimate(flops=1024, bytes_accessed=1024, transcendentals=0)


def swap_frm(array, bit):
    return lax.ppermute(array, "frm", [(j, j ^ bit) for j in range(4)])


def swap_core(array):
    return swap_frm(array, 1)


def swap_y(array):
    return swap_frm(array, 2)


def swap_win(array, bits):
    count = lax.axis_size("win")
    return lax.ppermute(array, "win", [(j, j ^ bits) for j in range(count)])


def exchange_all(array):
    return lax.all_to_all(array, BOTH, split_axis=0, concat_axis=0, tiled=True)


def pick(array, index, axis):
    return lax.dynamic_index_in_dim(array, index, axis, keepdims=False)


def sync(*arrays):
    return lax.optimization_barrier(arrays)


def exchange_z(blocks):
    groups = [[2 * z + x for z in range(4)] for x in range(2)]
    return lax.all_to_all(
        blocks, "win", split_axis=0, concat_axis=0, axis_index_groups=groups, tiled=True
    )


def gather_z(half):
    return exchange_z(jnp.broadcast_to(half[None], (4,) + half.shape))


def gather_z_direct(half):
    return [half] + [swap_win(half, 2 * k) for k in (1, 2, 3)]


def move_kernel(body, count, where, *refs):
    sems = refs[count]
    refs = refs[:count] + refs[count + 1 :]
    waits = []

    def copy(sources, target):
        sem = sems.at[len(waits)]
        if len(sources) == 1:
            pltpu.make_async_copy(sources[0], target, sem).start()
        else:
            condition, first, second = sources

            @pl.when(condition)
            def _():
                pltpu.make_async_copy(first, target, sem).start()

            @pl.when(jnp.logical_not(condition))
            def _():
                pltpu.make_async_copy(second, target, sem).start()

        waits.append(pltpu.make_async_copy(sources[-1], target, sem))

    def finish():
        for wait in waits:
            wait.wait()

    body(where, refs, copy, finish)


def move_call(body, name, where, inputs, outputs, copies, scratch=()):
    return pl.pallas_call(
        functools.partial(move_kernel, body, len(inputs) + len(outputs)),
        out_shape=outputs,
        in_specs=[pl.BlockSpec(memory_space=pltpu.SMEM)]
        + [pl.BlockSpec(memory_space=pltpu.HBM)] * len(inputs),
        out_specs=[pl.BlockSpec(memory_space=pltpu.VMEM)] * len(outputs),
        scratch_shapes=[pltpu.SemaphoreType.DMA((copies,))] + list(scratch),
        compiler_params=pltpu.CompilerParams(vmem_limit_bytes=VMEM_LIMIT),
        cost_estimate=SMALL,
        name=name,
    )(where, *inputs)


def low_shape(*shape):
    return jax.ShapeDtypeStruct(shape, bf16)


def halves(where, w_qkv, w_out, w_up, w_down):
    rows, width = w_out.shape
    blocks = w_up.shape[1] // 256
    block = w_down.shape[0] // 4

    def body(where, refs, copy, finish):
        qkv, out, up, down, q_half, up_half, down_half = refs
        y, c = where[2], where[3]
        quarter = rows // 4
        q_rows = pl.ds(pl.multiple_of((c * 2 + y) * quarter, quarter), quarter)
        copy([qkv.at[q_rows]], q_half.at[:, pl.ds(0, 3 * width)])
        copy([out.at[q_rows]], q_half.at[:, pl.ds(3 * width, width)])
        up_rows = pl.ds(pl.multiple_of(y * (rows // 2), rows // 2), rows // 2)
        for n in range(blocks):
            column = pl.multiple_of((2 * n + c) * 128, 128)
            copy([up.at[up_rows, pl.ds(column, 128)]], up_half.at[:, pl.ds(n * 128, 128)])
        copy([down.at[pl.ds(pl.multiple_of((y * 2 + c) * block, block), block)]], down_half)
        finish()

    return move_call(
        body,
        "halves",
        where,
        [w_qkv, w_out, w_up, w_down],
        [
            low_shape(rows // 4, 4 * width),
            low_shape(rows // 2, blocks * 128),
            low_shape(block, width),
        ],
        blocks + 3,
    )


def gather_near(along_z):
    return [along_z, swap_win(along_z, 1), swap_y(along_z)]


def gather_far(near, cut=0):
    if not cut:
        return [swap_win(near[2], 1)]
    return [swap_y(near[1][:cut]), swap_win(near[2][cut:], 1)]


PLACES = ((0, 0), (1, 0), (0, 1), (1, 1))


def piece(refs, number, k):
    if number < 3 or len(refs) == 4:
        return refs[number].at[k]
    cut = refs[3].shape[0]
    return refs[3].at[k] if k < cut else refs[4].at[k - cut]


def place_qkv(where, pieces):
    _, rows, columns = pieces[0].shape
    width = columns // 4

    def body(where, refs, copy, finish):
        z, x, y, c = where[0], where[1], where[2], where[3]
        for core in range(2):
            for n, (j, l) in enumerate(PLACES):
                for k in range(4):
                    source = piece(refs[4 * core : 4 * core + 4], n, k)
                    at = ((z ^ k) * 2 + (x ^ j), c ^ core, y ^ l)
                    copy([source.at[:, pl.ds(0, 3 * width)]], refs[8].at[at])
                    copy([source.at[:, pl.ds(3 * width, width)]], refs[9].at[at])
        finish()

    qkv, out = move_call(
        body,
        "place_qkv",
        where,
        pieces,
        [low_shape(8, 2, 2, rows, 3 * width), low_shape(8, 2, 2, rows, width)],
        64,
    )
    return qkv.reshape(32 * rows, 3 * width), out.reshape(32 * rows, width)


def place_up(where, pieces):
    _, rows, columns = pieces[0].shape

    def body(where, refs, copy, finish):
        z, x, y = where[0], where[1], where[2]
        for n, (j, l) in enumerate(PLACES):
            for k in range(4):
                copy([piece(refs[:4], n, k)], refs[4].at[(z ^ k) * 2 + (x ^ j), y ^ l])
        finish()

    return move_call(
        body, "place_up", where, pieces, [low_shape(8, 2, rows, columns)], 16
    )[0].reshape(16 * rows, columns)


def place_down(where, pieces):
    _, rows, columns = pieces[0].shape

    def body(where, refs, copy, finish):
        for n in range(4):
            for k in range(4):
                quarter = QUARTERS.index(PLACES[n])
                copy([piece(refs[:5], n, k)], refs[5].at[quarter, where[0] ^ k])
        finish()

    return move_call(
        body, "place_down", where, pieces, [low_shape(4, 4, rows, columns)], 16
    )[0].reshape(16 * rows, columns)


QUARTERS = ((1, 1), (1, 0), (0, 1), (0, 0))


FAR_CUT = 2
LAST_CUT = 1


def add_low(*terms):
    return functools.reduce(jnp.add, [term.astype(f32) for term in terms]).astype(bf16)


def block_specs(array, first, cut=0):
    if array.ndim == 4:
        return pl.BlockSpec((1, 1) + array.shape[2:], lambda i: (first, i, 0, 0))
    rows = array.shape[0] // (4 if first is None else first)
    last = array.shape[0] // rows - 1
    return pl.BlockSpec((rows, array.shape[1]), lambda i: (jnp.clip(i - cut, 0, last), 0))


def read(ref):
    return ref[...].reshape(ref.shape[-2:]).astype(f32)


def merge_kernel(counts, cut, *refs):
    x_terms, y_terms = refs[: counts[0]], refs[counts[0] : counts[0] + counts[1]]
    far_y, far_x, send_x, send_y = refs[-4:]
    first = pl.program_id(0) < cut
    to_x = functools.reduce(jnp.add, [read(ref) for ref in x_terms])
    to_y = functools.reduce(jnp.add, [read(ref) for ref in y_terms])
    send_x[...] = jnp.where(first, to_x + read(far_y), to_x).astype(bf16)
    send_y[...] = jnp.where(first, to_y, to_y + read(far_x)).astype(bf16)


def merge(x_terms, y_terms, far_y, far_x, cut=FAR_CUT):
    rows, width = far_y.shape[0] // cut, far_y.shape[1]
    block = pl.BlockSpec((rows, width), lambda i: (i, 0))
    return dense_call(
        functools.partial(merge_kernel, (len(x_terms), len(y_terms)), cut),
        "merge",
        (4,),
        [block_specs(*term) for term in list(x_terms) + list(y_terms)]
        + [block_specs(far_y, cut), block_specs(far_x, 4 - cut, cut)],
        [block, block],
        [low_shape(4 * rows, width)] * 2,
    )(*[term[0] for term in list(x_terms) + list(y_terms)], far_y, far_x)


def total_kernel(*refs):
    refs[-1][...] = functools.reduce(jnp.add, [read(ref) for ref in refs[:-1]]).astype(bf16)


def total(terms, rows, width):
    return dense_call(
        total_kernel,
        "total",
        (4,),
        [block_specs(*term) for term in terms],
        pl.BlockSpec((rows, width), lambda i: (i, 0)),
        low_shape(4 * rows, width),
    )(*[term[0] for term in terms])


def first_kernel(own_ref, got_ref, far_y, far_x, x_ref):
    far = own_ref[0].astype(f32) + got_ref[0].astype(f32)
    far_y[...] = far[:LAST_CUT].astype(bf16).reshape(far_y.shape)
    far_x[...] = far[LAST_CUT:].astype(bf16).reshape(far_x.shape)
    x_ref[...] = (own_ref[1].astype(f32) + got_ref[1].astype(f32)).astype(bf16).reshape(x_ref.shape)


def first_quarters(own, got):
    _, _, rows, width = own.shape
    shapes = [(LAST_CUT * rows, width), ((4 - LAST_CUT) * rows, width), (4 * rows, width)]
    return dense_call(
        first_kernel,
        "first_quarters",
        (1,),
        [full_spec(own.shape)] * 2,
        [full_spec(shape) for shape in shapes],
        [low_shape(*shape) for shape in shapes],
    )(own, got)


def sum_z(kept):
    blocks = kept.reshape((4, kept.shape[0] // 4) + kept.shape[1:])
    return jnp.sum(exchange_z(blocks).astype(f32), axis=0)


def sum_z_direct(kept, z):
    blocks = kept.reshape((4, kept.shape[0] // 4) + kept.shape[1:])
    sent = [swap_win(pick(blocks, z ^ k, 0), 2 * k) for k in (1, 2, 3)]
    return functools.reduce(jnp.add, [part.astype(f32) for part in [pick(blocks, z, 0)] + sent])


def scatter_plain(grad, where):
    mine = lax.psum_scatter(grad.astype(f32), "win", scatter_dimension=0, tiled=False)
    return pick(mine, where[2], 0) + swap_y(pick(mine, 1 - where[2], 0))


def windows_send(where, slots):
    def body(where, refs, copy, finish):
        for half in range(2):
            first = half * 8 + (1 - where[3]) * 4
            copy([refs[0].at[pl.ds(first, 4)]], refs[1].at[pl.ds(half * 4, 4)])
        finish()

    return move_call(body, "rows_send", where, [slots], [low_shape(8, *slots.shape[1:])], 2)[0]


def windows_pack(where, slots, got):
    def body(where, refs, copy, finish):
        own, other, here, away = refs
        y, c = where[2], where[3]
        for target, half in ((here, y), (away, 1 - y)):
            for t in range(2):
                window = half * 4 + c * 2 + t
                mine, theirs = window * 2, half * 4 + t * 2
                copy([c == 0, own.at[mine], other.at[theirs]], target.at[t * 3])
                copy([c == 0, other.at[theirs], own.at[mine]], target.at[t * 3 + 1])
                copy(
                    [where[6 + window] == where[4], own.at[mine + 1], other.at[theirs + 1]],
                    target.at[t * 3 + 2],
                )
        finish()

    shape = low_shape(6, *slots.shape[1:])
    return move_call(body, "rows_pack", where, [slots, got], [shape, shape], 12)


def windows_join(where, here, away):
    def body(where, refs, copy, finish):
        here, away, out = refs
        y = where[2]
        for t in range(2):
            for slot in range(4):
                source = t * 3 + slot % 2
                copy([y == slot // 2, here.at[source], away.at[source]], out.at[t * 5 + slot])
            near = where[6 + where[4] * 2 + t] // 2 == y
            copy([near, here.at[t * 3 + 2], away.at[t * 3 + 2]], out.at[t * 5 + 4])
        finish()

    shape = low_shape(10, *here.shape[1:])
    out = move_call(body, "rows_join", where, [here, away], [shape], 10)[0]
    return out.reshape(10 * here.shape[1], here.shape[2])


def windows_back_pack(where, rows, back):
    def body(where, refs, copy, finish):
        rows, back, out = refs
        y, c = where[2], where[3]
        for t in range(2):
            here, there = y * 4 + t * 2, (1 - y) * 4 + t * 2
            copy([rows.at[t * 5 + 2 * y + 1 - c]], out.at[here])
            copy([rows.at[t * 5 + 4]], out.at[here + 1])
            copy([back.at[t * 3 + 1 - c]], out.at[there])
            copy([back.at[t * 3 + 2]], out.at[there + 1])
        finish()

    slots = rows.reshape(10, SPATIAL, rows.shape[1])
    shape = low_shape(8, SPATIAL, rows.shape[1])
    return move_call(body, "rows_back_pack", where, [slots, back], [shape], 8)[0]


def windows_back_join(where, rows, back, got, dead, dtype):
    width = rows.shape[1]

    def body(where, refs, copy, finish):
        rows, back, got, dead, out, arrived = refs
        y, c, frm, count = where[2], where[3], where[4], where[5]
        for half in range(2):
            side = y if half == 0 else 1 - y
            for core in range(2):
                for t in range(2):
                    window = side * 4 + (c if core == 0 else 1 - c) * 2 + t
                    if core == 1:
                        even, odd = got.at[side * 4 + t * 2], got.at[side * 4 + t * 2 + 1]
                    elif half == 0:
                        even, odd = rows.at[t * 5 + 2 * y + c], rows.at[t * 5 + 4]
                    else:
                        even, odd = back.at[t * 3 + c], back.at[t * 3 + 2]
                    live = window < count
                    place = window * 2
                    copy([live, even, dead.at[place]], arrived.at[place])
                    doubled = jnp.logical_and(live, where[6 + window] == frm)
                    copy([doubled, odd, dead.at[place + 1]], arrived.at[place + 1])
        finish()
        out[...] = arrived[...].astype(out.dtype)

    slots = rows.reshape(10, SPATIAL, width)
    out = move_call(
        body,
        "rows_back_join",
        where,
        [slots, back, got, dead.reshape(16, SPATIAL, width)],
        [jax.ShapeDtypeStruct((16, SPATIAL, width), dtype)],
        16,
        [pltpu.VMEM((16, SPATIAL, width), bf16)],
    )[0]
    return out.reshape(dead.shape)


GROUP = 4
LANES = GROUP * 64


def head_lanes(head):
    lanes = lax.broadcasted_iota(jnp.int32, (1, LANES), 1)
    return (lanes // 64) == head


def attend_kernel(q_ref, k_ref, v_ref, space_ref, time_ref, o_ref, p_ref):
    q, k, v = q_ref[...], k_ref[...], v_ref[...]
    rows = q.shape[0]
    total = jnp.zeros((rows, LANES), f32)
    for head in range(GROUP):
        lanes = head_lanes(head)
        scaled = jnp.where(lanes, q * jnp.asarray(0.125, bf16), jnp.zeros_like(q))
        scores = lax.dot_general(scaled, k, (((1,), (1,)), ((), ())), preferred_element_type=f32)
        shaped = scores.reshape(rows // SPATIAL, SPATIAL, rows)
        shaped = shaped + space_ref[head][None] + time_ref[0, head, : rows // SPATIAL][:, None, :]
        scores = shaped.reshape(rows, rows)
        grown = jnp.exp(scores - jnp.max(scores, axis=-1, keepdims=True))
        inverse = 1.0 / jnp.sum(grown, axis=-1, keepdims=True)
        probs = (grown * inverse).astype(bf16)
        p_ref[0, head] = probs
        masked = jnp.where(lanes, v, jnp.zeros_like(v))
        total = total + jnp.dot(probs, masked, preferred_element_type=f32)
    o_ref[...] = total.astype(bf16)


def attend_back_kernel(
    q_ref, k_ref, v_ref, do_ref, o_ref, p_ref, grad_ref, space_ref, time_ref
):
    q, k, v, do = q_ref[...], k_ref[...], v_ref[...], do_ref[...]
    rows = q.shape[0]
    slots = rows // SPATIAL
    product = do.astype(f32) * o_ref[...].astype(f32)
    grad_q = jnp.zeros((rows, LANES), f32)
    grad_k = jnp.zeros((rows, LANES), f32)
    grad_v = jnp.zeros((rows, LANES), f32)

    @pl.when(pl.program_id(1) == 0)
    def _():
        space_ref[...] = jnp.zeros_like(space_ref)

    for head in range(GROUP):
        lanes = head_lanes(head)
        none = jnp.zeros_like(q)
        scale = jnp.asarray(0.125, bf16)
        row_dot = jnp.sum(jnp.where(lanes, product, 0.0), axis=-1, keepdims=True)
        grads = jnp.where(lanes, do, none)
        probs = p_ref[0, head]
        grad_probs = lax.dot_general(
            grads, v, (((1,), (1,)), ((), ())), preferred_element_type=f32
        )
        grad_scores = probs.astype(f32) * (grad_probs - row_dot)
        low = grad_scores.astype(bf16)
        over_rows = (((0,), (0,)), ((), ()))
        grad_v = grad_v + lax.dot_general(probs, grads, over_rows, preferred_element_type=f32)
        grad_k = grad_k + lax.dot_general(
            low, jnp.where(lanes, q * scale, none), over_rows, preferred_element_type=f32
        )
        grad_q = grad_q + jnp.dot(
            low, jnp.where(lanes, k * scale, none), preferred_element_type=f32
        )
        shaped = grad_scores.reshape(slots, SPATIAL, rows)
        space_ref[head] += jnp.sum(shaped, axis=0)
        time_ref[0, head, :slots] = jnp.sum(shaped, axis=1)
    grad_ref[0] = grad_q.astype(bf16)
    grad_ref[1] = grad_k.astype(bf16)
    grad_ref[2] = grad_v.astype(bf16)


def attention_specs(rows, groups):
    q_spec = pl.BlockSpec((rows, LANES), lambda group, window: (window, group))
    k_spec = pl.BlockSpec((rows, LANES), lambda group, window: (window, group + groups))
    v_spec = pl.BlockSpec((rows, LANES), lambda group, window: (window, group + 2 * groups))
    p_spec = pl.BlockSpec((1, GROUP, rows, rows), lambda group, window: (window, group, 0, 0))
    space_spec = pl.BlockSpec((GROUP, SPATIAL, rows), lambda group, window: (group, 0, 0))
    time_spec = pl.BlockSpec((1, GROUP, 8, rows), lambda group, window: (window, group, 0, 0))
    return q_spec, k_spec, v_spec, p_spec, space_spec, time_spec


def attend(projected, space_bias, time_bias, windows):
    rows = projected.shape[0] // windows
    heads = space_bias.shape[0]
    q_spec, k_spec, v_spec, p_spec, space_spec, time_spec = attention_specs(rows, heads // GROUP)
    width = heads * 64
    return pl.pallas_call(
        attend_kernel,
        grid=(heads // GROUP, windows),
        in_specs=[q_spec, k_spec, v_spec, space_spec, time_spec],
        out_specs=[q_spec, p_spec],
        out_shape=[
            pltpu.HBM((windows * rows, width), bf16),
            pltpu.HBM((windows, heads, rows, rows), bf16),
        ],
        compiler_params=pltpu.CompilerParams(vmem_limit_bytes=VMEM_LIMIT),
        cost_estimate=SMALL,
        name="attend",
    )(projected, projected, projected, space_bias, time_bias)


def attend_back(projected, grad_attended, attended, probs, windows):
    heads, rows = probs.shape[1], probs.shape[2]
    q_spec, k_spec, v_spec, p_spec, space_spec, time_spec = attention_specs(rows, heads // GROUP)
    width = heads * 64
    return pl.pallas_call(
        attend_back_kernel,
        grid=(heads // GROUP, windows),
        in_specs=[q_spec, k_spec, v_spec, q_spec, q_spec, p_spec],
        out_specs=[
            pl.BlockSpec((3, rows, LANES), lambda group, window: (0, window, group)),
            space_spec,
            time_spec,
        ],
        out_shape=[
            pltpu.HBM((3, windows * rows, width), bf16),
            pltpu.HBM((heads, SPATIAL, rows), f32),
            pltpu.HBM((windows, heads, 8, rows), f32),
        ],
        compiler_params=pltpu.CompilerParams(vmem_limit_bytes=VMEM_LIMIT),
        cost_estimate=SMALL,
        name="attend_back",
    )(projected, projected, projected, grad_attended, attended, probs)


def full_spec(shape):
    return pl.BlockSpec(shape, lambda *_: (0,) * len(shape))


def in_hbm(shapes):
    if isinstance(shapes, list):
        return [in_hbm(shape) for shape in shapes]
    return pltpu.HBM(shapes.shape, shapes.dtype)


def dense_call(kernel, name, grid, in_specs, out_specs, out_shape, scratch=()):
    return pl.pallas_call(
        kernel,
        grid=grid,
        in_specs=in_specs,
        out_specs=out_specs,
        out_shape=in_hbm(out_shape),
        scratch_shapes=list(scratch),
        compiler_params=pltpu.CompilerParams(vmem_limit_bytes=VMEM_LIMIT),
        cost_estimate=SMALL,
        name=name,
    )


def normalize(values_in):
    centred = values_in - jnp.mean(values_in, axis=-1, keepdims=True)
    inverse = lax.rsqrt(jnp.mean(centred * centred, axis=-1, keepdims=True) + EPS)
    return centred * inverse, inverse


def normalize_back(grad_normed, normed, inverse):
    return inverse * (
        grad_normed
        - jnp.mean(grad_normed, axis=-1, keepdims=True)
        - normed * jnp.mean(grad_normed * normed, axis=-1, keepdims=True)
    )


def dot32(left, right, dims):
    return lax.dot_general(left, right, (dims, ((), ())), preferred_element_type=f32)


def modulation(mod_ref, number, window=0):
    width = mod_ref.shape[2] // 6
    return mod_ref[window, :, number * width : (number + 1) * width]


PLAIN = ((1,), (0,))
RIGHT_T = ((1,), (1,))
LEFT_T = ((0,), (0,))


def qkv_kernel(tokens_ref, mod_ref, w_ref, projected_ref, hidden_ref):
    local = mod_ref.shape[0]
    rows = tokens_ref.shape[0] // local

    @pl.when(pl.program_id(0) == 0)
    def _():
        for window in range(local):
            part = pl.ds(window * rows, rows)
            normed, _ = normalize(tokens_ref[part, :].astype(f32))
            shift, scale = modulation(mod_ref, 0, window), modulation(mod_ref, 1, window)
            hidden_ref[part, :] = (normed * (1.0 + scale) + shift).astype(bf16)

    projected_ref[...] = dot32(hidden_ref[...], w_ref[...], PLAIN).astype(bf16)


def qkv_forward(tokens, mod, w_attn):
    count, width = tokens.shape
    tile = 512
    return dense_call(
        qkv_kernel,
        "qkv",
        (3 * width // tile,),
        [
            full_spec(tokens.shape),
            full_spec(mod.shape),
            pl.BlockSpec((width, tile), lambda i: (0, i)),
        ],
        [pl.BlockSpec((count, tile), lambda i: (0, i)), full_spec(tokens.shape)],
        [jax.ShapeDtypeStruct((count, 3 * width), bf16), jax.ShapeDtypeStruct((count, width), bf16)],
    )(tokens, mod, w_attn)


def out_kernel(attended_ref, w_ref, tokens_ref, mod_ref, branch_ref, mid_ref, hidden_ref):
    branch = dot32(attended_ref[...], w_ref[...], PLAIN)
    mid = tokens_ref[...].astype(f32) + modulation(mod_ref, 2) * branch
    normed, _ = normalize(mid)
    branch_ref[...] = branch.astype(bf16)
    mid_ref[...] = mid
    hidden_ref[...] = (normed * (1.0 + modulation(mod_ref, 4)) + modulation(mod_ref, 3)).astype(bf16)


def out_forward(attended, w_attn, tokens, mod):
    count, width = tokens.shape
    local = mod.shape[0]
    rows = count // local
    row_spec = pl.BlockSpec((rows, width), lambda i: (i, 0))
    return dense_call(
        out_kernel,
        "attn_out",
        (local,),
        [
            row_spec,
            full_spec((width, width)),
            row_spec,
            pl.BlockSpec((1,) + mod.shape[1:], lambda i: (i, 0, 0)),
        ],
        [row_spec] * 3,
        [
            jax.ShapeDtypeStruct((count, width), bf16),
            jax.ShapeDtypeStruct((count, width), f32),
            jax.ShapeDtypeStruct((count, width), bf16),
        ],
    )(attended, w_attn, tokens, mod)


def gelu_parts(value):
    factor = 0.7978845608028654
    square = value * value
    half = 0.5 + 0.5 * jnp.tanh(value * (factor + (factor * 0.044715) * square))
    gelu = value * half
    slope = half + gelu * (1.0 - half) * (2.0 * factor + (6.0 * factor * 0.044715) * square)
    return gelu, slope


def joined(refs, axis):
    parts = [ref[...] for ref in refs]
    return parts[0] if len(parts) == 1 else jnp.concatenate(parts, axis=axis)


def hidden_specs(width, tile, part, fast, rows):
    if not fast:
        return [pl.BlockSpec((rows, tile), lambda i, where: (0, 2 * part + i))]

    def block(z):
        def index(i, where):
            j, l = 1 - part, 1 - i
            return 0, z * 4 + (where[1] ^ j) * 2 + (where[2] ^ l)

        return pl.BlockSpec((rows, tile // 4), index)

    return [block(z) for z in range(4)]


def held_spec(shape):
    return pl.BlockSpec(shape, lambda i, where: (0,) * len(shape))


def hidden_call(kernel, name, where, inputs, in_specs, out_specs, out_shape, scratch=()):
    return pl.pallas_call(
        kernel,
        grid_spec=pltpu.PrefetchScalarGridSpec(
            num_scalar_prefetch=1,
            grid=(2,),
            in_specs=in_specs,
            out_specs=out_specs,
            scratch_shapes=list(scratch),
        ),
        out_shape=in_hbm(out_shape),
        compiler_params=pltpu.CompilerParams(vmem_limit_bytes=VMEM_LIMIT),
        cost_estimate=SMALL,
        name=name,
    )(where, *inputs)


def write_quarters(refs, value):
    @pl.when(pl.program_id(0) == 0)
    def _():
        start = 0
        for ref in refs[:-1]:
            ref[...] = value[start : start + ref.shape[0]].astype(bf16)
            start += ref.shape[0]

    @pl.when(pl.program_id(0) == 1)
    def _():
        refs[-1][...] = value.astype(bf16)


def quarter_shapes(tile, width, part):
    cut = FAR_CUT * tile // 4
    return [(tile, width)] * 2 if part else [(cut, width), (tile - cut, width), (tile, width)]


def up_kernel(pieces, where_ref, own_ref, other_ref, mlp_ref, mlp_other_ref, *refs):
    w, bias = joined(refs[:pieces], 1), joined(refs[pieces : 2 * pieces], 1)
    act_ref, slope_ref = refs[2 * pieces : 2 * pieces + 2]
    grad_refs = refs[2 * pieces + 2 :]
    total = None
    for half, (hidden, mlp) in enumerate(((own_ref, mlp_ref), (other_ref, mlp_other_ref))):
        activated, slope = gelu_parts(dot32(hidden[...], w, PLAIN) + bias)
        activated = activated.astype(bf16)
        act_ref[half] = activated
        slope_ref[half] = slope.astype(bf16)
        part = dot32(activated, mlp[...], LEFT_T)
        total = part if total is None else total + part
    write_quarters(grad_refs, total)


def up_forward(where, rows_both, w_up, bias, part, fast):
    count, width = rows_both[0].shape
    inner = w_up.shape[1]
    tile = inner // 4
    both = pl.BlockSpec((2, count, tile), lambda i, where: (0, 0, i))
    w_specs = hidden_specs(width, tile, part, fast, width)
    bias_specs = hidden_specs(width, tile, part, fast, 1)
    pieces = len(w_specs)
    return hidden_call(
        functools.partial(up_kernel, pieces),
        "mlp_up",
        where,
        list(rows_both) + [w_up] * pieces + [bias] * pieces,
        [held_spec((count, width))] * 4 + w_specs + bias_specs,
        [both, both] + [held_spec(shape) for shape in quarter_shapes(tile, width, part)],
        [low_shape(2, count, 2 * tile)] * 2
        + [low_shape(*shape) for shape in quarter_shapes(tile, width, part)],
    )


def down_back_kernel(pieces, part, where_ref, own_ref, other_ref, mlp_ref, mlp_other_ref, down_ref, *refs):
    up = joined(refs[:pieces], 1)
    slope_ref = refs[pieces]
    refs = refs[pieces + 1 :]
    earlier_ref = refs[0] if part else None
    outs = refs[1:] if part else refs
    quarters = 2 if part else 3
    grad_refs, bias_ref = outs[:quarters], outs[quarters]
    back_refs, total_ref = outs[quarters + 1 : -1], outs[-1]
    step = pl.program_id(0)
    down = down_ref[...]
    total, sums = None, None
    for half, (hidden, mlp) in enumerate(((own_ref, mlp_ref), (other_ref, mlp_other_ref))):
        grad_pre = dot32(mlp[...], down, RIGHT_T) * slope_ref[half].astype(f32)
        column = jnp.sum(grad_pre, axis=0, keepdims=True)
        grad_pre = grad_pre.astype(bf16)
        add = dot32(grad_pre, hidden[...], LEFT_T)
        total = add if total is None else total + add
        sums = column if sums is None else sums + column
        back = dot32(grad_pre, up, RIGHT_T)

        @pl.when(step == 0)
        def _(half=half, back=back):
            total_ref[half] = back + earlier_ref[half].astype(f32) if part else back

        @pl.when(step > 0)
        def _(half=half, back=back):
            total_ref[half] += back

    bias_ref[...] = sums
    write_quarters(grad_refs, total)

    @pl.when(step == 1)
    def _():
        if part:
            back_refs[0][...] = total_ref[0]
            back_refs[1][...] = total_ref[1].astype(bf16)
        else:
            back_refs[0][...] = total_ref[...].astype(bf16)


def down_backward(where, rows_both, w_down, w_up, slope, part, earlier, fast):
    count, width = rows_both[0].shape
    inner = w_up.shape[1]
    tile = inner // 4
    back_shape = (2, count, width)
    if part:
        back_specs = [held_spec((count, width))] * 2
        back_shapes = [jax.ShapeDtypeStruct((count, width), f32), low_shape(count, width)]
    else:
        back_specs = [held_spec(back_shape)]
        back_shapes = [low_shape(*back_shape)]
    w_specs = hidden_specs(width, tile, part, fast, width)
    pieces = len(w_specs)
    return hidden_call(
        functools.partial(down_back_kernel, pieces, part),
        "mlp_back",
        where,
        list(rows_both) + [w_down] + [w_up] * pieces + [slope] + ([earlier] if part else []),
        [held_spec((count, width))] * 4
        + [pl.BlockSpec((tile, width), lambda i, where: (2 * part + i, 0))]
        + w_specs
        + [pl.BlockSpec((2, count, tile), lambda i, where: (0, 0, i))]
        + ([held_spec(back_shape)] if part else []),
        [held_spec(shape) for shape in quarter_shapes(tile, width, part)]
        + [pl.BlockSpec((1, tile), lambda i, where: (0, i))]
        + back_specs,
        [low_shape(*shape) for shape in quarter_shapes(tile, width, part)]
        + [jax.ShapeDtypeStruct((1, 2 * tile), f32)]
        + back_shapes,
        [pltpu.VMEM(back_shape, f32)],
    )


def down_kernel(first_ref, second_ref, w_ref, own_ref, other_ref):
    half = first_ref.shape[2]
    for number, out_ref in enumerate((own_ref, other_ref)):
        total = dot32(first_ref[number], w_ref[:half], PLAIN)
        total = total + dot32(second_ref[number], w_ref[half:], PLAIN)
        out_ref[...] = total.astype(out_ref.dtype)


def down_forward(first, second, w_down):
    _, count, half = first.shape
    width = w_down.shape[1]
    tile = 256
    row_spec = pl.BlockSpec((count, tile), lambda i: (0, i))
    return dense_call(
        down_kernel,
        "mlp_down",
        (width // tile,),
        [full_spec(first.shape)] * 2 + [pl.BlockSpec((2 * half, tile), lambda i: (0, i))],
        [row_spec, row_spec],
        [jax.ShapeDtypeStruct((count, width), f32), low_shape(count, width)],
    )(first, second, w_down)


def split_away(where_ref, rows_ref, away_ref):
    first = pl.multiple_of((1 - where_ref[2]) * 2 * SPATIAL, 2 * SPATIAL)
    away_ref[: 2 * SPATIAL] = rows_ref[pl.ds(first, 2 * SPATIAL), :]
    away_ref[2 * SPATIAL :] = rows_ref[4 * SPATIAL :, :]


def result_kernel(
    where_ref, own_ref, other_ref, bias_ref, mid_ref, cot_ref, mod_ref, live_ref,
    result_ref, away_ref, gate_ref,
):
    branch = own_ref[...] + other_ref[...].astype(f32) + bias_ref[...]
    result_ref[...] = (mid_ref[...] + modulation(mod_ref, 5) * branch).astype(bf16)
    split_away(where_ref, result_ref, away_ref)
    gate_ref[0] = live_ref[0] * jnp.sum(branch * cot_ref[...].astype(f32), axis=0, keepdims=True)


def result_forward(where, own, other, bias, mid, cotangent, mod, live):
    count, width = own.shape
    local = mod.shape[0]
    row_spec = pl.BlockSpec((count // local, width), lambda i: (i, 0))
    one = pl.BlockSpec((1, 1, width), lambda i: (i, 0, 0))
    return dense_call(
        result_kernel,
        "result",
        (local,),
        [pl.BlockSpec(memory_space=pltpu.SMEM)]
        + [row_spec, row_spec, full_spec(bias.shape), row_spec, row_spec]
        + [pl.BlockSpec((1,) + mod.shape[1:], lambda i: (i, 0, 0)), one],
        [row_spec, pl.BlockSpec((3 * SPATIAL, width), lambda i: (i, 0)), one],
        [
            low_shape(count, width),
            low_shape(local * 3 * SPATIAL, width),
            jax.ShapeDtypeStruct((local, 1, width), f32),
        ],
    )(where, own, other, bias, mid, cotangent, mod, live)


def mid_back_kernel(
    own_ref, other_ref, mid_ref, cot_ref, branch_ref, attended_ref, w_ref, mod_ref, live_ref,
    grad_mid_ref, grad_attended_ref, sums_ref, grad_ref, total_ref,
):
    step, last = pl.program_id(0), pl.num_programs(0) - 1
    grad_hidden = own_ref[...] + other_ref[...].astype(f32)
    normed, inverse = normalize(mid_ref[...])
    back = normalize_back(grad_hidden * (1.0 + modulation(mod_ref, 4)), normed, inverse)
    grad_mid = cot_ref[...].astype(f32) + back
    grad_mid_ref[...] = grad_mid
    gate = jnp.sum(branch_ref[...].astype(f32) * grad_mid, axis=0, keepdims=True)
    sums_ref[0, 0:1] = live_ref[0] * gate
    sums_ref[0, 1:2] = jnp.sum(grad_hidden, axis=0, keepdims=True)
    sums_ref[0, 2:3] = jnp.sum(grad_hidden * normed, axis=0, keepdims=True)
    grad_branch = (modulation(mod_ref, 2) * grad_mid).astype(bf16)
    grad_attended_ref[...] = dot32(grad_branch, w_ref[...], RIGHT_T).astype(bf16)
    part = dot32(grad_branch, attended_ref[...], LEFT_T)

    @pl.when(step == 0)
    def _():
        total_ref[...] = part

    @pl.when(step > 0)
    def _():
        total_ref[...] += part

    @pl.when(step == last)
    def _():
        grad_ref[...] = total_ref[...].astype(bf16)


def mid_backward(own, other, mid, cotangent, branch, attended, w_attn, mod, live):
    count, width = own.shape
    local = mod.shape[0]
    row_spec = pl.BlockSpec((count // local, width), lambda i: (i, 0))
    return dense_call(
        mid_back_kernel,
        "mid_back",
        (local,),
        [row_spec] * 6
        + [
            full_spec((width, width)),
            pl.BlockSpec((1,) + mod.shape[1:], lambda i: (i, 0, 0)),
            pl.BlockSpec((1, 1, width), lambda i: (i, 0, 0)),
        ],
        [
            row_spec,
            row_spec,
            pl.BlockSpec((1, 8, width), lambda i: (i, 0, 0)),
            full_spec((width, width)),
        ],
        [
            jax.ShapeDtypeStruct((count, width), f32),
            jax.ShapeDtypeStruct((count, width), bf16),
            jax.ShapeDtypeStruct((local, 8, width), f32),
            jax.ShapeDtypeStruct((width, width), bf16),
        ],
        [pltpu.VMEM((width, width), f32)],
    )(own, other, mid, cotangent, branch, attended, w_attn, mod, live)


def grad_pieces(tiles, tile, width):
    block, out_block = tiles * tile // 32, width // 32
    pieces = []
    for number in range(32):
        pieces.append((0, number, None, number * out_block, block, out_block))
        first, rest, to = number * block, block, 0
        while rest:
            size = min(rest, tile - first % tile)
            pieces.append((first // tile, number, first // tile, first % tile, to, size))
            first, rest, to = first + size, rest - size, to + size
    return pieces


def qkv_grad_kernel(pieces, where_ref, grad_ref, hidden_ref, out_grad_ref, *refs):
    outs, whole_ref, sems = refs[:4], refs[4], refs[5]
    x, y, c = where_ref[1], where_ref[2], where_ref[3]
    step, steps = pl.program_id(0), pl.num_programs(0)
    whole_ref[step] = dot32(grad_ref[0], hidden_ref[...], LEFT_T).astype(bf16)

    for now in range(whole_ref.shape[0]):
        for here_x in range(2):
            for here_c in range(2):

                @pl.when((step == now) & (x == here_x) & (c == here_c))
                def _(now=now, here_x=here_x, here_c=here_c):
                    for count, (ready, number, tile, first, start, size) in enumerate(pieces):
                        if ready != now:
                            continue
                        z, l = number // 8, (number // 2 % 2) ^ y
                        j, core = (number // 4 % 2) ^ here_x, (number % 2) ^ here_c
                        rows = pl.ds(first, size)
                        source = out_grad_ref.at[rows] if tile is None else whole_ref.at[tile, rows]
                        place = outs[2 * core + 1 - j].at[1 - l, z, pl.ds(start, size)]
                        pltpu.make_async_copy(source, place, sems.at[count]).start()

    @pl.when(step == steps - 1)
    def _():
        for count, piece in enumerate(pieces):
            place = outs[0].at[0, 0, pl.ds(0, piece[5])]
            pltpu.make_async_copy(place, place, sems.at[count]).wait()


def qkv_grad(where, grad_projected, hidden, grad_out):
    count, width = hidden.shape
    tile = 512
    per = width // tile
    rows = 4 * width // 32
    shape = low_shape(2, 4, rows, width)
    pieces = grad_pieces(3 * per, tile, width)
    return pl.pallas_call(
        functools.partial(qkv_grad_kernel, pieces),
        grid=(3 * per,),
        in_specs=[
            pl.BlockSpec(memory_space=pltpu.SMEM),
            pl.BlockSpec((1, count, tile), lambda i: (i // per, 0, i % per)),
            full_spec(hidden.shape),
            full_spec(grad_out.shape),
        ],
        out_specs=[pl.BlockSpec(memory_space=pl.ANY)] * 4,
        out_shape=[shape] * 4,
        scratch_shapes=[
            pltpu.VMEM((3 * per, tile, width), bf16),
            pltpu.SemaphoreType.DMA((len(pieces),)),
        ],
        compiler_params=pltpu.CompilerParams(vmem_limit_bytes=VMEM_LIMIT),
        cost_estimate=SMALL,
        name="qkv_grad",
    )(where, grad_projected, hidden, grad_out)


def qkv_grad_plain(grad_projected, hidden):
    return lax.dot_general(
        grad_projected, hidden, (((1,), (0,)), ((), ())), preferred_element_type=f32
    ).astype(bf16)


def tokens_back_kernel(
    where_ref, grad_ref, w_ref, tokens_ref, grad_mid_ref, mod_ref, out_ref, away_ref, sums_ref
):
    width = tokens_ref.shape[1]
    grad_hidden = None
    for part in range(3):
        add = dot32(grad_ref[part], w_ref[:, part * width : (part + 1) * width], RIGHT_T)
        grad_hidden = add if grad_hidden is None else grad_hidden + add
    normed, inverse = normalize(tokens_ref[...].astype(f32))
    back = normalize_back(grad_hidden * (1.0 + modulation(mod_ref, 1)), normed, inverse)
    out_ref[...] = (grad_mid_ref[...] + back).astype(bf16)
    split_away(where_ref, out_ref, away_ref)
    sums_ref[0, 0:1] = jnp.sum(grad_hidden, axis=0, keepdims=True)
    sums_ref[0, 1:2] = jnp.sum(grad_hidden * normed, axis=0, keepdims=True)


def tokens_backward(where, grad_projected, w_qkv, tokens, grad_mid, mod):
    count, width = tokens.shape
    local = mod.shape[0]
    rows = count // local
    row_spec = pl.BlockSpec((rows, width), lambda i: (i, 0))
    return dense_call(
        tokens_back_kernel,
        "tokens_back",
        (local,),
        [
            pl.BlockSpec(memory_space=pltpu.SMEM),
            pl.BlockSpec((3, rows, width), lambda i: (0, i, 0)),
            full_spec((width, 3 * width)),
            row_spec,
            row_spec,
            pl.BlockSpec((1,) + mod.shape[1:], lambda i: (i, 0, 0)),
        ],
        [
            row_spec,
            pl.BlockSpec((3 * SPATIAL, width), lambda i: (i, 0)),
            pl.BlockSpec((1, 8, width), lambda i: (i, 0, 0)),
        ],
        [
            low_shape(count, width),
            low_shape(local * 3 * SPATIAL, width),
            jax.ShapeDtypeStruct((local, 8, width), f32),
        ],
    )(where, grad_projected, w_qkv, tokens, grad_mid, mod)


def modulation_kernel(parts_ref, bias_ref, live_ref, out_ref):
    sources, holders, local, part = parts_ref.shape
    width = out_ref.shape[2] // 6
    for window in range(local):
        for holder in range(holders):
            total = parts_ref[0, holder, window : window + 1]
            for source in range(1, sources):
                total = total + parts_ref[source, holder, window : window + 1]
            columns = slice(holder * part, (holder + 1) * part)
            out_ref[window, :, columns] = total + bias_ref[:, columns]
        for gate in (2, 5):
            columns = slice(gate * width, (gate + 1) * width)
            out_ref[window, :, columns] = out_ref[window, :, columns] * live_ref[window]


def modulate(parts, bias, live):
    local, _, width = live.shape
    return dense_call(
        modulation_kernel,
        "modulation",
        (1,),
        [full_spec(parts.shape), full_spec(bias.shape), full_spec(live.shape)],
        full_spec((local, 1, 6 * width)),
        jax.ShapeDtypeStruct((local, 1, 6 * width), f32),
    )(parts, bias, live)


def gated_kernel(where_ref, rows_ref, mod_ref, out_ref):
    out_ref[...] = (modulation(mod_ref, 5) * rows_ref[...].astype(f32)).astype(bf16)


def gated(where, rows, mod):
    count, width = rows.shape
    local = mod.shape[0]
    row_spec = pl.BlockSpec((count // local, width), lambda i: (i, 0))
    return dense_call(
        gated_kernel,
        "gated",
        (local,),
        [
            pl.BlockSpec(memory_space=pltpu.SMEM),
            row_spec,
            pl.BlockSpec((1,) + mod.shape[1:], lambda i: (i, 0, 0)),
        ],
        row_spec,
        low_shape(count, width),
    )(where, rows, mod)


def space_onehot():
    places = jnp.arange(SPATIAL, dtype=jnp.int32)
    across, along = places // SIDE, places % SIDE
    index = (across[:, None] - across[None, :] + SIDE - 1) * (2 * SIDE - 1) + (
        along[:, None] - along[None, :] + SIDE - 1
    )
    ids = jnp.arange((2 * SIDE - 1) ** 2, dtype=jnp.int32)
    return (index.reshape(-1)[:, None] == ids[None, :]).astype(f32)


def on_device(
    tokens,
    condition,
    doubled,
    window_count,
    w_ada,
    b_ada,
    w_qkv,
    w_out,
    w_up,
    b_up,
    w_down,
    b_down,
    table_space,
    table_time,
    cotangent,
):
    windows, _, width = tokens.shape
    heads = table_space.shape[0]
    n_win = lax.axis_size("win")
    devices = n_win * 4
    win = lax.axis_index("win")
    frm = lax.axis_index("frm")
    z, x, y, c = win // 2, win % 2, frm // 2, frm % 2
    where = jnp.concatenate([jnp.stack([z, x, y, c, frm, window_count[0]]), doubled])
    where = where.astype(jnp.int32)
    local = windows // 4
    count = local * FRAMES * SPATIAL
    ff = w_up.shape[1]
    ff_block = ff // devices
    shard_rows = w_qkv.shape[0]
    half_width = width // 2
    fast = n_win == 8
    slot_shape = (2 * windows, SPATIAL, width)

    tok_slots, cot_slots = tokens.reshape(slot_shape), cotangent.reshape(slot_shape)
    tok_send = windows_send(where, tok_slots)
    biases = jnp.concatenate([b_ada, b_up, b_down])
    bias_rows = -(-biases.shape[0] // width)
    biases = jnp.pad(biases, (0, bias_rows * width - biases.shape[0])).reshape(bias_rows, width)
    small = jnp.concatenate([condition, biases])
    if fast:
        q_half, up_half, down_half = halves(where, w_qkv, w_out, w_up, w_down)
        q_direct = gather_z_direct(q_half)
        tok_send, _ = sync(tok_send, q_half)
        small, _ = sync(small, tok_send)
    small_all = lax.all_to_all(
        jnp.broadcast_to(small[None], (n_win,) + small.shape),
        "win",
        split_axis=0,
        concat_axis=0,
        tiled=True,
    )
    tok_got = swap_core(tok_send)
    tok_here, tok_away = windows_pack(where, tok_slots, tok_got)
    tok_back = swap_y(tok_away)

    onehot_space = space_onehot()
    space_bias = jnp.dot(table_space, onehot_space.T, precision=exact_mode)
    space_bias = jnp.tile(space_bias.reshape(heads, SPATIAL, SPATIAL), (1, 1, FRAMES))
    mine_doubled = lax.dynamic_slice_in_dim(doubled, frm * local, local, 0)
    holders = jnp.arange(4, dtype=jnp.int32)
    frames = holders[None, :] + (holders[None, :] > mine_doubled[:, None]).astype(jnp.int32)
    frames = jnp.concatenate([frames, mine_doubled[:, None] + 1], axis=1)
    offset = frames[:, :, None] - frames[:, None, :] + FRAMES - 1
    onehot_time = (
        offset[..., None] == jnp.arange(table_time.shape[1], dtype=jnp.int32)
    ).astype(f32)
    time_bias = jnp.einsum("wabt,ht->whab", onehot_time, table_time, precision=exact_mode)
    time_bias = jnp.repeat(time_bias, SPATIAL, axis=-1)
    time_bias = jnp.pad(time_bias, ((0, 0), (0, 0), (0, 8 - FRAMES), (0, 0)))

    if fast:
        *q_direct, _ = sync(*q_direct, tok_away)
        q_stack = jnp.stack(q_direct)
        q_near = gather_near(q_stack)
        small_all, up_half, _ = sync(small_all, up_half, q_stack)
        up_direct = gather_z_direct(up_half)

    cond_all = small_all[:, :windows].reshape(n_win * windows, width).astype(f32)
    bias_all = small_all[:, windows:].reshape(n_win, bias_rows * width).astype(f32)
    cuts = [b_ada.shape[0], b_ada.shape[0] + b_up.shape[0]]
    ada_bias = bias_all[:, : cuts[0]].reshape(1, 6 * width)
    up_bias = bias_all[:, cuts[0] : cuts[1]].reshape(n_win * 2, 2, ff_block)
    up_bias = pick(up_bias, c, 1).reshape(1, ff // 2)
    down_bias = bias_all[:, cuts[1] : cuts[1] + b_down.shape[0]].reshape(1, width)
    silu_all = jax.nn.silu(cond_all).astype(bf16)
    silu_part = lax.dynamic_slice_in_dim(silu_all, win * shard_rows, shard_rows, 1)
    ada_quarter = 6 * width // 4
    ada_part = lax.dynamic_slice_in_dim(w_ada, frm * ada_quarter, ada_quarter, 1)
    mod_part = dot32(silu_part, ada_part, PLAIN)
    if fast:
        *q_near, mod_part, up_bias, down_bias, space_bias, time_bias = sync(
            *q_near, mod_part, up_bias, down_bias, space_bias, time_bias
        )
        q_far = gather_far(q_near)
        *up_direct, q_near[0], q_near[1], q_near[2] = sync(*up_direct, *q_near)
        q_other = [swap_core(part) for part in q_near]
    else:
        qkv_full = lax.all_gather(w_qkv, "win", axis=0).reshape(width, 3 * width)
        out_full = lax.all_gather(w_out, "win", axis=0).reshape(width, width)
        up_shard = pick(w_up.reshape(shard_rows, n_win * 2, 2, ff_block), c, 2)
        up_full = lax.all_gather(up_shard, "win", axis=0).reshape(width, ff // 2)
        down_shard = pick(w_down.reshape(2, 2, ff_block, width), c, 1)
        down_full = lax.all_gather(down_shard, "win", axis=0).reshape(ff // 2, width)
    mod_parts = exchange_all(mod_part.reshape(devices, local, ada_quarter))
    my_window = frm * local + jnp.arange(local, dtype=jnp.int32)
    live = (my_window < window_count[0]).astype(f32)[:, None, None]
    live = jnp.broadcast_to(live, (local, 1, width))
    cot_send = windows_send(where, cot_slots)
    if fast:
        up_stack = jnp.stack(up_direct)
        q_far[0], tok_back, mod_parts, cot_send, up_stack, *q_other = sync(
            q_far[0], tok_back, mod_parts, cot_send, up_stack, *q_other
        )
        q_other = q_other + [swap_core(part) for part in q_far]
        up_near = gather_near(up_stack)
        qkv_full, out_full = place_qkv(where, list(q_near) + list(q_far) + q_other)
    cot_got = swap_core(cot_send)
    token_rows = windows_join(where, tok_here, tok_back)
    mod = modulate(mod_parts.reshape(n_win, 4, local, ada_quarter), ada_bias, live)

    projected, hidden_one = qkv_forward(token_rows, mod, qkv_full)
    cot_here, cot_away = windows_pack(where, cot_slots, cot_got)
    if fast:
        projected, cot_away, down_half, *up_near = sync(
            projected, cot_away, down_half, *up_near
        )
        up_far = gather_far(up_near)
        down_direct = gather_z_direct(down_half)
    cot_back = swap_y(cot_away)
    attended, probs = attend(projected, space_bias, time_bias, local)
    if fast:
        attended, cot_back, up_far[0], *down_direct = sync(
            attended, cot_back, up_far[0], *down_direct
        )
        down_near = gather_near(jnp.stack(down_direct))
    branch_attn, mid, hidden_two = out_forward(attended, out_full, token_rows, mod)
    grad_out = windows_join(where, cot_here, cot_back)
    grad_mlp = gated(where, grad_out, mod)
    mlp_other = swap_core(grad_mlp)

    hidden_other = swap_core(hidden_two)
    if fast:
        up_full = place_up(where, list(up_near) + list(up_far))
    rows_both = (hidden_two, hidden_other, grad_mlp, mlp_other)
    act_first, slope_first, *down_grads = up_forward(where, rows_both, up_full, up_bias, 0, fast)
    if fast:
        act_first, up_bias, *down_near = sync(act_first, up_bias, *down_near)
        down_far = gather_far(down_near, FAR_CUT)
    act_second, slope_second, *more = up_forward(where, rows_both, up_full, up_bias, 1, fast)
    if fast:
        act_second, *down_far = sync(act_second, *down_far)
        down_fy, down_fx = swap_y(down_grads[0]), swap_win(down_grads[1], 1)
        down_full = place_down(where, list(down_near) + list(down_far))
    down_grads = list(down_grads) + more
    block_rows = ff_block
    *up_grads, up_b_first, back_first = down_backward(
        where, rows_both, down_full, up_full, slope_first, 0, None, fast
    )
    if fast:
        back_first, *up_grads, down_fy, down_fx = sync(back_first, *up_grads, down_fy, down_fx)
        send_x, send_y = merge(
            [(down_grads[2], None)], [(down_grads[3], None)], down_fy, down_fx
        )
        back_first, send_x, send_y = sync(back_first, send_x, send_y)
        down_x, down_y = swap_win(send_x, 1), swap_y(send_y)
    *more, up_b_second, back_own, back_other = down_backward(
        where, rows_both, down_full, up_full, slope_second, 1, back_first, fast
    )
    up_grads = list(up_grads) + more
    if fast:
        back_other, act_first, down_x, down_y = sync(back_other, act_first, down_x, down_y)
        up_fy, up_fx = swap_y(up_grads[0]), swap_win(up_grads[1], 1)
        down_kept = total(
            [(down_grads[4], None), (down_x, None), (down_y, None)], block_rows, width
        )
    back_got = swap_core(back_other)
    mlp_own, mlp_away = down_forward(act_first, act_second, down_full)

    if fast:
        back_got, mlp_away, down_kept, *up_grads, up_fy, up_fx = sync(
            back_got, mlp_away, down_kept, *up_grads, up_fy, up_fx
        )
        down_grad = sum_z(down_kept)
        send_x, send_y = merge([(up_grads[2], None)], [(up_grads[3], None)], up_fy, up_fx)
        back_got, send_x, send_y = sync(back_got, send_x, send_y)
        up_x, up_y = swap_win(send_x, 1), swap_y(send_y)
    mlp_got = swap_core(mlp_away)
    grad_mid, grad_attended, mid_sums, grad_out_w = mid_backward(
        back_own, back_got, mid, grad_out, branch_attn, attended, out_full, mod, live
    )
    grad_attended, mlp_got = sync(grad_attended, mlp_got)
    result, res_away, gate_two_sum = result_forward(
        where, mlp_own, mlp_got, down_bias, mid, grad_out, mod, live
    )
    grad_attended, res_away = sync(grad_attended, res_away)
    res_back = swap_y(res_away.reshape(6, SPATIAL, width))
    grad_projected, space_sums, time_sums = attend_back(
        projected, grad_attended, attended, probs, local
    )
    qkv_block, out_block = 3 * width // devices, width // devices
    if fast:
        grad_projected, up_x, up_y, res_back, down_grad = sync(
            grad_projected, up_x, up_y, res_back, down_grad
        )
        own_first, own_second, other_first, other_second = qkv_grad(
            where, grad_projected, hidden_one, grad_out_w
        )
        up_x, other_first, other_second = sync(up_x, other_first, other_second)
        up_kept = total([(up_grads[4], None), (up_x, None), (up_y, None)], block_rows, width)
        up_grad = sum_z(up_kept)
        got_first, got_second = swap_core(other_first), swap_core(other_second)
    if fast:
        got_first, up_kept = sync(got_first, up_kept)
        send_fy, send_fx, attn_gx = first_quarters(own_first, got_first)
        send_fy, send_fx, grad_projected = sync(send_fy, send_fx, grad_projected)
        attn_fy, attn_fx = swap_y(send_fy), swap_win(send_fx, 1)
    else:
        grad_attn_w = jnp.concatenate(
            [
                qkv_grad_plain(grad_projected, hidden_one).reshape(n_win, 2, 2, qkv_block, width),
                grad_out_w.reshape(n_win, 2, 2, out_block, width),
            ],
            axis=3,
        )
        got = swap_core(pick(grad_attn_w, 1 - c, 2))
        attn_grad = scatter_plain(add_low(pick(grad_attn_w, c, 2), got), where)
        up_grad = scatter_plain(jnp.concatenate(up_grads).reshape(n_win, 2, ff_block, width), where)
        down_grad = scatter_plain(
            jnp.concatenate(down_grads).reshape(n_win, 2, ff_block, width), where
        )
    grad_tokens, gt_away, token_sums = tokens_backward(
        where, grad_projected, qkv_full, token_rows, grad_mid, mod
    )
    gt_away = gt_away.reshape(6, SPATIAL, width)
    if fast:
        token_sums, attn_fy, attn_fx, got_second = sync(
            token_sums, attn_fy, attn_fx, got_second
        )
        send_x, send_y = merge(
            [(attn_gx, None)], [(own_second, 0), (got_second, 0)], attn_fy, attn_fx, LAST_CUT
        )
        attn_x, attn_y = swap_win(send_x, 1), swap_y(send_y)
        token_sums, res_back, _, _ = sync(token_sums, res_back, send_x, send_y)

    grad_mod = jnp.concatenate(
        [
            token_sums[:, 0],
            token_sums[:, 1],
            mid_sums[:, 0],
            mid_sums[:, 1],
            mid_sums[:, 2],
            gate_two_sum[:, 0],
        ],
        axis=-1,
    ).astype(bf16)
    ada_block = 6 * width // devices
    to_quarter = jnp.transpose(grad_mod.reshape(local, 4, ada_quarter), (1, 0, 2))
    to_quarter = jnp.broadcast_to(to_quarter[None], (n_win, 4, local, ada_quarter))
    to_block = jnp.transpose(grad_mod.reshape(local, devices, ada_block), (1, 0, 2))
    grad_up_b = jnp.concatenate([up_b_first, up_b_second], axis=1)
    if fast:
        grad_up_b = grad_up_b.reshape(2, 2, 4, ff_block)
        grad_up_b = jnp.where(x == 0, grad_up_b[::-1], grad_up_b)
        grad_up_b = jnp.where(y == 0, grad_up_b[:, ::-1], grad_up_b)
        grad_up_b = jnp.transpose(grad_up_b, (2, 0, 1, 3))
    grad_up_b = grad_up_b.reshape(n_win * 2, 1, ff_block)
    core_mask = (jnp.arange(2, dtype=jnp.int32) == c).astype(f32)[None, :, None]
    grad_up_b = (grad_up_b * core_mask).reshape(devices, ff_block)
    grad_down_b = jnp.sum(grad_mlp.astype(f32), axis=0).reshape(devices, width // devices)
    first_send = jnp.concatenate(
        [
            to_quarter.reshape(devices, local * ada_quarter),
            to_block.reshape(devices, local * ada_block),
            grad_up_b.astype(bf16),
            grad_down_b.astype(bf16),
        ],
        axis=1,
    )
    res_other = swap_core(windows_back_pack(where, result, res_back))
    first_got = exchange_all(first_send)
    if fast:
        attn_x, attn_y, gt_away, res_other, first_send = sync(
            attn_x, attn_y, gt_away, res_other, first_send
        )
        kept = total(
            [(own_second, 1), (got_second, 1), (attn_x, None), (attn_y, None)],
            qkv_block + out_block,
            width,
        )
        attn_grad = sum_z_direct(kept, z)
        first_got, _ = sync(first_got, kept)
    gt_back = swap_y(gt_away)
    if fast:
        space_sums, time_sums, gt_back = sync(space_sums, time_sums, gt_back)
    lanes = jnp.arange(FRAMES * SPATIAL, dtype=jnp.int32)
    to_place = (lanes[:, None] % SPATIAL == jnp.arange(SPATIAL)[None]).astype(f32)
    to_slot = (lanes[:, None] // SPATIAL == jnp.arange(FRAMES)[None]).astype(f32)
    space_sum = jnp.dot(
        space_sums.reshape(heads * SPATIAL, FRAMES * SPATIAL), to_place, precision=exact_mode
    )
    space_sum = jnp.dot(
        space_sum.reshape(heads, SPATIAL * SPATIAL), onehot_space, precision=exact_mode
    )
    time_sum = jnp.dot(
        time_sums.reshape(local * heads * 8, FRAMES * SPATIAL), to_slot, precision=exact_mode
    ).reshape(local, heads, 8, FRAMES)[:, :, :FRAMES]
    time_sum = jnp.einsum("whab,wabt->ht", time_sum, onehot_time, precision=exact_mode)
    tables = jnp.concatenate([space_sum.reshape(-1), time_sum.reshape(-1)])
    sizes = [local * ada_quarter, local * ada_block, ff_block, width // devices]
    ends = [sum(sizes[: n + 1]) for n in range(4)]
    mod_got = first_got[:, : ends[0]].reshape(n_win * windows, ada_quarter)
    mod_own = first_got[:, ends[0] : ends[1]].reshape(n_win * windows, ada_block)
    sums = jnp.sum(first_got[:, ends[1] :].astype(f32), axis=0)
    out_up_b = sums[:ff_block]
    out_down_b = sums[ff_block : ff_block + width // devices]
    grad_ada_w = dot32(silu_all, mod_own, LEFT_T)
    grad_ada_b = jnp.sum(mod_own.astype(f32), axis=0)
    cond_part = dot32(mod_got, ada_part, RIGHT_T)
    cond_send = cond_part.astype(bf16).reshape(n_win, 1, windows * shard_rows)
    cond_send = jnp.broadcast_to(cond_send, (n_win, 4, windows * shard_rows))
    cond_send = cond_send.reshape(devices, windows * shard_rows)
    table_send = jnp.broadcast_to(tables.astype(bf16)[None], (devices, tables.shape[0]))
    last_got = exchange_all(jnp.concatenate([cond_send, table_send], axis=1)).astype(f32)
    cond_grad = last_got[:, : windows * shard_rows].reshape(n_win, 4, windows, shard_rows)
    cond_grad = jnp.transpose(jnp.sum(cond_grad, axis=1), (1, 0, 2)).reshape(windows, width)
    _, silu_back = jax.vjp(jax.nn.silu, condition.astype(f32))
    grad_condition = silu_back(cond_grad)[0]
    table_all = jnp.sum(last_got[:, windows * shard_rows :], axis=0)
    space_size = table_space.size
    grad_space = table_all[:space_size].reshape(table_space.shape)
    grad_time = table_all[space_size : space_size + table_time.size].reshape(table_time.shape)

    gt_other = swap_core(windows_back_pack(where, grad_tokens, gt_back))
    result = windows_back_join(where, result, res_back, res_other, tokens, bf16)
    grad_tokens = windows_back_join(where, grad_tokens, gt_back, gt_other, cotangent, f32)

    return (
        result,
        grad_tokens,
        grad_condition,
        grad_ada_w,
        grad_ada_b,
        attn_grad[:qkv_block].T,
        attn_grad[qkv_block:].T,
        up_grad.T,
        out_up_b,
        down_grad,
        out_down_b,
        grad_space,
        grad_time,
    )


def solution(mesh):
    return jax.shard_map(
        on_device,
        mesh=mesh,
        in_specs=(
            P("win", "frm", None),
            P("win", None),
            P("win"),
            P("win"),
            P("win", None),
            P("win"),
            P("win", None),
            P("win", None),
            P("win", None),
            P("win"),
            P("win", None),
            P("win"),
            P(),
            P(),
            P("win", "frm", None),
        ),
        out_specs=(
            P("win", "frm", None),
            P("win", "frm", None),
            P("win", None),
            P(None, BOTH),
            P(BOTH),
            P(None, BOTH),
            P(None, BOTH),
            P(None, BOTH),
            P(BOTH),
            P(BOTH, None),
            P(BOTH),
            P(),
            P(),
        ),
        check_vma=False,
    )
```

```python
import functools

import jax
import jax.numpy as jnp
from jax import lax
from jax.experimental import pallas as pl
from jax.experimental.pallas import tpu as pltpu
from jax.sharding import PartitionSpec as P

SIDE = 8
FRAMES = 5
SPATIAL = SIDE * SIDE
BOTH = ("win", "frm")
EPS = 1e-06
VMEM_LIMIT = 50 * 1024 * 1024
WHOLE_LIMIT = 60 * 1024 * 1024

f32 = jnp.float32
bf16 = jnp.bfloat16
exact_mode = lax.Precision.HIGHEST
SMALL = pl.CostEstimate(flops=1024, bytes_accessed=1024, transcendentals=0)


def swap_frm(array, bit):
    return lax.ppermute(array, "frm", [(j, j ^ bit) for j in range(4)])


def swap_core(array):
    return swap_frm(array, 1)


def swap_y(array):
    return swap_frm(array, 2)


def swap_win(array, bits):
    count = lax.axis_size("win")
    return lax.ppermute(array, "win", [(j, j ^ bits) for j in range(count)])


def exchange_all(array):
    return lax.all_to_all(array, BOTH, split_axis=0, concat_axis=0, tiled=True)


def pick(array, index, axis):
    return lax.dynamic_index_in_dim(array, index, axis, keepdims=False)


def sync(*arrays):
    return lax.optimization_barrier(arrays)


def exchange_z(blocks):
    groups = [[2 * z + x for z in range(4)] for x in range(2)]
    return lax.all_to_all(
        blocks, "win", split_axis=0, concat_axis=0, axis_index_groups=groups, tiled=True
    )


def gather_z(half):
    return exchange_z(jnp.broadcast_to(half[None], (4,) + half.shape))


def gather_z_direct(half):
    return [half] + [swap_win(half, 2 * k) for k in (1, 2, 3)]


def move_kernel(body, count, where, *refs):
    sems = refs[count]
    refs = refs[:count] + refs[count + 1 :]
    waits = []

    def copy(sources, target):
        sem = sems.at[len(waits)]
        if len(sources) == 1:
            pltpu.make_async_copy(sources[0], target, sem).start()
        else:
            condition, first, second = sources

            @pl.when(condition)
            def _():
                pltpu.make_async_copy(first, target, sem).start()

            @pl.when(jnp.logical_not(condition))
            def _():
                pltpu.make_async_copy(second, target, sem).start()

        waits.append(pltpu.make_async_copy(sources[-1], target, sem))

    def finish():
        for wait in waits:
            wait.wait()

    body(where, refs, copy, finish)


def move_call(body, name, where, inputs, outputs, copies, scratch=(), limit=VMEM_LIMIT):
    return pl.pallas_call(
        functools.partial(move_kernel, body, len(inputs) + len(outputs)),
        out_shape=outputs,
        in_specs=[pl.BlockSpec(memory_space=pltpu.SMEM)]
        + [pl.BlockSpec(memory_space=pltpu.HBM)] * len(inputs),
        out_specs=[pl.BlockSpec(memory_space=pltpu.VMEM)] * len(outputs),
        scratch_shapes=[pltpu.SemaphoreType.DMA((copies,))] + list(scratch),
        compiler_params=pltpu.CompilerParams(vmem_limit_bytes=limit),
        cost_estimate=SMALL,
        name=name,
    )(where, *inputs)


def low_shape(*shape):
    return jax.ShapeDtypeStruct(shape, bf16)


def halves(where, w_qkv, w_out, w_up, w_down):
    rows, width = w_out.shape
    blocks = w_up.shape[1] // 256
    block = w_down.shape[0] // 4

    def body(where, refs, copy, finish):
        qkv, out, up, down, q_half, up_half, down_half = refs
        y, c = where[2], where[3]
        quarter = rows // 4
        q_rows = pl.ds(pl.multiple_of((c * 2 + y) * quarter, quarter), quarter)
        copy([qkv.at[q_rows]], q_half.at[:, pl.ds(0, 3 * width)])
        copy([out.at[q_rows]], q_half.at[:, pl.ds(3 * width, width)])
        up_rows = pl.ds(pl.multiple_of(y * (rows // 2), rows // 2), rows // 2)
        for n in range(blocks):
            column = pl.multiple_of((2 * n + c) * 128, 128)
            copy([up.at[up_rows, pl.ds(column, 128)]], up_half.at[:, pl.ds(n * 128, 128)])
        copy([down.at[pl.ds(pl.multiple_of((y * 2 + c) * block, block), block)]], down_half)
        finish()

    return move_call(
        body,
        "halves",
        where,
        [w_qkv, w_out, w_up, w_down],
        [
            low_shape(rows // 4, 4 * width),
            low_shape(rows // 2, blocks * 128),
            low_shape(block, width),
        ],
        blocks + 3,
        limit=WHOLE_LIMIT,
    )


def gather_near(along_z):
    return [along_z, swap_win(along_z, 1), swap_y(along_z)]


def gather_far(near, cut=0):
    if not cut:
        return [swap_win(near[2], 1)]
    return [swap_y(near[1][:cut]), swap_win(near[2][cut:], 1)]


PLACES = ((0, 0), (1, 0), (0, 1), (1, 1))


def piece(refs, number, k):
    if number < 3 or len(refs) == 4:
        return refs[number].at[k]
    cut = refs[3].shape[0]
    return refs[3].at[k] if k < cut else refs[4].at[k - cut]


def place_qkv(where, pieces):
    _, rows, columns = pieces[0].shape
    width = columns // 4

    def body(where, refs, copy, finish):
        z, x, y, c = where[0], where[1], where[2], where[3]
        for core in range(2):
            for n, (j, l) in enumerate(PLACES):
                for k in range(4):
                    source = piece(refs[4 * core : 4 * core + 4], n, k)
                    at = ((z ^ k) * 2 + (x ^ j), c ^ core, y ^ l)
                    copy([source.at[:, pl.ds(0, 3 * width)]], refs[8].at[at])
                    copy([source.at[:, pl.ds(3 * width, width)]], refs[9].at[at])
        finish()

    qkv, out = move_call(
        body,
        "place_qkv",
        where,
        pieces,
        [low_shape(8, 2, 2, rows, 3 * width), low_shape(8, 2, 2, rows, width)],
        64,
    )
    return qkv.reshape(32 * rows, 3 * width), out.reshape(32 * rows, width)


def place_up(where, pieces):
    _, rows, columns = pieces[0].shape

    def body(where, refs, copy, finish):
        z, x, y = where[0], where[1], where[2]
        for n, (j, l) in enumerate(PLACES):
            for k in range(4):
                copy([piece(refs[:4], n, k)], refs[4].at[(z ^ k) * 2 + (x ^ j), y ^ l])
        finish()

    return move_call(
        body, "place_up", where, pieces, [low_shape(8, 2, rows, columns)], 16
    )[0].reshape(16 * rows, columns)


def place_down(where, pieces):
    _, rows, columns = pieces[0].shape

    def body(where, refs, copy, finish):
        for n in range(4):
            for k in range(4):
                quarter = QUARTERS.index(PLACES[n])
                copy([piece(refs[:5], n, k)], refs[5].at[quarter, where[0] ^ k])
        finish()

    return move_call(
        body, "place_down", where, pieces, [low_shape(4, 4, rows, columns)], 16
    )[0].reshape(16 * rows, columns)


QUARTERS = ((1, 1), (1, 0), (0, 1), (0, 0))


FAR_CUT = 2
LAST_CUT = 1


def add_low(*terms):
    return functools.reduce(jnp.add, [term.astype(f32) for term in terms]).astype(bf16)


def block_specs(array, first, cut=0):
    if array.ndim == 4:
        return pl.BlockSpec((1, 1) + array.shape[2:], lambda i: (first, i, 0, 0))
    rows = array.shape[0] // (4 if first is None else first)
    last = array.shape[0] // rows - 1
    return pl.BlockSpec((rows, array.shape[1]), lambda i: (jnp.clip(i - cut, 0, last), 0))


def read(ref):
    return ref[...].reshape(ref.shape[-2:]).astype(f32)


def merge_kernel(counts, cut, *refs):
    x_terms, y_terms = refs[: counts[0]], refs[counts[0] : counts[0] + counts[1]]
    far_y, far_x, send_x, send_y = refs[-4:]
    first = pl.program_id(0) < cut
    to_x = functools.reduce(jnp.add, [read(ref) for ref in x_terms])
    to_y = functools.reduce(jnp.add, [read(ref) for ref in y_terms])
    send_x[...] = jnp.where(first, to_x + read(far_y), to_x).astype(bf16)
    send_y[...] = jnp.where(first, to_y, to_y + read(far_x)).astype(bf16)


def merge(x_terms, y_terms, far_y, far_x, cut=FAR_CUT):
    rows, width = far_y.shape[0] // cut, far_y.shape[1]
    block = pl.BlockSpec((rows, width), lambda i: (i, 0))
    return dense_call(
        functools.partial(merge_kernel, (len(x_terms), len(y_terms)), cut),
        "merge",
        (4,),
        [block_specs(*term) for term in list(x_terms) + list(y_terms)]
        + [block_specs(far_y, cut), block_specs(far_x, 4 - cut, cut)],
        [block, block],
        [low_shape(4 * rows, width)] * 2,
    )(*[term[0] for term in list(x_terms) + list(y_terms)], far_y, far_x)


def total_kernel(*refs):
    refs[-1][...] = functools.reduce(jnp.add, [read(ref) for ref in refs[:-1]]).astype(bf16)


def total(terms, rows, width):
    return dense_call(
        total_kernel,
        "total",
        (4,),
        [block_specs(*term) for term in terms],
        pl.BlockSpec((rows, width), lambda i: (i, 0)),
        low_shape(4 * rows, width),
    )(*[term[0] for term in terms])


def first_kernel(own_ref, got_ref, far_y, far_x, x_ref):
    far = own_ref[0].astype(f32) + got_ref[0].astype(f32)
    far_y[...] = far[:LAST_CUT].astype(bf16).reshape(far_y.shape)
    far_x[...] = far[LAST_CUT:].astype(bf16).reshape(far_x.shape)
    x_ref[...] = (own_ref[1].astype(f32) + got_ref[1].astype(f32)).astype(bf16).reshape(x_ref.shape)


def first_quarters(own, got):
    _, _, rows, width = own.shape
    shapes = [(LAST_CUT * rows, width), ((4 - LAST_CUT) * rows, width), (4 * rows, width)]
    return dense_call(
        first_kernel,
        "first_quarters",
        (1,),
        [full_spec(own.shape)] * 2,
        [full_spec(shape) for shape in shapes],
        [low_shape(*shape) for shape in shapes],
    )(own, got)


def parts_z(kept):
    return exchange_z(kept.reshape((4, kept.shape[0] // 4) + kept.shape[1:]))


def add_z(parts):
    return jnp.sum(parts.astype(f32), axis=0)


def sum_z_direct(kept, z):
    blocks = kept.reshape((4, kept.shape[0] // 4) + kept.shape[1:])
    sent = [swap_win(pick(blocks, z ^ k, 0), 2 * k) for k in (1, 2, 3)]
    return functools.reduce(jnp.add, [part.astype(f32) for part in [pick(blocks, z, 0)] + sent])


def scatter_plain(grad, where):
    mine = lax.psum_scatter(grad.astype(f32), "win", scatter_dimension=0, tiled=False)
    return pick(mine, where[2], 0) + swap_y(pick(mine, 1 - where[2], 0))


def windows_send(where, slots):
    def body(where, refs, copy, finish):
        for half in range(2):
            first = half * 8 + (1 - where[3]) * 4
            copy([refs[0].at[pl.ds(first, 4)]], refs[1].at[pl.ds(half * 4, 4)])
        finish()

    return move_call(body, "rows_send", where, [slots], [low_shape(8, *slots.shape[1:])], 2, limit=WHOLE_LIMIT)[0]


def windows_pack(where, slots, got):
    def body(where, refs, copy, finish):
        own, other, here, away = refs
        y, c = where[2], where[3]
        for target, half in ((here, y), (away, 1 - y)):
            for t in range(2):
                window = half * 4 + c * 2 + t
                mine, theirs = window * 2, half * 4 + t * 2
                copy([c == 0, own.at[mine], other.at[theirs]], target.at[t * 3])
                copy([c == 0, other.at[theirs], own.at[mine]], target.at[t * 3 + 1])
                copy(
                    [where[6 + window] == where[4], own.at[mine + 1], other.at[theirs + 1]],
                    target.at[t * 3 + 2],
                )
        finish()

    shape = low_shape(6, *slots.shape[1:])
    return move_call(body, "rows_pack", where, [slots, got], [shape, shape], 12)


def windows_join(where, here, away):
    def body(where, refs, copy, finish):
        here, away, out = refs
        y = where[2]
        for t in range(2):
            for slot in range(4):
                source = t * 3 + slot % 2
                copy([y == slot // 2, here.at[source], away.at[source]], out.at[t * 5 + slot])
            near = where[6 + where[4] * 2 + t] // 2 == y
            copy([near, here.at[t * 3 + 2], away.at[t * 3 + 2]], out.at[t * 5 + 4])
        finish()

    shape = low_shape(10, *here.shape[1:])
    out = move_call(body, "rows_join", where, [here, away], [shape], 10)[0]
    return out.reshape(10 * here.shape[1], here.shape[2])


def windows_back_pack(where, rows, back):
    def body(where, refs, copy, finish):
        rows, back, out = refs
        y, c = where[2], where[3]
        for t in range(2):
            here, there = y * 4 + t * 2, (1 - y) * 4 + t * 2
            copy([rows.at[t * 5 + 2 * y + 1 - c]], out.at[here])
            copy([rows.at[t * 5 + 4]], out.at[here + 1])
            copy([back.at[t * 3 + 1 - c]], out.at[there])
            copy([back.at[t * 3 + 2]], out.at[there + 1])
        finish()

    slots = rows.reshape(10, SPATIAL, rows.shape[1])
    shape = low_shape(8, SPATIAL, rows.shape[1])
    return move_call(body, "rows_back_pack", where, [slots, back], [shape], 8)[0]


def windows_back_join(where, rows, back, got, dead, dtype):
    width = rows.shape[1]

    def body(where, refs, copy, finish):
        rows, back, got, dead, out, arrived = refs
        y, c, frm, count = where[2], where[3], where[4], where[5]
        for half in range(2):
            side = y if half == 0 else 1 - y
            for core in range(2):
                for t in range(2):
                    window = side * 4 + (c if core == 0 else 1 - c) * 2 + t
                    if core == 1:
                        even, odd = got.at[side * 4 + t * 2], got.at[side * 4 + t * 2 + 1]
                    elif half == 0:
                        even, odd = rows.at[t * 5 + 2 * y + c], rows.at[t * 5 + 4]
                    else:
                        even, odd = back.at[t * 3 + c], back.at[t * 3 + 2]
                    live = window < count
                    place = window * 2
                    copy([live, even, dead.at[place]], arrived.at[place])
                    doubled = jnp.logical_and(live, where[6 + window] == frm)
                    copy([doubled, odd, dead.at[place + 1]], arrived.at[place + 1])
        finish()
        out[...] = arrived[...].astype(out.dtype)

    slots = rows.reshape(10, SPATIAL, width)
    out = move_call(
        body,
        "rows_back_join",
        where,
        [slots, back, got, dead.reshape(16, SPATIAL, width)],
        [jax.ShapeDtypeStruct((16, SPATIAL, width), dtype)],
        16,
        [pltpu.VMEM((16, SPATIAL, width), bf16)],
    )[0]
    return out.reshape(dead.shape)


GROUP = 4
LANES = GROUP * 64


def head_lanes(head):
    lanes = lax.broadcasted_iota(jnp.int32, (1, LANES), 1)
    return (lanes // 64) == head


def attend_kernel(q_ref, k_ref, v_ref, space_ref, time_ref, o_ref, p_ref):
    q, k, v = q_ref[...], k_ref[...], v_ref[...]
    rows = q.shape[0]
    total = jnp.zeros((rows, LANES), f32)
    for head in range(GROUP):
        lanes = head_lanes(head)
        scaled = jnp.where(lanes, q * jnp.asarray(0.125, bf16), jnp.zeros_like(q))
        scores = lax.dot_general(scaled, k, (((1,), (1,)), ((), ())), preferred_element_type=f32)
        shaped = scores.reshape(rows // SPATIAL, SPATIAL, rows)
        shaped = shaped + space_ref[head][None] + time_ref[0, head, : rows // SPATIAL][:, None, :]
        scores = shaped.reshape(rows, rows)
        grown = jnp.exp(scores - jnp.max(scores, axis=-1, keepdims=True))
        inverse = 1.0 / jnp.sum(grown, axis=-1, keepdims=True)
        probs = (grown * inverse).astype(bf16)
        p_ref[0, head] = probs
        masked = jnp.where(lanes, v, jnp.zeros_like(v))
        total = total + jnp.dot(probs, masked, preferred_element_type=f32)
    o_ref[...] = total.astype(bf16)


def attend_back_kernel(
    q_ref, k_ref, v_ref, do_ref, o_ref, p_ref, grad_ref, space_ref, time_ref
):
    q, k, v, do = q_ref[...], k_ref[...], v_ref[...], do_ref[...]
    rows = q.shape[0]
    slots = rows // SPATIAL
    product = do.astype(f32) * o_ref[...].astype(f32)
    grad_q = jnp.zeros((rows, LANES), f32)
    grad_k = jnp.zeros((rows, LANES), f32)
    grad_v = jnp.zeros((rows, LANES), f32)

    @pl.when(pl.program_id(1) == 0)
    def _():
        space_ref[...] = jnp.zeros_like(space_ref)

    for head in range(GROUP):
        lanes = head_lanes(head)
        none = jnp.zeros_like(q)
        scale = jnp.asarray(0.125, bf16)
        row_dot = jnp.sum(jnp.where(lanes, product, 0.0), axis=-1, keepdims=True)
        grads = jnp.where(lanes, do, none)
        probs = p_ref[0, head]
        grad_probs = lax.dot_general(
            grads, v, (((1,), (1,)), ((), ())), preferred_element_type=f32
        )
        grad_scores = probs.astype(f32) * (grad_probs - row_dot)
        low = grad_scores.astype(bf16)
        over_rows = (((0,), (0,)), ((), ()))
        grad_v = grad_v + lax.dot_general(probs, grads, over_rows, preferred_element_type=f32)
        grad_k = grad_k + lax.dot_general(
            low, jnp.where(lanes, q * scale, none), over_rows, preferred_element_type=f32
        )
        grad_q = grad_q + jnp.dot(
            low, jnp.where(lanes, k * scale, none), preferred_element_type=f32
        )
        shaped = grad_scores.reshape(slots, SPATIAL, rows)
        space_ref[head] += jnp.sum(shaped, axis=0)
        time_ref[0, head, :slots] = jnp.sum(shaped, axis=1)
    grad_ref[0] = grad_q.astype(bf16)
    grad_ref[1] = grad_k.astype(bf16)
    grad_ref[2] = grad_v.astype(bf16)


def attention_specs(rows, groups):
    q_spec = pl.BlockSpec((rows, LANES), lambda group, window: (window, group))
    k_spec = pl.BlockSpec((rows, LANES), lambda group, window: (window, group + groups))
    v_spec = pl.BlockSpec((rows, LANES), lambda group, window: (window, group + 2 * groups))
    p_spec = pl.BlockSpec((1, GROUP, rows, rows), lambda group, window: (window, group, 0, 0))
    space_spec = pl.BlockSpec((GROUP, SPATIAL, rows), lambda group, window: (group, 0, 0))
    time_spec = pl.BlockSpec((1, GROUP, 8, rows), lambda group, window: (window, group, 0, 0))
    return q_spec, k_spec, v_spec, p_spec, space_spec, time_spec


def attend(projected, space_bias, time_bias, windows):
    rows = projected.shape[0] // windows
    heads = space_bias.shape[0]
    q_spec, k_spec, v_spec, p_spec, space_spec, time_spec = attention_specs(rows, heads // GROUP)
    width = heads * 64
    return pl.pallas_call(
        attend_kernel,
        grid=(heads // GROUP, windows),
        in_specs=[q_spec, k_spec, v_spec, space_spec, time_spec],
        out_specs=[q_spec, p_spec],
        out_shape=[
            pltpu.HBM((windows * rows, width), bf16),
            pltpu.HBM((windows, heads, rows, rows), bf16),
        ],
        compiler_params=pltpu.CompilerParams(vmem_limit_bytes=VMEM_LIMIT),
        cost_estimate=SMALL,
        name="attend",
    )(projected, projected, projected, space_bias, time_bias)


def attend_back(projected, grad_attended, attended, probs, windows):
    heads, rows = probs.shape[1], probs.shape[2]
    q_spec, k_spec, v_spec, p_spec, space_spec, time_spec = attention_specs(rows, heads // GROUP)
    width = heads * 64
    return pl.pallas_call(
        attend_back_kernel,
        grid=(heads // GROUP, windows),
        in_specs=[q_spec, k_spec, v_spec, q_spec, q_spec, p_spec],
        out_specs=[
            pl.BlockSpec((3, rows, LANES), lambda group, window: (0, window, group)),
            space_spec,
            time_spec,
        ],
        out_shape=[
            pltpu.HBM((3, windows * rows, width), bf16),
            pltpu.HBM((heads, SPATIAL, rows), f32),
            pltpu.HBM((windows, heads, 8, rows), f32),
        ],
        compiler_params=pltpu.CompilerParams(vmem_limit_bytes=VMEM_LIMIT),
        cost_estimate=SMALL,
        name="attend_back",
    )(projected, projected, projected, grad_attended, attended, probs)


def full_spec(shape):
    return pl.BlockSpec(shape, lambda *_: (0,) * len(shape))


def in_hbm(shapes):
    if isinstance(shapes, list):
        return [in_hbm(shape) for shape in shapes]
    return pltpu.HBM(shapes.shape, shapes.dtype)


def dense_call(kernel, name, grid, in_specs, out_specs, out_shape, scratch=()):
    return pl.pallas_call(
        kernel,
        grid=grid,
        in_specs=in_specs,
        out_specs=out_specs,
        out_shape=in_hbm(out_shape),
        scratch_shapes=list(scratch),
        compiler_params=pltpu.CompilerParams(vmem_limit_bytes=VMEM_LIMIT),
        cost_estimate=SMALL,
        name=name,
    )


def normalize(values_in):
    centred = values_in - jnp.mean(values_in, axis=-1, keepdims=True)
    inverse = lax.rsqrt(jnp.mean(centred * centred, axis=-1, keepdims=True) + EPS)
    return centred * inverse, inverse


def normalize_back(grad_normed, normed, inverse):
    return inverse * (
        grad_normed
        - jnp.mean(grad_normed, axis=-1, keepdims=True)
        - normed * jnp.mean(grad_normed * normed, axis=-1, keepdims=True)
    )


def dot32(left, right, dims):
    return lax.dot_general(left, right, (dims, ((), ())), preferred_element_type=f32)


def modulation(mod_ref, number, window=0):
    width = mod_ref.shape[2] // 6
    return mod_ref[window, :, number * width : (number + 1) * width]


PLAIN = ((1,), (0,))
RIGHT_T = ((1,), (1,))
LEFT_T = ((0,), (0,))


def qkv_kernel(tokens_ref, mod_ref, w_ref, projected_ref, hidden_ref):
    local = mod_ref.shape[0]
    rows = tokens_ref.shape[0] // local

    @pl.when(pl.program_id(0) == 0)
    def _():
        for window in range(local):
            part = pl.ds(window * rows, rows)
            normed, _ = normalize(tokens_ref[part, :].astype(f32))
            shift, scale = modulation(mod_ref, 0, window), modulation(mod_ref, 1, window)
            hidden_ref[part, :] = (normed * (1.0 + scale) + shift).astype(bf16)

    projected_ref[...] = dot32(hidden_ref[...], w_ref[...], PLAIN).astype(bf16)


def qkv_forward(tokens, mod, w_attn):
    count, width = tokens.shape
    tile = 512
    return dense_call(
        qkv_kernel,
        "qkv",
        (3 * width // tile,),
        [
            full_spec(tokens.shape),
            full_spec(mod.shape),
            pl.BlockSpec((width, tile), lambda i: (0, i)),
        ],
        [pl.BlockSpec((count, tile), lambda i: (0, i)), full_spec(tokens.shape)],
        [jax.ShapeDtypeStruct((count, 3 * width), bf16), jax.ShapeDtypeStruct((count, width), bf16)],
    )(tokens, mod, w_attn)


def out_kernel(attended_ref, w_ref, tokens_ref, mod_ref, branch_ref, mid_ref, hidden_ref):
    branch = dot32(attended_ref[...], w_ref[...], PLAIN)
    mid = tokens_ref[...].astype(f32) + modulation(mod_ref, 2) * branch
    normed, _ = normalize(mid)
    branch_ref[...] = branch.astype(bf16)
    mid_ref[...] = mid
    hidden_ref[...] = (normed * (1.0 + modulation(mod_ref, 4)) + modulation(mod_ref, 3)).astype(bf16)


def out_forward(attended, w_attn, tokens, mod):
    count, width = tokens.shape
    local = mod.shape[0]
    rows = count // local
    row_spec = pl.BlockSpec((rows, width), lambda i: (i, 0))
    return dense_call(
        out_kernel,
        "attn_out",
        (local,),
        [
            row_spec,
            full_spec((width, width)),
            row_spec,
            pl.BlockSpec((1,) + mod.shape[1:], lambda i: (i, 0, 0)),
        ],
        [row_spec] * 3,
        [
            jax.ShapeDtypeStruct((count, width), bf16),
            jax.ShapeDtypeStruct((count, width), f32),
            jax.ShapeDtypeStruct((count, width), bf16),
        ],
    )(attended, w_attn, tokens, mod)


def gelu_parts(value):
    factor = 0.7978845608028654
    square = value * value
    half = 0.5 + 0.5 * jnp.tanh(value * (factor + (factor * 0.044715) * square))
    gelu = value * half
    slope = half + gelu * (1.0 - half) * (2.0 * factor + (6.0 * factor * 0.044715) * square)
    return gelu, slope


def joined(refs, axis):
    parts = [ref[...] for ref in refs]
    return parts[0] if len(parts) == 1 else jnp.concatenate(parts, axis=axis)


def hidden_specs(width, tile, part, fast, rows):
    if not fast:
        return [pl.BlockSpec((rows, tile), lambda i, where: (0, 2 * part + i))]

    def block(z):
        def index(i, where):
            j, l = 1 - part, 1 - i
            return 0, z * 4 + (where[1] ^ j) * 2 + (where[2] ^ l)

        return pl.BlockSpec((rows, tile // 4), index)

    return [block(z) for z in range(4)]


def held_spec(shape):
    return pl.BlockSpec(shape, lambda i, where: (0,) * len(shape))


def hidden_call(kernel, name, where, inputs, in_specs, out_specs, out_shape, scratch=()):
    return pl.pallas_call(
        kernel,
        grid_spec=pltpu.PrefetchScalarGridSpec(
            num_scalar_prefetch=1,
            grid=(2,),
            in_specs=in_specs,
            out_specs=out_specs,
            scratch_shapes=list(scratch),
        ),
        out_shape=in_hbm(out_shape),
        compiler_params=pltpu.CompilerParams(vmem_limit_bytes=VMEM_LIMIT),
        cost_estimate=SMALL,
        name=name,
    )(where, *inputs)


def write_quarters(refs, value):
    @pl.when(pl.program_id(0) == 0)
    def _():
        start = 0
        for ref in refs[:-1]:
            ref[...] = value[start : start + ref.shape[0]].astype(bf16)
            start += ref.shape[0]

    @pl.when(pl.program_id(0) == 1)
    def _():
        refs[-1][...] = value.astype(bf16)


def quarter_shapes(tile, width, part):
    cut = FAR_CUT * tile // 4
    return [(tile, width)] * 2 if part else [(cut, width), (tile - cut, width), (tile, width)]


def up_kernel(pieces, where_ref, own_ref, other_ref, mlp_ref, mlp_other_ref, *refs):
    w, bias = joined(refs[:pieces], 1), joined(refs[pieces : 2 * pieces], 1)
    act_ref, slope_ref = refs[2 * pieces : 2 * pieces + 2]
    grad_refs = refs[2 * pieces + 2 :]
    total = None
    for half, (hidden, mlp) in enumerate(((own_ref, mlp_ref), (other_ref, mlp_other_ref))):
        activated, slope = gelu_parts(dot32(hidden[...], w, PLAIN) + bias)
        activated = activated.astype(bf16)
        act_ref[half] = activated
        slope_ref[half] = slope.astype(bf16)
        part = dot32(activated, mlp[...], LEFT_T)
        total = part if total is None else total + part
    write_quarters(grad_refs, total)


def up_forward(where, rows_both, w_up, bias, part, fast):
    count, width = rows_both[0].shape
    inner = w_up.shape[1]
    tile = inner // 4
    both = pl.BlockSpec((2, count, tile), lambda i, where: (0, 0, i))
    w_specs = hidden_specs(width, tile, part, fast, width)
    bias_specs = hidden_specs(width, tile, part, fast, 1)
    pieces = len(w_specs)
    return hidden_call(
        functools.partial(up_kernel, pieces),
        "mlp_up",
        where,
        list(rows_both) + [w_up] * pieces + [bias] * pieces,
        [held_spec((count, width))] * 4 + w_specs + bias_specs,
        [both, both] + [held_spec(shape) for shape in quarter_shapes(tile, width, part)],
        [low_shape(2, count, 2 * tile)] * 2
        + [low_shape(*shape) for shape in quarter_shapes(tile, width, part)],
    )


def down_back_kernel(pieces, part, where_ref, own_ref, other_ref, mlp_ref, mlp_other_ref, down_ref, *refs):
    up = joined(refs[:pieces], 1)
    slope_ref = refs[pieces]
    refs = refs[pieces + 1 :]
    earlier_ref = refs[0] if part else None
    outs = refs[1:] if part else refs
    quarters = 2 if part else 3
    grad_refs, bias_ref = outs[:quarters], outs[quarters]
    back_refs, total_ref = outs[quarters + 1 : -1], outs[-1]
    step = pl.program_id(0)
    down = down_ref[...]
    total, sums = None, None
    for half, (hidden, mlp) in enumerate(((own_ref, mlp_ref), (other_ref, mlp_other_ref))):
        grad_pre = dot32(mlp[...], down, RIGHT_T) * slope_ref[half].astype(f32)
        column = jnp.sum(grad_pre, axis=0, keepdims=True)
        grad_pre = grad_pre.astype(bf16)
        add = dot32(grad_pre, hidden[...], LEFT_T)
        total = add if total is None else total + add
        sums = column if sums is None else sums + column
        back = dot32(grad_pre, up, RIGHT_T)

        @pl.when(step == 0)
        def _(half=half, back=back):
            total_ref[half] = back + earlier_ref[half].astype(f32) if part else back

        @pl.when(step > 0)
        def _(half=half, back=back):
            total_ref[half] += back

    bias_ref[...] = sums
    write_quarters(grad_refs, total)

    @pl.when(step == 1)
    def _():
        if part:
            back_refs[0][...] = total_ref[0]
            back_refs[1][...] = total_ref[1].astype(bf16)
        else:
            back_refs[0][...] = total_ref[...].astype(bf16)


def down_backward(where, rows_both, w_down, w_up, slope, part, earlier, fast):
    count, width = rows_both[0].shape
    inner = w_up.shape[1]
    tile = inner // 4
    back_shape = (2, count, width)
    if part:
        back_specs = [held_spec((count, width))] * 2
        back_shapes = [jax.ShapeDtypeStruct((count, width), f32), low_shape(count, width)]
    else:
        back_specs = [held_spec(back_shape)]
        back_shapes = [low_shape(*back_shape)]
    w_specs = hidden_specs(width, tile, part, fast, width)
    pieces = len(w_specs)
    return hidden_call(
        functools.partial(down_back_kernel, pieces, part),
        "mlp_back",
        where,
        list(rows_both) + [w_down] + [w_up] * pieces + [slope] + ([earlier] if part else []),
        [held_spec((count, width))] * 4
        + [pl.BlockSpec((tile, width), lambda i, where: (2 * part + i, 0))]
        + w_specs
        + [pl.BlockSpec((2, count, tile), lambda i, where: (0, 0, i))]
        + ([held_spec(back_shape)] if part else []),
        [held_spec(shape) for shape in quarter_shapes(tile, width, part)]
        + [pl.BlockSpec((1, tile), lambda i, where: (0, i))]
        + back_specs,
        [low_shape(*shape) for shape in quarter_shapes(tile, width, part)]
        + [jax.ShapeDtypeStruct((1, 2 * tile), f32)]
        + back_shapes,
        [pltpu.VMEM(back_shape, f32)],
    )


def down_kernel(first_ref, second_ref, w_ref, own_ref, other_ref):
    half = first_ref.shape[2]
    for number, out_ref in enumerate((own_ref, other_ref)):
        total = dot32(first_ref[number], w_ref[:half], PLAIN)
        total = total + dot32(second_ref[number], w_ref[half:], PLAIN)
        out_ref[...] = total.astype(out_ref.dtype)


def down_forward(first, second, w_down):
    _, count, half = first.shape
    width = w_down.shape[1]
    tile = 256
    row_spec = pl.BlockSpec((count, tile), lambda i: (0, i))
    return dense_call(
        down_kernel,
        "mlp_down",
        (width // tile,),
        [full_spec(first.shape)] * 2 + [pl.BlockSpec((2 * half, tile), lambda i: (0, i))],
        [row_spec, row_spec],
        [jax.ShapeDtypeStruct((count, width), f32), low_shape(count, width)],
    )(first, second, w_down)


def split_away(where_ref, rows_ref, away_ref):
    first = pl.multiple_of((1 - where_ref[2]) * 2 * SPATIAL, 2 * SPATIAL)
    away_ref[: 2 * SPATIAL] = rows_ref[pl.ds(first, 2 * SPATIAL), :]
    away_ref[2 * SPATIAL :] = rows_ref[4 * SPATIAL :, :]


def result_kernel(
    where_ref, own_ref, other_ref, bias_ref, mid_ref, cot_ref, mod_ref, live_ref,
    result_ref, away_ref, gate_ref,
):
    branch = own_ref[...] + other_ref[...].astype(f32) + bias_ref[...]
    result_ref[...] = (mid_ref[...] + modulation(mod_ref, 5) * branch).astype(bf16)
    split_away(where_ref, result_ref, away_ref)
    gate_ref[0] = live_ref[0] * jnp.sum(branch * cot_ref[...].astype(f32), axis=0, keepdims=True)


def result_forward(where, own, other, bias, mid, cotangent, mod, live):
    count, width = own.shape
    local = mod.shape[0]
    row_spec = pl.BlockSpec((count // local, width), lambda i: (i, 0))
    one = pl.BlockSpec((1, 1, width), lambda i: (i, 0, 0))
    return dense_call(
        result_kernel,
        "result",
        (local,),
        [pl.BlockSpec(memory_space=pltpu.SMEM)]
        + [row_spec, row_spec, full_spec(bias.shape), row_spec, row_spec]
        + [pl.BlockSpec((1,) + mod.shape[1:], lambda i: (i, 0, 0)), one],
        [row_spec, pl.BlockSpec((3 * SPATIAL, width), lambda i: (i, 0)), one],
        [
            low_shape(count, width),
            low_shape(local * 3 * SPATIAL, width),
            jax.ShapeDtypeStruct((local, 1, width), f32),
        ],
    )(where, own, other, bias, mid, cotangent, mod, live)


def mid_back_kernel(
    own_ref, other_ref, mid_ref, cot_ref, branch_ref, attended_ref, w_ref, mod_ref, live_ref,
    grad_mid_ref, grad_attended_ref, sums_ref, grad_ref, total_ref,
):
    step, last = pl.program_id(0), pl.num_programs(0) - 1
    grad_hidden = own_ref[...] + other_ref[...].astype(f32)
    normed, inverse = normalize(mid_ref[...])
    back = normalize_back(grad_hidden * (1.0 + modulation(mod_ref, 4)), normed, inverse)
    grad_mid = cot_ref[...].astype(f32) + back
    grad_mid_ref[...] = grad_mid
    gate = jnp.sum(branch_ref[...].astype(f32) * grad_mid, axis=0, keepdims=True)
    sums_ref[0, 0:1] = live_ref[0] * gate
    sums_ref[0, 1:2] = jnp.sum(grad_hidden, axis=0, keepdims=True)
    sums_ref[0, 2:3] = jnp.sum(grad_hidden * normed, axis=0, keepdims=True)
    grad_branch = (modulation(mod_ref, 2) * grad_mid).astype(bf16)
    grad_attended_ref[...] = dot32(grad_branch, w_ref[...], RIGHT_T).astype(bf16)
    part = dot32(grad_branch, attended_ref[...], LEFT_T)

    @pl.when(step == 0)
    def _():
        total_ref[...] = part

    @pl.when(step > 0)
    def _():
        total_ref[...] += part

    @pl.when(step == last)
    def _():
        grad_ref[...] = total_ref[...].astype(bf16)


def mid_backward(own, other, mid, cotangent, branch, attended, w_attn, mod, live):
    count, width = own.shape
    local = mod.shape[0]
    row_spec = pl.BlockSpec((count // local, width), lambda i: (i, 0))
    return dense_call(
        mid_back_kernel,
        "mid_back",
        (local,),
        [row_spec] * 6
        + [
            full_spec((width, width)),
            pl.BlockSpec((1,) + mod.shape[1:], lambda i: (i, 0, 0)),
            pl.BlockSpec((1, 1, width), lambda i: (i, 0, 0)),
        ],
        [
            row_spec,
            row_spec,
            pl.BlockSpec((1, 8, width), lambda i: (i, 0, 0)),
            full_spec((width, width)),
        ],
        [
            jax.ShapeDtypeStruct((count, width), f32),
            jax.ShapeDtypeStruct((count, width), bf16),
            jax.ShapeDtypeStruct((local, 8, width), f32),
            jax.ShapeDtypeStruct((width, width), bf16),
        ],
        [pltpu.VMEM((width, width), f32)],
    )(own, other, mid, cotangent, branch, attended, w_attn, mod, live)


def grad_pieces(tiles, tile, width):
    block, out_block = tiles * tile // 32, width // 32
    pieces = []
    for number in range(32):
        pieces.append((0, number, None, number * out_block, block, out_block))
        first, rest, to = number * block, block, 0
        while rest:
            size = min(rest, tile - first % tile)
            pieces.append((first // tile, number, first // tile, first % tile, to, size))
            first, rest, to = first + size, rest - size, to + size
    return pieces


def qkv_grad_kernel(pieces, where_ref, grad_ref, hidden_ref, out_grad_ref, *refs):
    outs, whole_ref, sems = refs[:4], refs[4], refs[5]
    x, y, c = where_ref[1], where_ref[2], where_ref[3]
    step, steps = pl.program_id(0), pl.num_programs(0)
    whole_ref[step] = dot32(grad_ref[0], hidden_ref[...], LEFT_T).astype(bf16)

    for now in range(whole_ref.shape[0]):
        for here_x in range(2):
            for here_c in range(2):

                @pl.when((step == now) & (x == here_x) & (c == here_c))
                def _(now=now, here_x=here_x, here_c=here_c):
                    for count, (ready, number, tile, first, start, size) in enumerate(pieces):
                        if ready != now:
                            continue
                        z, l = number // 8, (number // 2 % 2) ^ y
                        j, core = (number // 4 % 2) ^ here_x, (number % 2) ^ here_c
                        rows = pl.ds(first, size)
                        source = out_grad_ref.at[rows] if tile is None else whole_ref.at[tile, rows]
                        place = outs[2 * core + 1 - j].at[1 - l, z, pl.ds(start, size)]
                        pltpu.make_async_copy(source, place, sems.at[count]).start()

    @pl.when(step == steps - 1)
    def _():
        for count, piece in enumerate(pieces):
            place = outs[0].at[0, 0, pl.ds(0, piece[5])]
            pltpu.make_async_copy(place, place, sems.at[count]).wait()


def qkv_grad(where, grad_projected, hidden, grad_out):
    count, width = hidden.shape
    tile = 512
    per = width // tile
    rows = 4 * width // 32
    shape = low_shape(2, 4, rows, width)
    pieces = grad_pieces(3 * per, tile, width)
    return pl.pallas_call(
        functools.partial(qkv_grad_kernel, pieces),
        grid=(3 * per,),
        in_specs=[
            pl.BlockSpec(memory_space=pltpu.SMEM),
            pl.BlockSpec((1, count, tile), lambda i: (i // per, 0, i % per)),
            full_spec(hidden.shape),
            full_spec(grad_out.shape),
        ],
        out_specs=[pl.BlockSpec(memory_space=pl.ANY)] * 4,
        out_shape=[shape] * 4,
        scratch_shapes=[
            pltpu.VMEM((3 * per, tile, width), bf16),
            pltpu.SemaphoreType.DMA((len(pieces),)),
        ],
        compiler_params=pltpu.CompilerParams(vmem_limit_bytes=VMEM_LIMIT),
        cost_estimate=SMALL,
        name="qkv_grad",
    )(where, grad_projected, hidden, grad_out)


def qkv_grad_plain(grad_projected, hidden):
    return lax.dot_general(
        grad_projected, hidden, (((1,), (0,)), ((), ())), preferred_element_type=f32
    ).astype(bf16)


def tokens_back_kernel(
    where_ref, grad_ref, w_ref, tokens_ref, grad_mid_ref, mod_ref, out_ref, away_ref, sums_ref
):
    width = tokens_ref.shape[1]
    grad_hidden = None
    for part in range(3):
        add = dot32(grad_ref[part], w_ref[:, part * width : (part + 1) * width], RIGHT_T)
        grad_hidden = add if grad_hidden is None else grad_hidden + add
    normed, inverse = normalize(tokens_ref[...].astype(f32))
    back = normalize_back(grad_hidden * (1.0 + modulation(mod_ref, 1)), normed, inverse)
    out_ref[...] = (grad_mid_ref[...] + back).astype(bf16)
    split_away(where_ref, out_ref, away_ref)
    sums_ref[0, 0:1] = jnp.sum(grad_hidden, axis=0, keepdims=True)
    sums_ref[0, 1:2] = jnp.sum(grad_hidden * normed, axis=0, keepdims=True)


def tokens_backward(where, grad_projected, w_qkv, tokens, grad_mid, mod):
    count, width = tokens.shape
    local = mod.shape[0]
    rows = count // local
    row_spec = pl.BlockSpec((rows, width), lambda i: (i, 0))
    return dense_call(
        tokens_back_kernel,
        "tokens_back",
        (local,),
        [
            pl.BlockSpec(memory_space=pltpu.SMEM),
            pl.BlockSpec((3, rows, width), lambda i: (0, i, 0)),
            full_spec((width, 3 * width)),
            row_spec,
            row_spec,
            pl.BlockSpec((1,) + mod.shape[1:], lambda i: (i, 0, 0)),
        ],
        [
            row_spec,
            pl.BlockSpec((3 * SPATIAL, width), lambda i: (i, 0)),
            pl.BlockSpec((1, 8, width), lambda i: (i, 0, 0)),
        ],
        [
            low_shape(count, width),
            low_shape(local * 3 * SPATIAL, width),
            jax.ShapeDtypeStruct((local, 8, width), f32),
        ],
    )(where, grad_projected, w_qkv, tokens, grad_mid, mod)


def modulation_kernel(parts_ref, bias_ref, live_ref, out_ref):
    sources, holders, local, part = parts_ref.shape
    width = out_ref.shape[2] // 6
    for window in range(local):
        for holder in range(holders):
            total = parts_ref[0, holder, window : window + 1]
            for source in range(1, sources):
                total = total + parts_ref[source, holder, window : window + 1]
            columns = slice(holder * part, (holder + 1) * part)
            out_ref[window, :, columns] = total + bias_ref[:, columns]
        for gate in (2, 5):
            columns = slice(gate * width, (gate + 1) * width)
            out_ref[window, :, columns] = out_ref[window, :, columns] * live_ref[window]


def modulate(parts, bias, live):
    local, _, width = live.shape
    return dense_call(
        modulation_kernel,
        "modulation",
        (1,),
        [full_spec(parts.shape), full_spec(bias.shape), full_spec(live.shape)],
        full_spec((local, 1, 6 * width)),
        jax.ShapeDtypeStruct((local, 1, 6 * width), f32),
    )(parts, bias, live)


def gated_kernel(where_ref, rows_ref, mod_ref, out_ref):
    out_ref[...] = (modulation(mod_ref, 5) * rows_ref[...].astype(f32)).astype(bf16)


def gated(where, rows, mod):
    count, width = rows.shape
    local = mod.shape[0]
    row_spec = pl.BlockSpec((count // local, width), lambda i: (i, 0))
    return dense_call(
        gated_kernel,
        "gated",
        (local,),
        [
            pl.BlockSpec(memory_space=pltpu.SMEM),
            row_spec,
            pl.BlockSpec((1,) + mod.shape[1:], lambda i: (i, 0, 0)),
        ],
        row_spec,
        low_shape(count, width),
    )(where, rows, mod)


def space_onehot():
    places = jnp.arange(SPATIAL, dtype=jnp.int32)
    across, along = places // SIDE, places % SIDE
    index = (across[:, None] - across[None, :] + SIDE - 1) * (2 * SIDE - 1) + (
        along[:, None] - along[None, :] + SIDE - 1
    )
    ids = jnp.arange((2 * SIDE - 1) ** 2, dtype=jnp.int32)
    return (index.reshape(-1)[:, None] == ids[None, :]).astype(f32)


def on_device(
    tokens,
    condition,
    doubled,
    window_count,
    w_ada,
    b_ada,
    w_qkv,
    w_out,
    w_up,
    b_up,
    w_down,
    b_down,
    table_space,
    table_time,
    cotangent,
):
    windows, _, width = tokens.shape
    heads = table_space.shape[0]
    n_win = lax.axis_size("win")
    devices = n_win * 4
    win = lax.axis_index("win")
    frm = lax.axis_index("frm")
    z, x, y, c = win // 2, win % 2, frm // 2, frm % 2
    where = jnp.concatenate([jnp.stack([z, x, y, c, frm, window_count[0]]), doubled])
    where = where.astype(jnp.int32)
    local = windows // 4
    count = local * FRAMES * SPATIAL
    ff = w_up.shape[1]
    ff_block = ff // devices
    shard_rows = w_qkv.shape[0]
    half_width = width // 2
    fast = n_win == 8
    slot_shape = (2 * windows, SPATIAL, width)

    tok_slots, cot_slots = tokens.reshape(slot_shape), cotangent.reshape(slot_shape)
    tok_send = windows_send(where, tok_slots)
    biases = jnp.concatenate([b_ada, b_up, b_down])
    bias_rows = -(-biases.shape[0] // width)
    biases = jnp.pad(biases, (0, bias_rows * width - biases.shape[0])).reshape(bias_rows, width)
    small = jnp.concatenate([condition, biases])
    if fast:
        q_half, up_half, down_half = halves(where, w_qkv, w_out, w_up, w_down)
        q_direct = gather_z_direct(q_half)
        tok_send, _ = sync(tok_send, q_half)
        small, _ = sync(small, tok_send)
    small_all = lax.all_to_all(
        jnp.broadcast_to(small[None], (n_win,) + small.shape),
        "win",
        split_axis=0,
        concat_axis=0,
        tiled=True,
    )
    tok_got = swap_core(tok_send)
    tok_here, tok_away = windows_pack(where, tok_slots, tok_got)
    tok_back = swap_y(tok_away)

    onehot_space = space_onehot()
    space_bias = jnp.dot(table_space, onehot_space.T, precision=exact_mode)
    space_bias = jnp.tile(space_bias.reshape(heads, SPATIAL, SPATIAL), (1, 1, FRAMES))
    mine_doubled = lax.dynamic_slice_in_dim(doubled, frm * local, local, 0)
    holders = jnp.arange(4, dtype=jnp.int32)
    frames = holders[None, :] + (holders[None, :] > mine_doubled[:, None]).astype(jnp.int32)
    frames = jnp.concatenate([frames, mine_doubled[:, None] + 1], axis=1)
    offset = frames[:, :, None] - frames[:, None, :] + FRAMES - 1
    onehot_time = (
        offset[..., None] == jnp.arange(table_time.shape[1], dtype=jnp.int32)
    ).astype(f32)
    time_bias = jnp.einsum("wabt,ht->whab", onehot_time, table_time, precision=exact_mode)
    time_bias = jnp.repeat(time_bias, SPATIAL, axis=-1)
    time_bias = jnp.pad(time_bias, ((0, 0), (0, 0), (0, 8 - FRAMES), (0, 0)))

    if fast:
        *q_direct, _ = sync(*q_direct, tok_away)
        q_stack = jnp.stack(q_direct)
        q_near = gather_near(q_stack)
        small_all, up_half, _ = sync(small_all, up_half, q_stack)
        up_direct = gather_z_direct(up_half)

    cond_all = small_all[:, :windows].reshape(n_win * windows, width).astype(f32)
    bias_all = small_all[:, windows:].reshape(n_win, bias_rows * width).astype(f32)
    cuts = [b_ada.shape[0], b_ada.shape[0] + b_up.shape[0]]
    ada_bias = bias_all[:, : cuts[0]].reshape(1, 6 * width)
    up_bias = bias_all[:, cuts[0] : cuts[1]].reshape(n_win * 2, 2, ff_block)
    up_bias = pick(up_bias, c, 1).reshape(1, ff // 2)
    down_bias = bias_all[:, cuts[1] : cuts[1] + b_down.shape[0]].reshape(1, width)
    silu_all = jax.nn.silu(cond_all).astype(bf16)
    silu_part = lax.dynamic_slice_in_dim(silu_all, win * shard_rows, shard_rows, 1)
    ada_quarter = 6 * width // 4
    ada_part = lax.dynamic_slice_in_dim(w_ada, frm * ada_quarter, ada_quarter, 1)
    mod_part = dot32(silu_part, ada_part, PLAIN)
    if fast:
        *q_near, mod_part, up_bias, down_bias, space_bias, time_bias = sync(
            *q_near, mod_part, up_bias, down_bias, space_bias, time_bias
        )
        q_far = gather_far(q_near)
        *up_direct, q_near[0], q_near[1], q_near[2] = sync(*up_direct, *q_near)
        q_other = [swap_core(part) for part in q_near]
    else:
        qkv_full = lax.all_gather(w_qkv, "win", axis=0).reshape(width, 3 * width)
        out_full = lax.all_gather(w_out, "win", axis=0).reshape(width, width)
        up_shard = pick(w_up.reshape(shard_rows, n_win * 2, 2, ff_block), c, 2)
        up_full = lax.all_gather(up_shard, "win", axis=0).reshape(width, ff // 2)
        down_shard = pick(w_down.reshape(2, 2, ff_block, width), c, 1)
        down_full = lax.all_gather(down_shard, "win", axis=0).reshape(ff // 2, width)
    mod_parts = exchange_all(mod_part.reshape(devices, local, ada_quarter))
    my_window = frm * local + jnp.arange(local, dtype=jnp.int32)
    live = (my_window < window_count[0]).astype(f32)[:, None, None]
    live = jnp.broadcast_to(live, (local, 1, width))
    cot_send = windows_send(where, cot_slots)
    if fast:
        up_stack = jnp.stack(up_direct)
        q_far[0], tok_back, mod_parts, cot_send, up_stack, *q_other = sync(
            q_far[0], tok_back, mod_parts, cot_send, up_stack, *q_other
        )
        q_other = q_other + [swap_core(part) for part in q_far]
        up_near = gather_near(up_stack)
        qkv_full, out_full = place_qkv(where, list(q_near) + list(q_far) + q_other)
    cot_got = swap_core(cot_send)
    token_rows = windows_join(where, tok_here, tok_back)
    mod = modulate(mod_parts.reshape(n_win, 4, local, ada_quarter), ada_bias, live)

    projected, hidden_one = qkv_forward(token_rows, mod, qkv_full)
    cot_here, cot_away = windows_pack(where, cot_slots, cot_got)
    if fast:
        projected, cot_away, down_half, *up_near = sync(
            projected, cot_away, down_half, *up_near
        )
        up_far = gather_far(up_near)
        down_direct = gather_z_direct(down_half)
    cot_back = swap_y(cot_away)
    attended, probs = attend(projected, space_bias, time_bias, local)
    if fast:
        attended, cot_back, up_far[0], *down_direct = sync(
            attended, cot_back, up_far[0], *down_direct
        )
        down_near = gather_near(jnp.stack(down_direct))
    branch_attn, mid, hidden_two = out_forward(attended, out_full, token_rows, mod)
    grad_out = windows_join(where, cot_here, cot_back)
    grad_mlp = gated(where, grad_out, mod)
    mlp_other = swap_core(grad_mlp)

    hidden_other = swap_core(hidden_two)
    if fast:
        up_full = place_up(where, list(up_near) + list(up_far))
    rows_both = (hidden_two, hidden_other, grad_mlp, mlp_other)
    act_first, slope_first, *down_grads = up_forward(where, rows_both, up_full, up_bias, 0, fast)
    if fast:
        act_first, up_bias, *down_near = sync(act_first, up_bias, *down_near)
        down_far = gather_far(down_near, FAR_CUT)
    act_second, slope_second, *more = up_forward(where, rows_both, up_full, up_bias, 1, fast)
    if fast:
        act_second, *down_far = sync(act_second, *down_far)
        down_fy, down_fx = swap_y(down_grads[0]), swap_win(down_grads[1], 1)
        down_full = place_down(where, list(down_near) + list(down_far))
    down_grads = list(down_grads) + more
    block_rows = ff_block
    *up_grads, up_b_first, back_first = down_backward(
        where, rows_both, down_full, up_full, slope_first, 0, None, fast
    )
    if fast:
        back_first, *up_grads, down_fy, down_fx = sync(back_first, *up_grads, down_fy, down_fx)
        send_x, send_y = merge(
            [(down_grads[2], None)], [(down_grads[3], None)], down_fy, down_fx
        )
        back_first, send_x, send_y = sync(back_first, send_x, send_y)
        down_x, down_y = swap_win(send_x, 1), swap_y(send_y)
    *more, up_b_second, back_own, back_other = down_backward(
        where, rows_both, down_full, up_full, slope_second, 1, back_first, fast
    )
    up_grads = list(up_grads) + more
    if fast:
        back_other, act_first, down_x, down_y = sync(back_other, act_first, down_x, down_y)
        up_fy, up_fx = swap_y(up_grads[0]), swap_win(up_grads[1], 1)
        down_kept = total(
            [(down_grads[4], None), (down_x, None), (down_y, None)], block_rows, width
        )
    back_got = swap_core(back_other)
    mlp_own, mlp_away = down_forward(act_first, act_second, down_full)

    if fast:
        back_got, mlp_away, down_kept, *up_grads, up_fy, up_fx = sync(
            back_got, mlp_away, down_kept, *up_grads, up_fy, up_fx
        )
        down_parts = parts_z(down_kept)
        send_x, send_y = merge([(up_grads[2], None)], [(up_grads[3], None)], up_fy, up_fx)
        back_got, send_x, send_y = sync(back_got, send_x, send_y)
        up_x, up_y = swap_win(send_x, 1), swap_y(send_y)
    mlp_got = swap_core(mlp_away)
    grad_mid, grad_attended, mid_sums, grad_out_w = mid_backward(
        back_own, back_got, mid, grad_out, branch_attn, attended, out_full, mod, live
    )
    grad_attended, mlp_got = sync(grad_attended, mlp_got)
    result, res_away, gate_two_sum = result_forward(
        where, mlp_own, mlp_got, down_bias, mid, grad_out, mod, live
    )
    grad_attended, res_away = sync(grad_attended, res_away)
    res_back = swap_y(res_away.reshape(6, SPATIAL, width))
    grad_projected, space_sums, time_sums = attend_back(
        projected, grad_attended, attended, probs, local
    )
    qkv_block, out_block = 3 * width // devices, width // devices
    if fast:
        grad_projected, up_x, up_y, res_back, down_parts = sync(
            grad_projected, up_x, up_y, res_back, down_parts
        )
        own_first, own_second, other_first, other_second = qkv_grad(
            where, grad_projected, hidden_one, grad_out_w
        )
        up_x, other_first, other_second = sync(up_x, other_first, other_second)
        up_kept = total([(up_grads[4], None), (up_x, None), (up_y, None)], block_rows, width)
        up_grad = add_z(parts_z(up_kept))
        got_first, got_second = swap_core(other_first), swap_core(other_second)
    if fast:
        got_first, up_kept = sync(got_first, up_kept)
        send_fy, send_fx, attn_gx = first_quarters(own_first, got_first)
        send_fy, send_fx, grad_projected = sync(send_fy, send_fx, grad_projected)
        attn_fy, attn_fx = swap_y(send_fy), swap_win(send_fx, 1)
    else:
        grad_attn_w = jnp.concatenate(
            [
                qkv_grad_plain(grad_projected, hidden_one).reshape(n_win, 2, 2, qkv_block, width),
                grad_out_w.reshape(n_win, 2, 2, out_block, width),
            ],
            axis=3,
        )
        got = swap_core(pick(grad_attn_w, 1 - c, 2))
        attn_grad = scatter_plain(add_low(pick(grad_attn_w, c, 2), got), where)
        up_grad = scatter_plain(jnp.concatenate(up_grads).reshape(n_win, 2, ff_block, width), where)
        down_grad = scatter_plain(
            jnp.concatenate(down_grads).reshape(n_win, 2, ff_block, width), where
        )
    grad_tokens, gt_away, token_sums = tokens_backward(
        where, grad_projected, qkv_full, token_rows, grad_mid, mod
    )
    gt_away = gt_away.reshape(6, SPATIAL, width)
    if fast:
        token_sums, attn_fy, attn_fx, got_second = sync(
            token_sums, attn_fy, attn_fx, got_second
        )
        send_x, send_y = merge(
            [(attn_gx, None)], [(own_second, 0), (got_second, 0)], attn_fy, attn_fx, LAST_CUT
        )
        attn_x, attn_y = swap_win(send_x, 1), swap_y(send_y)
        token_sums, res_back, _, _ = sync(token_sums, res_back, send_x, send_y)

    grad_mod = jnp.concatenate(
        [
            token_sums[:, 0],
            token_sums[:, 1],
            mid_sums[:, 0],
            mid_sums[:, 1],
            mid_sums[:, 2],
            gate_two_sum[:, 0],
        ],
        axis=-1,
    ).astype(bf16)
    ada_block = 6 * width // devices
    to_quarter = jnp.transpose(grad_mod.reshape(local, 4, ada_quarter), (1, 0, 2))
    to_quarter = jnp.broadcast_to(to_quarter[None], (n_win, 4, local, ada_quarter))
    to_block = jnp.transpose(grad_mod.reshape(local, devices, ada_block), (1, 0, 2))
    grad_up_b = jnp.concatenate([up_b_first, up_b_second], axis=1)
    if fast:
        grad_up_b = grad_up_b.reshape(2, 2, 4, ff_block)
        grad_up_b = jnp.where(x == 0, grad_up_b[::-1], grad_up_b)
        grad_up_b = jnp.where(y == 0, grad_up_b[:, ::-1], grad_up_b)
        grad_up_b = jnp.transpose(grad_up_b, (2, 0, 1, 3))
    grad_up_b = grad_up_b.reshape(n_win * 2, 1, ff_block)
    core_mask = (jnp.arange(2, dtype=jnp.int32) == c).astype(f32)[None, :, None]
    grad_up_b = (grad_up_b * core_mask).reshape(devices, ff_block)
    grad_down_b = jnp.sum(grad_mlp.astype(f32), axis=0).reshape(devices, width // devices)
    first_send = jnp.concatenate(
        [
            to_quarter.reshape(devices, local * ada_quarter),
            to_block.reshape(devices, local * ada_block),
            grad_up_b.astype(bf16),
            grad_down_b.astype(bf16),
        ],
        axis=1,
    )
    res_other = swap_core(windows_back_pack(where, result, res_back))
    first_got = exchange_all(first_send)
    if fast:
        down_grad = add_z(down_parts)
        attn_x, attn_y, gt_away, res_other, first_send = sync(
            attn_x, attn_y, gt_away, res_other, first_send
        )
        kept = total(
            [(own_second, 1), (got_second, 1), (attn_x, None), (attn_y, None)],
            qkv_block + out_block,
            width,
        )
        attn_grad = sum_z_direct(kept, z)
        first_got, _ = sync(first_got, kept)
    gt_back = swap_y(gt_away)
    if fast:
        space_sums, time_sums, gt_back = sync(space_sums, time_sums, gt_back)
    lanes = jnp.arange(FRAMES * SPATIAL, dtype=jnp.int32)
    to_place = (lanes[:, None] % SPATIAL == jnp.arange(SPATIAL)[None]).astype(f32)
    to_slot = (lanes[:, None] // SPATIAL == jnp.arange(FRAMES)[None]).astype(f32)
    space_sum = jnp.dot(
        space_sums.reshape(heads * SPATIAL, FRAMES * SPATIAL), to_place, precision=exact_mode
    )
    space_sum = jnp.dot(
        space_sum.reshape(heads, SPATIAL * SPATIAL), onehot_space, precision=exact_mode
    )
    time_sum = jnp.dot(
        time_sums.reshape(local * heads * 8, FRAMES * SPATIAL), to_slot, precision=exact_mode
    ).reshape(local, heads, 8, FRAMES)[:, :, :FRAMES]
    time_sum = jnp.einsum("whab,wabt->ht", time_sum, onehot_time, precision=exact_mode)
    tables = jnp.concatenate([space_sum.reshape(-1), time_sum.reshape(-1)])
    sizes = [local * ada_quarter, local * ada_block, ff_block, width // devices]
    ends = [sum(sizes[: n + 1]) for n in range(4)]
    mod_got = first_got[:, : ends[0]].reshape(n_win * windows, ada_quarter)
    mod_own = first_got[:, ends[0] : ends[1]].reshape(n_win * windows, ada_block)
    sums = jnp.sum(first_got[:, ends[1] :].astype(f32), axis=0)
    out_up_b = sums[:ff_block]
    out_down_b = sums[ff_block : ff_block + width // devices]
    grad_ada_w = dot32(silu_all, mod_own, LEFT_T)
    grad_ada_b = jnp.sum(mod_own.astype(f32), axis=0)
    cond_part = dot32(mod_got, ada_part, RIGHT_T)
    cond_send = cond_part.astype(bf16).reshape(n_win, 1, windows * shard_rows)
    cond_send = jnp.broadcast_to(cond_send, (n_win, 4, windows * shard_rows))
    cond_send = cond_send.reshape(devices, windows * shard_rows)
    table_send = jnp.broadcast_to(tables.astype(bf16)[None], (devices, tables.shape[0]))
    last_got = exchange_all(jnp.concatenate([cond_send, table_send], axis=1)).astype(f32)
    cond_grad = last_got[:, : windows * shard_rows].reshape(n_win, 4, windows, shard_rows)
    cond_grad = jnp.transpose(jnp.sum(cond_grad, axis=1), (1, 0, 2)).reshape(windows, width)
    _, silu_back = jax.vjp(jax.nn.silu, condition.astype(f32))
    grad_condition = silu_back(cond_grad)[0]
    table_all = jnp.sum(last_got[:, windows * shard_rows :], axis=0)
    space_size = table_space.size
    grad_space = table_all[:space_size].reshape(table_space.shape)
    grad_time = table_all[space_size : space_size + table_time.size].reshape(table_time.shape)

    gt_other = swap_core(windows_back_pack(where, grad_tokens, gt_back))
    result = windows_back_join(where, result, res_back, res_other, tokens, bf16)
    grad_tokens = windows_back_join(where, grad_tokens, gt_back, gt_other, cotangent, f32)

    return (
        result,
        grad_tokens,
        grad_condition,
        grad_ada_w,
        grad_ada_b,
        attn_grad[:qkv_block].T,
        attn_grad[qkv_block:].T,
        up_grad.T,
        out_up_b,
        down_grad,
        out_down_b,
        grad_space,
        grad_time,
    )


def solution(mesh):
    return jax.shard_map(
        on_device,
        mesh=mesh,
        in_specs=(
            P("win", "frm", None),
            P("win", None),
            P("win"),
            P("win"),
            P("win", None),
            P("win"),
            P("win", None),
            P("win", None),
            P("win", None),
            P("win"),
            P("win", None),
            P("win"),
            P(),
            P(),
            P("win", "frm", None),
        ),
        out_specs=(
            P("win", "frm", None),
            P("win", "frm", None),
            P("win", None),
            P(None, BOTH),
            P(BOTH),
            P(None, BOTH),
            P(None, BOTH),
            P(None, BOTH),
            P(BOTH),
            P(BOTH, None),
            P(BOTH),
            P(),
            P(),
        ),
        check_vma=False,
    )
```

```python
import functools

import jax
import jax.numpy as jnp
from jax import lax
from jax.experimental import pallas as pl
from jax.experimental.pallas import tpu as pltpu
from jax.sharding import PartitionSpec as P

SIDE = 8
FRAMES = 5
SPATIAL = SIDE * SIDE
BOTH = ("win", "frm")
EPS = 1e-06
VMEM_LIMIT = 50 * 1024 * 1024
WHOLE_LIMIT = 60 * 1024 * 1024

f32 = jnp.float32
bf16 = jnp.bfloat16
exact_mode = lax.Precision.HIGHEST
SMALL = pl.CostEstimate(flops=1024, bytes_accessed=1024, transcendentals=0)


def swap_frm(array, bit):
    return lax.ppermute(array, "frm", [(j, j ^ bit) for j in range(4)])


def swap_core(array):
    return swap_frm(array, 1)


def swap_y(array):
    return swap_frm(array, 2)


def swap_win(array, bits):
    count = lax.axis_size("win")
    return lax.ppermute(array, "win", [(j, j ^ bits) for j in range(count)])


def exchange_all(array):
    return lax.all_to_all(array, BOTH, split_axis=0, concat_axis=0, tiled=True)


def pick(array, index, axis):
    return lax.dynamic_index_in_dim(array, index, axis, keepdims=False)


def sync(*arrays):
    return lax.optimization_barrier(arrays)


def exchange_z(blocks):
    groups = [[2 * z + x for z in range(4)] for x in range(2)]
    return lax.all_to_all(
        blocks, "win", split_axis=0, concat_axis=0, axis_index_groups=groups, tiled=True
    )


def gather_z(half):
    return exchange_z(jnp.broadcast_to(half[None], (4,) + half.shape))


def gather_z_direct(half):
    return [half] + [swap_win(half, 2 * k) for k in (1, 2, 3)]


def move_kernel(body, count, where, *refs):
    sems = refs[count]
    refs = refs[:count] + refs[count + 1 :]
    waits = []

    def copy(sources, target):
        sem = sems.at[len(waits)]
        if len(sources) == 1:
            pltpu.make_async_copy(sources[0], target, sem).start()
        else:
            condition, first, second = sources

            @pl.when(condition)
            def _():
                pltpu.make_async_copy(first, target, sem).start()

            @pl.when(jnp.logical_not(condition))
            def _():
                pltpu.make_async_copy(second, target, sem).start()

        waits.append(pltpu.make_async_copy(sources[-1], target, sem))

    def finish():
        for wait in waits:
            wait.wait()

    body(where, refs, copy, finish)


def move_call(body, name, where, inputs, outputs, copies, scratch=(), limit=VMEM_LIMIT):
    return pl.pallas_call(
        functools.partial(move_kernel, body, len(inputs) + len(outputs)),
        out_shape=outputs,
        in_specs=[pl.BlockSpec(memory_space=pltpu.SMEM)]
        + [pl.BlockSpec(memory_space=pltpu.HBM)] * len(inputs),
        out_specs=[pl.BlockSpec(memory_space=pltpu.VMEM)] * len(outputs),
        scratch_shapes=[pltpu.SemaphoreType.DMA((copies,))] + list(scratch),
        compiler_params=pltpu.CompilerParams(vmem_limit_bytes=limit),
        cost_estimate=SMALL,
        name=name,
    )(where, *inputs)


def low_shape(*shape):
    return jax.ShapeDtypeStruct(shape, bf16)


def halves(where, w_qkv, w_out, w_up, w_down):
    rows, width = w_out.shape
    blocks = w_up.shape[1] // 256
    block = w_down.shape[0] // 4

    def body(where, refs, copy, finish):
        qkv, out, up, down, q_half, up_half, down_half = refs
        y, c = where[2], where[3]
        quarter = rows // 4
        q_rows = pl.ds(pl.multiple_of((c * 2 + y) * quarter, quarter), quarter)
        copy([qkv.at[q_rows]], q_half.at[:, pl.ds(0, 3 * width)])
        copy([out.at[q_rows]], q_half.at[:, pl.ds(3 * width, width)])
        up_rows = pl.ds(pl.multiple_of(y * (rows // 2), rows // 2), rows // 2)
        for n in range(blocks):
            column = pl.multiple_of((2 * n + c) * 128, 128)
            copy([up.at[up_rows, pl.ds(column, 128)]], up_half.at[:, pl.ds(n * 128, 128)])
        copy([down.at[pl.ds(pl.multiple_of((y * 2 + c) * block, block), block)]], down_half)
        finish()

    return move_call(
        body,
        "halves",
        where,
        [w_qkv, w_out, w_up, w_down],
        [
            low_shape(rows // 4, 4 * width),
            low_shape(rows // 2, blocks * 128),
            low_shape(block, width),
        ],
        blocks + 3,
        limit=WHOLE_LIMIT,
    )


def gather_near(along_z):
    return [along_z, swap_win(along_z, 1), swap_y(along_z)]


def gather_far(near, cut=0):
    if not cut:
        return [swap_win(near[2], 1)]
    return [swap_y(near[1][:cut]), swap_win(near[2][cut:], 1)]


PLACES = ((0, 0), (1, 0), (0, 1), (1, 1))


def piece(refs, number, k):
    if number < 3 or len(refs) == 4:
        return refs[number].at[k]
    cut = refs[3].shape[0]
    return refs[3].at[k] if k < cut else refs[4].at[k - cut]


def place_qkv(where, pieces):
    _, rows, columns = pieces[0].shape
    width = columns // 4

    def body(where, refs, copy, finish):
        z, x, y, c = where[0], where[1], where[2], where[3]
        for core in range(2):
            for n, (j, l) in enumerate(PLACES):
                for k in range(4):
                    source = piece(refs[4 * core : 4 * core + 4], n, k)
                    at = ((z ^ k) * 2 + (x ^ j), c ^ core, y ^ l)
                    copy([source.at[:, pl.ds(0, 3 * width)]], refs[8].at[at])
                    copy([source.at[:, pl.ds(3 * width, width)]], refs[9].at[at])
        finish()

    qkv, out = move_call(
        body,
        "place_qkv",
        where,
        pieces,
        [low_shape(8, 2, 2, rows, 3 * width), low_shape(8, 2, 2, rows, width)],
        64,
    )
    return qkv.reshape(32 * rows, 3 * width), out.reshape(32 * rows, width)


def place_up(where, pieces):
    _, rows, columns = pieces[0].shape

    def body(where, refs, copy, finish):
        z, x, y = where[0], where[1], where[2]
        for n, (j, l) in enumerate(PLACES):
            for k in range(4):
                copy([piece(refs[:4], n, k)], refs[4].at[(z ^ k) * 2 + (x ^ j), y ^ l])
        finish()

    return move_call(
        body, "place_up", where, pieces, [low_shape(8, 2, rows, columns)], 16
    )[0].reshape(16 * rows, columns)


def place_down(where, pieces):
    _, rows, columns = pieces[0].shape

    def body(where, refs, copy, finish):
        for n in range(4):
            for k in range(4):
                quarter = QUARTERS.index(PLACES[n])
                copy([piece(refs[:5], n, k)], refs[5].at[quarter, where[0] ^ k])
        finish()

    return move_call(
        body, "place_down", where, pieces, [low_shape(4, 4, rows, columns)], 16
    )[0].reshape(16 * rows, columns)


QUARTERS = ((1, 1), (1, 0), (0, 1), (0, 0))


FAR_CUT = 2
LAST_CUT = 1


def add_low(*terms):
    return functools.reduce(jnp.add, [term.astype(f32) for term in terms]).astype(bf16)


def block_specs(array, first, cut=0):
    if array.ndim == 4:
        return pl.BlockSpec((1, 1) + array.shape[2:], lambda i: (first, i, 0, 0))
    rows = array.shape[0] // (4 if first is None else first)
    last = array.shape[0] // rows - 1
    return pl.BlockSpec((rows, array.shape[1]), lambda i: (jnp.clip(i - cut, 0, last), 0))


def read(ref):
    return ref[...].reshape(ref.shape[-2:]).astype(f32)


def merge_kernel(counts, cut, *refs):
    x_terms, y_terms = refs[: counts[0]], refs[counts[0] : counts[0] + counts[1]]
    far_y, far_x, send_x, send_y = refs[-4:]
    first = pl.program_id(0) < cut
    to_x = functools.reduce(jnp.add, [read(ref) for ref in x_terms])
    to_y = functools.reduce(jnp.add, [read(ref) for ref in y_terms])
    send_x[...] = jnp.where(first, to_x + read(far_y), to_x).astype(bf16)
    send_y[...] = jnp.where(first, to_y, to_y + read(far_x)).astype(bf16)


def merge(x_terms, y_terms, far_y, far_x, cut=FAR_CUT):
    rows, width = far_y.shape[0] // cut, far_y.shape[1]
    block = pl.BlockSpec((rows, width), lambda i: (i, 0))
    return dense_call(
        functools.partial(merge_kernel, (len(x_terms), len(y_terms)), cut),
        "merge",
        (4,),
        [block_specs(*term) for term in list(x_terms) + list(y_terms)]
        + [block_specs(far_y, cut), block_specs(far_x, 4 - cut, cut)],
        [block, block],
        [low_shape(4 * rows, width)] * 2,
    )(*[term[0] for term in list(x_terms) + list(y_terms)], far_y, far_x)


def total_kernel(*refs):
    refs[-1][...] = functools.reduce(jnp.add, [read(ref) for ref in refs[:-1]]).astype(bf16)


def total(terms, rows, width):
    return dense_call(
        total_kernel,
        "total",
        (4,),
        [block_specs(*term) for term in terms],
        pl.BlockSpec((rows, width), lambda i: (i, 0)),
        low_shape(4 * rows, width),
    )(*[term[0] for term in terms])


def first_kernel(own_ref, got_ref, far_y, far_x, x_ref):
    far = own_ref[0].astype(f32) + got_ref[0].astype(f32)
    far_y[...] = far[:LAST_CUT].astype(bf16).reshape(far_y.shape)
    far_x[...] = far[LAST_CUT:].astype(bf16).reshape(far_x.shape)
    x_ref[...] = (own_ref[1].astype(f32) + got_ref[1].astype(f32)).astype(bf16).reshape(x_ref.shape)


def first_quarters(own, got):
    _, _, rows, width = own.shape
    shapes = [(LAST_CUT * rows, width), ((4 - LAST_CUT) * rows, width), (4 * rows, width)]
    return dense_call(
        first_kernel,
        "first_quarters",
        (1,),
        [full_spec(own.shape)] * 2,
        [full_spec(shape) for shape in shapes],
        [low_shape(*shape) for shape in shapes],
    )(own, got)


def parts_z(kept):
    return exchange_z(kept.reshape((4, kept.shape[0] // 4) + kept.shape[1:]))


def add_z(parts):
    return jnp.sum(parts.astype(f32), axis=0)


def sum_z_direct(kept, z):
    blocks = kept.reshape((4, kept.shape[0] // 4) + kept.shape[1:])
    sent = [swap_win(pick(blocks, z ^ k, 0), 2 * k) for k in (1, 2, 3)]
    return functools.reduce(jnp.add, [part.astype(f32) for part in [pick(blocks, z, 0)] + sent])


def scatter_plain(grad, where):
    mine = lax.psum_scatter(grad.astype(f32), "win", scatter_dimension=0, tiled=False)
    return pick(mine, where[2], 0) + swap_y(pick(mine, 1 - where[2], 0))


def windows_send(where, slots):
    def body(where, refs, copy, finish):
        for half in range(2):
            first = half * 8 + (1 - where[3]) * 4
            copy([refs[0].at[pl.ds(first, 4)]], refs[1].at[pl.ds(half * 4, 4)])
        finish()

    return move_call(body, "rows_send", where, [slots], [low_shape(8, *slots.shape[1:])], 2, limit=WHOLE_LIMIT)[0]


def windows_pack(where, slots, got):
    def body(where, refs, copy, finish):
        own, other, here, away = refs
        y, c = where[2], where[3]
        for target, half in ((here, y), (away, 1 - y)):
            for t in range(2):
                window = half * 4 + c * 2 + t
                mine, theirs = window * 2, half * 4 + t * 2
                copy([c == 0, own.at[mine], other.at[theirs]], target.at[t * 3])
                copy([c == 0, other.at[theirs], own.at[mine]], target.at[t * 3 + 1])
                copy(
                    [where[6 + window] == where[4], own.at[mine + 1], other.at[theirs + 1]],
                    target.at[t * 3 + 2],
                )
        finish()

    shape = low_shape(6, *slots.shape[1:])
    return move_call(body, "rows_pack", where, [slots, got], [shape, shape], 12)


def windows_join(where, here, away):
    def body(where, refs, copy, finish):
        here, away, out = refs
        y = where[2]
        for t in range(2):
            for slot in range(4):
                source = t * 3 + slot % 2
                copy([y == slot // 2, here.at[source], away.at[source]], out.at[t * 5 + slot])
            near = where[6 + where[4] * 2 + t] // 2 == y
            copy([near, here.at[t * 3 + 2], away.at[t * 3 + 2]], out.at[t * 5 + 4])
        finish()

    shape = low_shape(10, *here.shape[1:])
    out = move_call(body, "rows_join", where, [here, away], [shape], 10)[0]
    return out.reshape(10 * here.shape[1], here.shape[2])


def windows_back_pack(where, rows, back):
    def body(where, refs, copy, finish):
        rows, back, out = refs
        y, c = where[2], where[3]
        for t in range(2):
            here, there = y * 4 + t * 2, (1 - y) * 4 + t * 2
            copy([rows.at[t * 5 + 2 * y + 1 - c]], out.at[here])
            copy([rows.at[t * 5 + 4]], out.at[here + 1])
            copy([back.at[t * 3 + 1 - c]], out.at[there])
            copy([back.at[t * 3 + 2]], out.at[there + 1])
        finish()

    slots = rows.reshape(10, SPATIAL, rows.shape[1])
    shape = low_shape(8, SPATIAL, rows.shape[1])
    return move_call(
        body, "rows_back_pack", where, [slots, back], [shape], 8, limit=WHOLE_LIMIT
    )[0]


def windows_back_join(where, rows, back, got, dead, dtype):
    width = rows.shape[1]

    def body(where, refs, copy, finish):
        rows, back, got, dead, out, arrived = refs
        y, c, frm, count = where[2], where[3], where[4], where[5]
        for half in range(2):
            side = y if half == 0 else 1 - y
            for core in range(2):
                for t in range(2):
                    window = side * 4 + (c if core == 0 else 1 - c) * 2 + t
                    if core == 1:
                        even, odd = got.at[side * 4 + t * 2], got.at[side * 4 + t * 2 + 1]
                    elif half == 0:
                        even, odd = rows.at[t * 5 + 2 * y + c], rows.at[t * 5 + 4]
                    else:
                        even, odd = back.at[t * 3 + c], back.at[t * 3 + 2]
                    live = window < count
                    place = window * 2
                    copy([live, even, dead.at[place]], arrived.at[place])
                    doubled = jnp.logical_and(live, where[6 + window] == frm)
                    copy([doubled, odd, dead.at[place + 1]], arrived.at[place + 1])
        finish()
        out[...] = arrived[...].astype(out.dtype)

    slots = rows.reshape(10, SPATIAL, width)
    out = move_call(
        body,
        "rows_back_join",
        where,
        [slots, back, got, dead.reshape(16, SPATIAL, width)],
        [jax.ShapeDtypeStruct((16, SPATIAL, width), dtype)],
        16,
        [pltpu.VMEM((16, SPATIAL, width), bf16)],
        WHOLE_LIMIT,
    )[0]
    return out.reshape(dead.shape)


GROUP = 4
LANES = GROUP * 64


def head_lanes(head):
    lanes = lax.broadcasted_iota(jnp.int32, (1, LANES), 1)
    return (lanes // 64) == head


def attend_kernel(q_ref, k_ref, v_ref, space_ref, time_ref, o_ref, p_ref):
    q, k, v = q_ref[...], k_ref[...], v_ref[...]
    rows = q.shape[0]
    total = jnp.zeros((rows, LANES), f32)
    for head in range(GROUP):
        lanes = head_lanes(head)
        scaled = jnp.where(lanes, q * jnp.asarray(0.125, bf16), jnp.zeros_like(q))
        scores = lax.dot_general(scaled, k, (((1,), (1,)), ((), ())), preferred_element_type=f32)
        shaped = scores.reshape(rows // SPATIAL, SPATIAL, rows)
        shaped = shaped + space_ref[head][None] + time_ref[0, head, : rows // SPATIAL][:, None, :]
        scores = shaped.reshape(rows, rows)
        grown = jnp.exp(scores - jnp.max(scores, axis=-1, keepdims=True))
        inverse = 1.0 / jnp.sum(grown, axis=-1, keepdims=True)
        probs = (grown * inverse).astype(bf16)
        p_ref[0, head] = probs
        masked = jnp.where(lanes, v, jnp.zeros_like(v))
        total = total + jnp.dot(probs, masked, preferred_element_type=f32)
    o_ref[...] = total.astype(bf16)


def attend_back_kernel(
    q_ref, k_ref, v_ref, do_ref, o_ref, p_ref, grad_ref, space_ref, time_ref
):
    q, k, v, do = q_ref[...], k_ref[...], v_ref[...], do_ref[...]
    rows = q.shape[0]
    slots = rows // SPATIAL
    product = do.astype(f32) * o_ref[...].astype(f32)
    grad_q = jnp.zeros((rows, LANES), f32)
    grad_k = jnp.zeros((rows, LANES), f32)
    grad_v = jnp.zeros((rows, LANES), f32)

    @pl.when(pl.program_id(1) == 0)
    def _():
        space_ref[...] = jnp.zeros_like(space_ref)

    for head in range(GROUP):
        lanes = head_lanes(head)
        none = jnp.zeros_like(q)
        scale = jnp.asarray(0.125, bf16)
        row_dot = jnp.sum(jnp.where(lanes, product, 0.0), axis=-1, keepdims=True)
        grads = jnp.where(lanes, do, none)
        probs = p_ref[0, head]
        grad_probs = lax.dot_general(
            grads, v, (((1,), (1,)), ((), ())), preferred_element_type=f32
        )
        grad_scores = probs.astype(f32) * (grad_probs - row_dot)
        low = grad_scores.astype(bf16)
        over_rows = (((0,), (0,)), ((), ()))
        grad_v = grad_v + lax.dot_general(probs, grads, over_rows, preferred_element_type=f32)
        grad_k = grad_k + lax.dot_general(
            low, jnp.where(lanes, q * scale, none), over_rows, preferred_element_type=f32
        )
        grad_q = grad_q + jnp.dot(
            low, jnp.where(lanes, k * scale, none), preferred_element_type=f32
        )
        shaped = grad_scores.reshape(slots, SPATIAL, rows)
        space_ref[head] += jnp.sum(shaped, axis=0)
        time_ref[0, head, :slots] = jnp.sum(shaped, axis=1)
    grad_ref[0] = grad_q.astype(bf16)
    grad_ref[1] = grad_k.astype(bf16)
    grad_ref[2] = grad_v.astype(bf16)


def attention_specs(rows, groups):
    q_spec = pl.BlockSpec((rows, LANES), lambda group, window: (window, group))
    k_spec = pl.BlockSpec((rows, LANES), lambda group, window: (window, group + groups))
    v_spec = pl.BlockSpec((rows, LANES), lambda group, window: (window, group + 2 * groups))
    p_spec = pl.BlockSpec((1, GROUP, rows, rows), lambda group, window: (window, group, 0, 0))
    space_spec = pl.BlockSpec((GROUP, SPATIAL, rows), lambda group, window: (group, 0, 0))
    time_spec = pl.BlockSpec((1, GROUP, 8, rows), lambda group, window: (window, group, 0, 0))
    return q_spec, k_spec, v_spec, p_spec, space_spec, time_spec


def attend(projected, space_bias, time_bias, windows):
    rows = projected.shape[0] // windows
    heads = space_bias.shape[0]
    q_spec, k_spec, v_spec, p_spec, space_spec, time_spec = attention_specs(rows, heads // GROUP)
    width = heads * 64
    return pl.pallas_call(
        attend_kernel,
        grid=(heads // GROUP, windows),
        in_specs=[q_spec, k_spec, v_spec, space_spec, time_spec],
        out_specs=[q_spec, p_spec],
        out_shape=[
            pltpu.HBM((windows * rows, width), bf16),
            pltpu.HBM((windows, heads, rows, rows), bf16),
        ],
        compiler_params=pltpu.CompilerParams(vmem_limit_bytes=VMEM_LIMIT),
        cost_estimate=SMALL,
        name="attend",
    )(projected, projected, projected, space_bias, time_bias)


def attend_back(projected, grad_attended, attended, probs, windows):
    heads, rows = probs.shape[1], probs.shape[2]
    q_spec, k_spec, v_spec, p_spec, space_spec, time_spec = attention_specs(rows, heads // GROUP)
    width = heads * 64
    return pl.pallas_call(
        attend_back_kernel,
        grid=(heads // GROUP, windows),
        in_specs=[q_spec, k_spec, v_spec, q_spec, q_spec, p_spec],
        out_specs=[
            pl.BlockSpec((3, rows, LANES), lambda group, window: (0, window, group)),
            space_spec,
            time_spec,
        ],
        out_shape=[
            pltpu.HBM((3, windows * rows, width), bf16),
            pltpu.HBM((heads, SPATIAL, rows), f32),
            pltpu.HBM((windows, heads, 8, rows), f32),
        ],
        compiler_params=pltpu.CompilerParams(vmem_limit_bytes=VMEM_LIMIT),
        cost_estimate=SMALL,
        name="attend_back",
    )(projected, projected, projected, grad_attended, attended, probs)


def full_spec(shape):
    return pl.BlockSpec(shape, lambda *_: (0,) * len(shape))


def in_hbm(shapes):
    if isinstance(shapes, list):
        return [in_hbm(shape) for shape in shapes]
    return pltpu.HBM(shapes.shape, shapes.dtype)


def dense_call(kernel, name, grid, in_specs, out_specs, out_shape, scratch=()):
    return pl.pallas_call(
        kernel,
        grid=grid,
        in_specs=in_specs,
        out_specs=out_specs,
        out_shape=in_hbm(out_shape),
        scratch_shapes=list(scratch),
        compiler_params=pltpu.CompilerParams(vmem_limit_bytes=VMEM_LIMIT),
        cost_estimate=SMALL,
        name=name,
    )


def normalize(values_in):
    centred = values_in - jnp.mean(values_in, axis=-1, keepdims=True)
    inverse = lax.rsqrt(jnp.mean(centred * centred, axis=-1, keepdims=True) + EPS)
    return centred * inverse, inverse


def normalize_back(grad_normed, normed, inverse):
    return inverse * (
        grad_normed
        - jnp.mean(grad_normed, axis=-1, keepdims=True)
        - normed * jnp.mean(grad_normed * normed, axis=-1, keepdims=True)
    )


def dot32(left, right, dims):
    return lax.dot_general(left, right, (dims, ((), ())), preferred_element_type=f32)


def modulation(mod_ref, number, window=0):
    width = mod_ref.shape[2] // 6
    return mod_ref[window, :, number * width : (number + 1) * width]


PLAIN = ((1,), (0,))
RIGHT_T = ((1,), (1,))
LEFT_T = ((0,), (0,))


def qkv_kernel(tokens_ref, mod_ref, w_ref, projected_ref, hidden_ref):
    local = mod_ref.shape[0]
    rows = tokens_ref.shape[0] // local

    @pl.when(pl.program_id(0) == 0)
    def _():
        for window in range(local):
            part = pl.ds(window * rows, rows)
            normed, _ = normalize(tokens_ref[part, :].astype(f32))
            shift, scale = modulation(mod_ref, 0, window), modulation(mod_ref, 1, window)
            hidden_ref[part, :] = (normed * (1.0 + scale) + shift).astype(bf16)

    projected_ref[...] = dot32(hidden_ref[...], w_ref[...], PLAIN).astype(bf16)


def qkv_forward(tokens, mod, w_attn):
    count, width = tokens.shape
    tile = 512
    return dense_call(
        qkv_kernel,
        "qkv",
        (3 * width // tile,),
        [
            full_spec(tokens.shape),
            full_spec(mod.shape),
            pl.BlockSpec((width, tile), lambda i: (0, i)),
        ],
        [pl.BlockSpec((count, tile), lambda i: (0, i)), full_spec(tokens.shape)],
        [jax.ShapeDtypeStruct((count, 3 * width), bf16), jax.ShapeDtypeStruct((count, width), bf16)],
    )(tokens, mod, w_attn)


def out_kernel(attended_ref, w_ref, tokens_ref, mod_ref, branch_ref, mid_ref, hidden_ref):
    branch = dot32(attended_ref[...], w_ref[...], PLAIN)
    mid = tokens_ref[...].astype(f32) + modulation(mod_ref, 2) * branch
    normed, _ = normalize(mid)
    branch_ref[...] = branch.astype(bf16)
    mid_ref[...] = mid
    hidden_ref[...] = (normed * (1.0 + modulation(mod_ref, 4)) + modulation(mod_ref, 3)).astype(bf16)


def out_forward(attended, w_attn, tokens, mod):
    count, width = tokens.shape
    local = mod.shape[0]
    rows = count // local
    row_spec = pl.BlockSpec((rows, width), lambda i: (i, 0))
    return dense_call(
        out_kernel,
        "attn_out",
        (local,),
        [
            row_spec,
            full_spec((width, width)),
            row_spec,
            pl.BlockSpec((1,) + mod.shape[1:], lambda i: (i, 0, 0)),
        ],
        [row_spec] * 3,
        [
            jax.ShapeDtypeStruct((count, width), bf16),
            jax.ShapeDtypeStruct((count, width), f32),
            jax.ShapeDtypeStruct((count, width), bf16),
        ],
    )(attended, w_attn, tokens, mod)


def gelu_parts(value):
    factor = 0.7978845608028654
    square = value * value
    half = 0.5 + 0.5 * jnp.tanh(value * (factor + (factor * 0.044715) * square))
    gelu = value * half
    slope = half + gelu * (1.0 - half) * (2.0 * factor + (6.0 * factor * 0.044715) * square)
    return gelu, slope


def joined(refs, axis):
    parts = [ref[...] for ref in refs]
    return parts[0] if len(parts) == 1 else jnp.concatenate(parts, axis=axis)


def hidden_specs(width, tile, part, fast, rows):
    if not fast:
        return [pl.BlockSpec((rows, tile), lambda i, where: (0, 2 * part + i))]

    def block(z):
        def index(i, where):
            j, l = 1 - part, 1 - i
            return 0, z * 4 + (where[1] ^ j) * 2 + (where[2] ^ l)

        return pl.BlockSpec((rows, tile // 4), index)

    return [block(z) for z in range(4)]


def held_spec(shape):
    return pl.BlockSpec(shape, lambda i, where: (0,) * len(shape))


def hidden_call(kernel, name, where, inputs, in_specs, out_specs, out_shape, scratch=()):
    return pl.pallas_call(
        kernel,
        grid_spec=pltpu.PrefetchScalarGridSpec(
            num_scalar_prefetch=1,
            grid=(2,),
            in_specs=in_specs,
            out_specs=out_specs,
            scratch_shapes=list(scratch),
        ),
        out_shape=in_hbm(out_shape),
        compiler_params=pltpu.CompilerParams(vmem_limit_bytes=VMEM_LIMIT),
        cost_estimate=SMALL,
        name=name,
    )(where, *inputs)


def write_quarters(refs, value):
    @pl.when(pl.program_id(0) == 0)
    def _():
        start = 0
        for ref in refs[:-1]:
            ref[...] = value[start : start + ref.shape[0]].astype(bf16)
            start += ref.shape[0]

    @pl.when(pl.program_id(0) == 1)
    def _():
        refs[-1][...] = value.astype(bf16)


def quarter_shapes(tile, width, part):
    cut = FAR_CUT * tile // 4
    return [(tile, width)] * 2 if part else [(cut, width), (tile - cut, width), (tile, width)]


def up_kernel(pieces, where_ref, own_ref, other_ref, mlp_ref, mlp_other_ref, *refs):
    w, bias = joined(refs[:pieces], 1), joined(refs[pieces : 2 * pieces], 1)
    act_ref, slope_ref = refs[2 * pieces : 2 * pieces + 2]
    grad_refs = refs[2 * pieces + 2 :]
    total = None
    for half, (hidden, mlp) in enumerate(((own_ref, mlp_ref), (other_ref, mlp_other_ref))):
        activated, slope = gelu_parts(dot32(hidden[...], w, PLAIN) + bias)
        activated = activated.astype(bf16)
        act_ref[half] = activated
        slope_ref[half] = slope.astype(bf16)
        part = dot32(activated, mlp[...], LEFT_T)
        total = part if total is None else total + part
    write_quarters(grad_refs, total)


def up_forward(where, rows_both, w_up, bias, part, fast):
    count, width = rows_both[0].shape
    inner = w_up.shape[1]
    tile = inner // 4
    both = pl.BlockSpec((2, count, tile), lambda i, where: (0, 0, i))
    w_specs = hidden_specs(width, tile, part, fast, width)
    bias_specs = hidden_specs(width, tile, part, fast, 1)
    pieces = len(w_specs)
    return hidden_call(
        functools.partial(up_kernel, pieces),
        "mlp_up",
        where,
        list(rows_both) + [w_up] * pieces + [bias] * pieces,
        [held_spec((count, width))] * 4 + w_specs + bias_specs,
        [both, both] + [held_spec(shape) for shape in quarter_shapes(tile, width, part)],
        [low_shape(2, count, 2 * tile)] * 2
        + [low_shape(*shape) for shape in quarter_shapes(tile, width, part)],
    )


def down_back_kernel(pieces, part, where_ref, own_ref, other_ref, mlp_ref, mlp_other_ref, down_ref, *refs):
    up = joined(refs[:pieces], 1)
    slope_ref = refs[pieces]
    refs = refs[pieces + 1 :]
    earlier_ref = refs[0] if part else None
    outs = refs[1:] if part else refs
    quarters = 2 if part else 3
    grad_refs, bias_ref = outs[:quarters], outs[quarters]
    back_refs, total_ref = outs[quarters + 1 : -1], outs[-1]
    step = pl.program_id(0)
    down = down_ref[...]
    total, sums = None, None
    for half, (hidden, mlp) in enumerate(((own_ref, mlp_ref), (other_ref, mlp_other_ref))):
        grad_pre = dot32(mlp[...], down, RIGHT_T) * slope_ref[half].astype(f32)
        column = jnp.sum(grad_pre, axis=0, keepdims=True)
        grad_pre = grad_pre.astype(bf16)
        add = dot32(grad_pre, hidden[...], LEFT_T)
        total = add if total is None else total + add
        sums = column if sums is None else sums + column
        back = dot32(grad_pre, up, RIGHT_T)

        @pl.when(step == 0)
        def _(half=half, back=back):
            total_ref[half] = back + earlier_ref[half].astype(f32) if part else back

        @pl.when(step > 0)
        def _(half=half, back=back):
            total_ref[half] += back

    bias_ref[...] = sums
    write_quarters(grad_refs, total)

    @pl.when(step == 1)
    def _():
        if part:
            back_refs[0][...] = total_ref[0]
            back_refs[1][...] = total_ref[1].astype(bf16)
        else:
            back_refs[0][...] = total_ref[...].astype(bf16)


def down_backward(where, rows_both, w_down, w_up, slope, part, earlier, fast):
    count, width = rows_both[0].shape
    inner = w_up.shape[1]
    tile = inner // 4
    back_shape = (2, count, width)
    if part:
        back_specs = [held_spec((count, width))] * 2
        back_shapes = [jax.ShapeDtypeStruct((count, width), f32), low_shape(count, width)]
    else:
        back_specs = [held_spec(back_shape)]
        back_shapes = [low_shape(*back_shape)]
    w_specs = hidden_specs(width, tile, part, fast, width)
    pieces = len(w_specs)
    return hidden_call(
        functools.partial(down_back_kernel, pieces, part),
        "mlp_back",
        where,
        list(rows_both) + [w_down] + [w_up] * pieces + [slope] + ([earlier] if part else []),
        [held_spec((count, width))] * 4
        + [pl.BlockSpec((tile, width), lambda i, where: (2 * part + i, 0))]
        + w_specs
        + [pl.BlockSpec((2, count, tile), lambda i, where: (0, 0, i))]
        + ([held_spec(back_shape)] if part else []),
        [held_spec(shape) for shape in quarter_shapes(tile, width, part)]
        + [pl.BlockSpec((1, tile), lambda i, where: (0, i))]
        + back_specs,
        [low_shape(*shape) for shape in quarter_shapes(tile, width, part)]
        + [jax.ShapeDtypeStruct((1, 2 * tile), f32)]
        + back_shapes,
        [pltpu.VMEM(back_shape, f32)],
    )


def down_kernel(first_ref, second_ref, w_ref, own_ref, other_ref):
    half = first_ref.shape[2]
    for number, out_ref in enumerate((own_ref, other_ref)):
        total = dot32(first_ref[number], w_ref[:half], PLAIN)
        total = total + dot32(second_ref[number], w_ref[half:], PLAIN)
        out_ref[...] = total.astype(out_ref.dtype)


def down_forward(first, second, w_down):
    _, count, half = first.shape
    width = w_down.shape[1]
    tile = 256
    row_spec = pl.BlockSpec((count, tile), lambda i: (0, i))
    return dense_call(
        down_kernel,
        "mlp_down",
        (width // tile,),
        [full_spec(first.shape)] * 2 + [pl.BlockSpec((2 * half, tile), lambda i: (0, i))],
        [row_spec, row_spec],
        [jax.ShapeDtypeStruct((count, width), f32), low_shape(count, width)],
    )(first, second, w_down)


def split_away(where_ref, rows_ref, away_ref):
    first = pl.multiple_of((1 - where_ref[2]) * 2 * SPATIAL, 2 * SPATIAL)
    away_ref[: 2 * SPATIAL] = rows_ref[pl.ds(first, 2 * SPATIAL), :]
    away_ref[2 * SPATIAL :] = rows_ref[4 * SPATIAL :, :]


def result_kernel(
    where_ref, own_ref, other_ref, bias_ref, mid_ref, cot_ref, mod_ref, live_ref,
    result_ref, away_ref, gate_ref,
):
    branch = own_ref[...] + other_ref[...].astype(f32) + bias_ref[...]
    result_ref[...] = (mid_ref[...] + modulation(mod_ref, 5) * branch).astype(bf16)
    split_away(where_ref, result_ref, away_ref)
    gate_ref[0] = live_ref[0] * jnp.sum(branch * cot_ref[...].astype(f32), axis=0, keepdims=True)


def result_forward(where, own, other, bias, mid, cotangent, mod, live):
    count, width = own.shape
    local = mod.shape[0]
    row_spec = pl.BlockSpec((count // local, width), lambda i: (i, 0))
    one = pl.BlockSpec((1, 1, width), lambda i: (i, 0, 0))
    return dense_call(
        result_kernel,
        "result",
        (local,),
        [pl.BlockSpec(memory_space=pltpu.SMEM)]
        + [row_spec, row_spec, full_spec(bias.shape), row_spec, row_spec]
        + [pl.BlockSpec((1,) + mod.shape[1:], lambda i: (i, 0, 0)), one],
        [row_spec, pl.BlockSpec((3 * SPATIAL, width), lambda i: (i, 0)), one],
        [
            low_shape(count, width),
            low_shape(local * 3 * SPATIAL, width),
            jax.ShapeDtypeStruct((local, 1, width), f32),
        ],
    )(where, own, other, bias, mid, cotangent, mod, live)


def mid_back_kernel(
    own_ref, other_ref, mid_ref, cot_ref, branch_ref, attended_ref, w_ref, mod_ref, live_ref,
    grad_mid_ref, grad_attended_ref, sums_ref, grad_ref, total_ref,
):
    step, last = pl.program_id(0), pl.num_programs(0) - 1
    grad_hidden = own_ref[...] + other_ref[...].astype(f32)
    normed, inverse = normalize(mid_ref[...])
    back = normalize_back(grad_hidden * (1.0 + modulation(mod_ref, 4)), normed, inverse)
    grad_mid = cot_ref[...].astype(f32) + back
    grad_mid_ref[...] = grad_mid
    gate = jnp.sum(branch_ref[...].astype(f32) * grad_mid, axis=0, keepdims=True)
    sums_ref[0, 0:1] = live_ref[0] * gate
    sums_ref[0, 1:2] = jnp.sum(grad_hidden, axis=0, keepdims=True)
    sums_ref[0, 2:3] = jnp.sum(grad_hidden * normed, axis=0, keepdims=True)
    grad_branch = (modulation(mod_ref, 2) * grad_mid).astype(bf16)
    grad_attended_ref[...] = dot32(grad_branch, w_ref[...], RIGHT_T).astype(bf16)
    part = dot32(grad_branch, attended_ref[...], LEFT_T)

    @pl.when(step == 0)
    def _():
        total_ref[...] = part

    @pl.when(step > 0)
    def _():
        total_ref[...] += part

    @pl.when(step == last)
    def _():
        grad_ref[...] = total_ref[...].astype(bf16)


def mid_backward(own, other, mid, cotangent, branch, attended, w_attn, mod, live):
    count, width = own.shape
    local = mod.shape[0]
    row_spec = pl.BlockSpec((count // local, width), lambda i: (i, 0))
    return dense_call(
        mid_back_kernel,
        "mid_back",
        (local,),
        [row_spec] * 6
        + [
            full_spec((width, width)),
            pl.BlockSpec((1,) + mod.shape[1:], lambda i: (i, 0, 0)),
            pl.BlockSpec((1, 1, width), lambda i: (i, 0, 0)),
        ],
        [
            row_spec,
            row_spec,
            pl.BlockSpec((1, 8, width), lambda i: (i, 0, 0)),
            full_spec((width, width)),
        ],
        [
            jax.ShapeDtypeStruct((count, width), f32),
            jax.ShapeDtypeStruct((count, width), bf16),
            jax.ShapeDtypeStruct((local, 8, width), f32),
            jax.ShapeDtypeStruct((width, width), bf16),
        ],
        [pltpu.VMEM((width, width), f32)],
    )(own, other, mid, cotangent, branch, attended, w_attn, mod, live)


def grad_pieces(tiles, tile, width):
    block, out_block = tiles * tile // 32, width // 32
    pieces = []
    for number in range(32):
        pieces.append((0, number, None, number * out_block, block, out_block))
        first, rest, to = number * block, block, 0
        while rest:
            size = min(rest, tile - first % tile)
            pieces.append((first // tile, number, first // tile, first % tile, to, size))
            first, rest, to = first + size, rest - size, to + size
    return pieces


def qkv_grad_kernel(pieces, where_ref, grad_ref, hidden_ref, out_grad_ref, *refs):
    outs, whole_ref, sems = refs[:4], refs[4], refs[5]
    x, y, c = where_ref[1], where_ref[2], where_ref[3]
    step, steps = pl.program_id(0), pl.num_programs(0)
    whole_ref[step] = dot32(grad_ref[0], hidden_ref[...], LEFT_T).astype(bf16)

    for now in range(whole_ref.shape[0]):
        for here_x in range(2):
            for here_c in range(2):

                @pl.when((step == now) & (x == here_x) & (c == here_c))
                def _(now=now, here_x=here_x, here_c=here_c):
                    for count, (ready, number, tile, first, start, size) in enumerate(pieces):
                        if ready != now:
                            continue
                        z, l = number // 8, (number // 2 % 2) ^ y
                        j, core = (number // 4 % 2) ^ here_x, (number % 2) ^ here_c
                        rows = pl.ds(first, size)
                        source = out_grad_ref.at[rows] if tile is None else whole_ref.at[tile, rows]
                        place = outs[2 * core + 1 - j].at[1 - l, z, pl.ds(start, size)]
                        pltpu.make_async_copy(source, place, sems.at[count]).start()

    @pl.when(step == steps - 1)
    def _():
        for count, piece in enumerate(pieces):
            place = outs[0].at[0, 0, pl.ds(0, piece[5])]
            pltpu.make_async_copy(place, place, sems.at[count]).wait()


def qkv_grad(where, grad_projected, hidden, grad_out):
    count, width = hidden.shape
    tile = 512
    per = width // tile
    rows = 4 * width // 32
    shape = low_shape(2, 4, rows, width)
    pieces = grad_pieces(3 * per, tile, width)
    return pl.pallas_call(
        functools.partial(qkv_grad_kernel, pieces),
        grid=(3 * per,),
        in_specs=[
            pl.BlockSpec(memory_space=pltpu.SMEM),
            pl.BlockSpec((1, count, tile), lambda i: (i // per, 0, i % per)),
            full_spec(hidden.shape),
            full_spec(grad_out.shape),
        ],
        out_specs=[pl.BlockSpec(memory_space=pl.ANY)] * 4,
        out_shape=[shape] * 4,
        scratch_shapes=[
            pltpu.VMEM((3 * per, tile, width), bf16),
            pltpu.SemaphoreType.DMA((len(pieces),)),
        ],
        compiler_params=pltpu.CompilerParams(vmem_limit_bytes=VMEM_LIMIT),
        cost_estimate=SMALL,
        name="qkv_grad",
    )(where, grad_projected, hidden, grad_out)


def qkv_grad_plain(grad_projected, hidden):
    return lax.dot_general(
        grad_projected, hidden, (((1,), (0,)), ((), ())), preferred_element_type=f32
    ).astype(bf16)


def tokens_back_kernel(
    where_ref, grad_ref, w_ref, tokens_ref, grad_mid_ref, mod_ref, out_ref, away_ref, sums_ref
):
    width = tokens_ref.shape[1]
    grad_hidden = None
    for part in range(3):
        add = dot32(grad_ref[part], w_ref[:, part * width : (part + 1) * width], RIGHT_T)
        grad_hidden = add if grad_hidden is None else grad_hidden + add
    normed, inverse = normalize(tokens_ref[...].astype(f32))
    back = normalize_back(grad_hidden * (1.0 + modulation(mod_ref, 1)), normed, inverse)
    out_ref[...] = (grad_mid_ref[...] + back).astype(bf16)
    split_away(where_ref, out_ref, away_ref)
    sums_ref[0, 0:1] = jnp.sum(grad_hidden, axis=0, keepdims=True)
    sums_ref[0, 1:2] = jnp.sum(grad_hidden * normed, axis=0, keepdims=True)


def tokens_backward(where, grad_projected, w_qkv, tokens, grad_mid, mod):
    count, width = tokens.shape
    local = mod.shape[0]
    rows = count // local
    row_spec = pl.BlockSpec((rows, width), lambda i: (i, 0))
    return dense_call(
        tokens_back_kernel,
        "tokens_back",
        (local,),
        [
            pl.BlockSpec(memory_space=pltpu.SMEM),
            pl.BlockSpec((3, rows, width), lambda i: (0, i, 0)),
            full_spec((width, 3 * width)),
            row_spec,
            row_spec,
            pl.BlockSpec((1,) + mod.shape[1:], lambda i: (i, 0, 0)),
        ],
        [
            row_spec,
            pl.BlockSpec((3 * SPATIAL, width), lambda i: (i, 0)),
            pl.BlockSpec((1, 8, width), lambda i: (i, 0, 0)),
        ],
        [
            low_shape(count, width),
            low_shape(local * 3 * SPATIAL, width),
            jax.ShapeDtypeStruct((local, 8, width), f32),
        ],
    )(where, grad_projected, w_qkv, tokens, grad_mid, mod)


def modulation_kernel(parts_ref, bias_ref, live_ref, out_ref):
    sources, holders, local, part = parts_ref.shape
    width = out_ref.shape[2] // 6
    for window in range(local):
        for holder in range(holders):
            total = parts_ref[0, holder, window : window + 1]
            for source in range(1, sources):
                total = total + parts_ref[source, holder, window : window + 1]
            columns = slice(holder * part, (holder + 1) * part)
            out_ref[window, :, columns] = total + bias_ref[:, columns]
        for gate in (2, 5):
            columns = slice(gate * width, (gate + 1) * width)
            out_ref[window, :, columns] = out_ref[window, :, columns] * live_ref[window]


def modulate(parts, bias, live):
    local, _, width = live.shape
    return dense_call(
        modulation_kernel,
        "modulation",
        (1,),
        [full_spec(parts.shape), full_spec(bias.shape), full_spec(live.shape)],
        full_spec((local, 1, 6 * width)),
        jax.ShapeDtypeStruct((local, 1, 6 * width), f32),
    )(parts, bias, live)


def gated_kernel(where_ref, rows_ref, mod_ref, out_ref):
    out_ref[...] = (modulation(mod_ref, 5) * rows_ref[...].astype(f32)).astype(bf16)


def gated(where, rows, mod):
    count, width = rows.shape
    local = mod.shape[0]
    row_spec = pl.BlockSpec((count // local, width), lambda i: (i, 0))
    return dense_call(
        gated_kernel,
        "gated",
        (local,),
        [
            pl.BlockSpec(memory_space=pltpu.SMEM),
            row_spec,
            pl.BlockSpec((1,) + mod.shape[1:], lambda i: (i, 0, 0)),
        ],
        row_spec,
        low_shape(count, width),
    )(where, rows, mod)


def space_onehot():
    places = jnp.arange(SPATIAL, dtype=jnp.int32)
    across, along = places // SIDE, places % SIDE
    index = (across[:, None] - across[None, :] + SIDE - 1) * (2 * SIDE - 1) + (
        along[:, None] - along[None, :] + SIDE - 1
    )
    ids = jnp.arange((2 * SIDE - 1) ** 2, dtype=jnp.int32)
    return (index.reshape(-1)[:, None] == ids[None, :]).astype(f32)


def on_device(
    tokens,
    condition,
    doubled,
    window_count,
    w_ada,
    b_ada,
    w_qkv,
    w_out,
    w_up,
    b_up,
    w_down,
    b_down,
    table_space,
    table_time,
    cotangent,
):
    windows, _, width = tokens.shape
    heads = table_space.shape[0]
    n_win = lax.axis_size("win")
    devices = n_win * 4
    win = lax.axis_index("win")
    frm = lax.axis_index("frm")
    z, x, y, c = win // 2, win % 2, frm // 2, frm % 2
    where = jnp.concatenate([jnp.stack([z, x, y, c, frm, window_count[0]]), doubled])
    where = where.astype(jnp.int32)
    local = windows // 4
    count = local * FRAMES * SPATIAL
    ff = w_up.shape[1]
    ff_block = ff // devices
    shard_rows = w_qkv.shape[0]
    half_width = width // 2
    fast = n_win == 8
    slot_shape = (2 * windows, SPATIAL, width)

    tok_slots, cot_slots = tokens.reshape(slot_shape), cotangent.reshape(slot_shape)
    tok_send = windows_send(where, tok_slots)
    biases = jnp.concatenate([b_ada, b_up, b_down])
    bias_rows = -(-biases.shape[0] // width)
    biases = jnp.pad(biases, (0, bias_rows * width - biases.shape[0])).reshape(bias_rows, width)
    small = jnp.concatenate([condition, biases])
    if fast:
        q_half, up_half, down_half = halves(where, w_qkv, w_out, w_up, w_down)
        q_direct = gather_z_direct(q_half)
        tok_send, _ = sync(tok_send, q_half)
        small, _ = sync(small, tok_send)
    small_all = lax.all_to_all(
        jnp.broadcast_to(small[None], (n_win,) + small.shape),
        "win",
        split_axis=0,
        concat_axis=0,
        tiled=True,
    )
    tok_got = swap_core(tok_send)
    tok_here, tok_away = windows_pack(where, tok_slots, tok_got)
    tok_back = swap_y(tok_away)

    onehot_space = space_onehot()
    space_bias = jnp.dot(table_space, onehot_space.T, precision=exact_mode)
    space_bias = jnp.tile(space_bias.reshape(heads, SPATIAL, SPATIAL), (1, 1, FRAMES))
    mine_doubled = lax.dynamic_slice_in_dim(doubled, frm * local, local, 0)
    holders = jnp.arange(4, dtype=jnp.int32)
    frames = holders[None, :] + (holders[None, :] > mine_doubled[:, None]).astype(jnp.int32)
    frames = jnp.concatenate([frames, mine_doubled[:, None] + 1], axis=1)
    offset = frames[:, :, None] - frames[:, None, :] + FRAMES - 1
    onehot_time = (
        offset[..., None] == jnp.arange(table_time.shape[1], dtype=jnp.int32)
    ).astype(f32)
    time_bias = jnp.einsum("wabt,ht->whab", onehot_time, table_time, precision=exact_mode)
    time_bias = jnp.repeat(time_bias, SPATIAL, axis=-1)
    time_bias = jnp.pad(time_bias, ((0, 0), (0, 0), (0, 8 - FRAMES), (0, 0)))

    if fast:
        *q_direct, _ = sync(*q_direct, tok_away)
        q_stack = jnp.stack(q_direct)
        q_near = gather_near(q_stack)
        small_all, up_half, _ = sync(small_all, up_half, q_stack)
        up_direct = gather_z_direct(up_half)

    cond_all = small_all[:, :windows].reshape(n_win * windows, width).astype(f32)
    bias_all = small_all[:, windows:].reshape(n_win, bias_rows * width).astype(f32)
    cuts = [b_ada.shape[0], b_ada.shape[0] + b_up.shape[0]]
    ada_bias = bias_all[:, : cuts[0]].reshape(1, 6 * width)
    up_bias = bias_all[:, cuts[0] : cuts[1]].reshape(n_win * 2, 2, ff_block)
    up_bias = pick(up_bias, c, 1).reshape(1, ff // 2)
    down_bias = bias_all[:, cuts[1] : cuts[1] + b_down.shape[0]].reshape(1, width)
    silu_all = jax.nn.silu(cond_all).astype(bf16)
    silu_part = lax.dynamic_slice_in_dim(silu_all, win * shard_rows, shard_rows, 1)
    ada_quarter = 6 * width // 4
    ada_part = lax.dynamic_slice_in_dim(w_ada, frm * ada_quarter, ada_quarter, 1)
    mod_part = dot32(silu_part, ada_part, PLAIN)
    if fast:
        *q_near, mod_part, up_bias, down_bias, space_bias, time_bias = sync(
            *q_near, mod_part, up_bias, down_bias, space_bias, time_bias
        )
        q_far = gather_far(q_near)
        *up_direct, q_near[0], q_near[1], q_near[2] = sync(*up_direct, *q_near)
        q_other = [swap_core(part) for part in q_near]
    else:
        qkv_full = lax.all_gather(w_qkv, "win", axis=0).reshape(width, 3 * width)
        out_full = lax.all_gather(w_out, "win", axis=0).reshape(width, width)
        up_shard = pick(w_up.reshape(shard_rows, n_win * 2, 2, ff_block), c, 2)
        up_full = lax.all_gather(up_shard, "win", axis=0).reshape(width, ff // 2)
        down_shard = pick(w_down.reshape(2, 2, ff_block, width), c, 1)
        down_full = lax.all_gather(down_shard, "win", axis=0).reshape(ff // 2, width)
    mod_parts = exchange_all(mod_part.reshape(devices, local, ada_quarter))
    my_window = frm * local + jnp.arange(local, dtype=jnp.int32)
    live = (my_window < window_count[0]).astype(f32)[:, None, None]
    live = jnp.broadcast_to(live, (local, 1, width))
    cot_send = windows_send(where, cot_slots)
    if fast:
        up_stack = jnp.stack(up_direct)
        q_far[0], tok_back, mod_parts, cot_send, up_stack, *q_other = sync(
            q_far[0], tok_back, mod_parts, cot_send, up_stack, *q_other
        )
        q_other = q_other + [swap_core(part) for part in q_far]
        up_near = gather_near(up_stack)
        qkv_full, out_full = place_qkv(where, list(q_near) + list(q_far) + q_other)
    cot_got = swap_core(cot_send)
    token_rows = windows_join(where, tok_here, tok_back)
    mod = modulate(mod_parts.reshape(n_win, 4, local, ada_quarter), ada_bias, live)

    projected, hidden_one = qkv_forward(token_rows, mod, qkv_full)
    cot_here, cot_away = windows_pack(where, cot_slots, cot_got)
    if fast:
        projected, cot_away, down_half, *up_near = sync(
            projected, cot_away, down_half, *up_near
        )
        up_far = gather_far(up_near)
        down_direct = gather_z_direct(down_half)
    cot_back = swap_y(cot_away)
    attended, probs = attend(projected, space_bias, time_bias, local)
    if fast:
        attended, cot_back, up_far[0], *down_direct = sync(
            attended, cot_back, up_far[0], *down_direct
        )
        down_near = gather_near(jnp.stack(down_direct))
    branch_attn, mid, hidden_two = out_forward(attended, out_full, token_rows, mod)
    grad_out = windows_join(where, cot_here, cot_back)
    grad_mlp = gated(where, grad_out, mod)
    mlp_other = swap_core(grad_mlp)

    hidden_other = swap_core(hidden_two)
    if fast:
        up_full = place_up(where, list(up_near) + list(up_far))
    rows_both = (hidden_two, hidden_other, grad_mlp, mlp_other)
    act_first, slope_first, *down_grads = up_forward(where, rows_both, up_full, up_bias, 0, fast)
    if fast:
        act_first, up_bias, *down_near = sync(act_first, up_bias, *down_near)
        down_far = gather_far(down_near, FAR_CUT)
    act_second, slope_second, *more = up_forward(where, rows_both, up_full, up_bias, 1, fast)
    if fast:
        act_second, *down_far = sync(act_second, *down_far)
        down_fy, down_fx = swap_y(down_grads[0]), swap_win(down_grads[1], 1)
        down_full = place_down(where, list(down_near) + list(down_far))
    down_grads = list(down_grads) + more
    block_rows = ff_block
    *up_grads, up_b_first, back_first = down_backward(
        where, rows_both, down_full, up_full, slope_first, 0, None, fast
    )
    if fast:
        back_first, *up_grads, down_fy, down_fx = sync(back_first, *up_grads, down_fy, down_fx)
        send_x, send_y = merge(
            [(down_grads[2], None)], [(down_grads[3], None)], down_fy, down_fx
        )
        back_first, send_x, send_y = sync(back_first, send_x, send_y)
        down_x, down_y = swap_win(send_x, 1), swap_y(send_y)
    *more, up_b_second, back_own, back_other = down_backward(
        where, rows_both, down_full, up_full, slope_second, 1, back_first, fast
    )
    up_grads = list(up_grads) + more
    if fast:
        back_other, act_first, down_x, down_y = sync(back_other, act_first, down_x, down_y)
        up_fy, up_fx = swap_y(up_grads[0]), swap_win(up_grads[1], 1)
        down_kept = total(
            [(down_grads[4], None), (down_x, None), (down_y, None)], block_rows, width
        )
    back_got = swap_core(back_other)
    mlp_own, mlp_away = down_forward(act_first, act_second, down_full)

    if fast:
        back_got, mlp_away, down_kept, *up_grads, up_fy, up_fx = sync(
            back_got, mlp_away, down_kept, *up_grads, up_fy, up_fx
        )
        down_parts = parts_z(down_kept)
        send_x, send_y = merge([(up_grads[2], None)], [(up_grads[3], None)], up_fy, up_fx)
        back_got, send_x, send_y = sync(back_got, send_x, send_y)
        up_x, up_y = swap_win(send_x, 1), swap_y(send_y)
    mlp_got = swap_core(mlp_away)
    grad_mid, grad_attended, mid_sums, grad_out_w = mid_backward(
        back_own, back_got, mid, grad_out, branch_attn, attended, out_full, mod, live
    )
    grad_attended, mlp_got = sync(grad_attended, mlp_got)
    result, res_away, gate_two_sum = result_forward(
        where, mlp_own, mlp_got, down_bias, mid, grad_out, mod, live
    )
    grad_attended, res_away = sync(grad_attended, res_away)
    res_back = swap_y(res_away.reshape(6, SPATIAL, width))
    grad_projected, space_sums, time_sums = attend_back(
        projected, grad_attended, attended, probs, local
    )
    qkv_block, out_block = 3 * width // devices, width // devices
    if fast:
        grad_projected, up_x, up_y, res_back, down_parts = sync(
            grad_projected, up_x, up_y, res_back, down_parts
        )
        own_first, own_second, other_first, other_second = qkv_grad(
            where, grad_projected, hidden_one, grad_out_w
        )
        up_x, other_first, other_second = sync(up_x, other_first, other_second)
        up_kept = total([(up_grads[4], None), (up_x, None), (up_y, None)], block_rows, width)
        up_grad = add_z(parts_z(up_kept))
        got_first, got_second = swap_core(other_first), swap_core(other_second)
    if fast:
        got_first, up_kept = sync(got_first, up_kept)
        send_fy, send_fx, attn_gx = first_quarters(own_first, got_first)
        send_fy, send_fx, grad_projected = sync(send_fy, send_fx, grad_projected)
        attn_fy, attn_fx = swap_y(send_fy), swap_win(send_fx, 1)
    else:
        grad_attn_w = jnp.concatenate(
            [
                qkv_grad_plain(grad_projected, hidden_one).reshape(n_win, 2, 2, qkv_block, width),
                grad_out_w.reshape(n_win, 2, 2, out_block, width),
            ],
            axis=3,
        )
        got = swap_core(pick(grad_attn_w, 1 - c, 2))
        attn_grad = scatter_plain(add_low(pick(grad_attn_w, c, 2), got), where)
        up_grad = scatter_plain(jnp.concatenate(up_grads).reshape(n_win, 2, ff_block, width), where)
        down_grad = scatter_plain(
            jnp.concatenate(down_grads).reshape(n_win, 2, ff_block, width), where
        )
    grad_tokens, gt_away, token_sums = tokens_backward(
        where, grad_projected, qkv_full, token_rows, grad_mid, mod
    )
    gt_away = gt_away.reshape(6, SPATIAL, width)
    if fast:
        token_sums, attn_fy, attn_fx, got_second = sync(
            token_sums, attn_fy, attn_fx, got_second
        )
        send_x, send_y = merge(
            [(attn_gx, None)], [(own_second, 0), (got_second, 0)], attn_fy, attn_fx, LAST_CUT
        )
        attn_x, attn_y = swap_win(send_x, 1), swap_y(send_y)
        token_sums, res_back, _, _ = sync(token_sums, res_back, send_x, send_y)

    grad_mod = jnp.concatenate(
        [
            token_sums[:, 0],
            token_sums[:, 1],
            mid_sums[:, 0],
            mid_sums[:, 1],
            mid_sums[:, 2],
            gate_two_sum[:, 0],
        ],
        axis=-1,
    ).astype(bf16)
    ada_block = 6 * width // devices
    to_quarter = jnp.transpose(grad_mod.reshape(local, 4, ada_quarter), (1, 0, 2))
    to_quarter = jnp.broadcast_to(to_quarter[None], (n_win, 4, local, ada_quarter))
    to_block = jnp.transpose(grad_mod.reshape(local, devices, ada_block), (1, 0, 2))
    grad_up_b = jnp.concatenate([up_b_first, up_b_second], axis=1)
    if fast:
        grad_up_b = grad_up_b.reshape(2, 2, 4, ff_block)
        grad_up_b = jnp.where(x == 0, grad_up_b[::-1], grad_up_b)
        grad_up_b = jnp.where(y == 0, grad_up_b[:, ::-1], grad_up_b)
        grad_up_b = jnp.transpose(grad_up_b, (2, 0, 1, 3))
    grad_up_b = grad_up_b.reshape(n_win * 2, 1, ff_block)
    core_mask = (jnp.arange(2, dtype=jnp.int32) == c).astype(f32)[None, :, None]
    grad_up_b = (grad_up_b * core_mask).reshape(devices, ff_block)
    grad_down_b = jnp.sum(grad_mlp.astype(f32), axis=0).reshape(devices, width // devices)
    first_send = jnp.concatenate(
        [
            to_quarter.reshape(devices, local * ada_quarter),
            to_block.reshape(devices, local * ada_block),
            grad_up_b.astype(bf16),
            grad_down_b.astype(bf16),
        ],
        axis=1,
    )
    res_other = swap_core(windows_back_pack(where, result, res_back))
    first_got = exchange_all(first_send)
    if fast:
        down_grad = add_z(down_parts)
        attn_x, attn_y, gt_away, res_other, first_send = sync(
            attn_x, attn_y, gt_away, res_other, first_send
        )
        kept = total(
            [(own_second, 1), (got_second, 1), (attn_x, None), (attn_y, None)],
            qkv_block + out_block,
            width,
        )
        attn_grad = sum_z_direct(kept, z)
        first_got, _ = sync(first_got, kept)
    gt_back = swap_y(gt_away)
    if fast:
        space_sums, time_sums, gt_back = sync(space_sums, time_sums, gt_back)
    lanes = jnp.arange(FRAMES * SPATIAL, dtype=jnp.int32)
    to_place = (lanes[:, None] % SPATIAL == jnp.arange(SPATIAL)[None]).astype(f32)
    to_slot = (lanes[:, None] // SPATIAL == jnp.arange(FRAMES)[None]).astype(f32)
    space_sum = jnp.dot(
        space_sums.reshape(heads * SPATIAL, FRAMES * SPATIAL), to_place, precision=exact_mode
    )
    space_sum = jnp.dot(
        space_sum.reshape(heads, SPATIAL * SPATIAL), onehot_space, precision=exact_mode
    )
    time_sum = jnp.dot(
        time_sums.reshape(local * heads * 8, FRAMES * SPATIAL), to_slot, precision=exact_mode
    ).reshape(local, heads, 8, FRAMES)[:, :, :FRAMES]
    time_sum = jnp.einsum("whab,wabt->ht", time_sum, onehot_time, precision=exact_mode)
    tables = jnp.concatenate([space_sum.reshape(-1), time_sum.reshape(-1)])
    sizes = [local * ada_quarter, local * ada_block, ff_block, width // devices]
    ends = [sum(sizes[: n + 1]) for n in range(4)]
    mod_got = first_got[:, : ends[0]].reshape(n_win * windows, ada_quarter)
    mod_own = first_got[:, ends[0] : ends[1]].reshape(n_win * windows, ada_block)
    sums = jnp.sum(first_got[:, ends[1] :].astype(f32), axis=0)
    out_up_b = sums[:ff_block]
    out_down_b = sums[ff_block : ff_block + width // devices]
    grad_ada_w = dot32(silu_all, mod_own, LEFT_T)
    grad_ada_b = jnp.sum(mod_own.astype(f32), axis=0)
    cond_part = dot32(mod_got, ada_part, RIGHT_T)
    cond_send = cond_part.astype(bf16).reshape(n_win, 1, windows * shard_rows)
    cond_send = jnp.broadcast_to(cond_send, (n_win, 4, windows * shard_rows))
    cond_send = cond_send.reshape(devices, windows * shard_rows)
    table_send = jnp.broadcast_to(tables.astype(bf16)[None], (devices, tables.shape[0]))
    last_got = exchange_all(jnp.concatenate([cond_send, table_send], axis=1)).astype(f32)
    cond_grad = last_got[:, : windows * shard_rows].reshape(n_win, 4, windows, shard_rows)
    cond_grad = jnp.transpose(jnp.sum(cond_grad, axis=1), (1, 0, 2)).reshape(windows, width)
    _, silu_back = jax.vjp(jax.nn.silu, condition.astype(f32))
    grad_condition = silu_back(cond_grad)[0]
    table_all = jnp.sum(last_got[:, windows * shard_rows :], axis=0)
    space_size = table_space.size
    grad_space = table_all[:space_size].reshape(table_space.shape)
    grad_time = table_all[space_size : space_size + table_time.size].reshape(table_time.shape)

    gt_other = swap_core(windows_back_pack(where, grad_tokens, gt_back))
    result = windows_back_join(where, result, res_back, res_other, tokens, bf16)
    grad_tokens = windows_back_join(where, grad_tokens, gt_back, gt_other, cotangent, f32)

    return (
        result,
        grad_tokens,
        grad_condition,
        grad_ada_w,
        grad_ada_b,
        attn_grad[:qkv_block].T,
        attn_grad[qkv_block:].T,
        up_grad.T,
        out_up_b,
        down_grad,
        out_down_b,
        grad_space,
        grad_time,
    )


def solution(mesh):
    return jax.shard_map(
        on_device,
        mesh=mesh,
        in_specs=(
            P("win", "frm", None),
            P("win", None),
            P("win"),
            P("win"),
            P("win", None),
            P("win"),
            P("win", None),
            P("win", None),
            P("win", None),
            P("win"),
            P("win", None),
            P("win"),
            P(),
            P(),
            P("win", "frm", None),
        ),
        out_specs=(
            P("win", "frm", None),
            P("win", "frm", None),
            P("win", None),
            P(None, BOTH),
            P(BOTH),
            P(None, BOTH),
            P(None, BOTH),
            P(None, BOTH),
            P(BOTH),
            P(BOTH, None),
            P(BOTH),
            P(),
            P(),
        ),
        check_vma=False,
    )
```
